256 devices in a mesh: ens: 8 (over y, x_lo), tile: 32 (over z, x_hi, core).
Axes of the slice: x: 4 (x_hi: 2, x_lo: 2; x = x_hi * 2 + x_lo), y: 4, z: 8, core: 2. Of those that a mesh axis runs over, the one named last changes fastest.
Arguments:
- ens_control: float32 [64, 8, 128, 1024], P('ens', None, 'tile'), may hold values from -6 to 6
- static_control: float32 [8, 128, 1024], P(None, 'tile'), may hold values from -6 to 6
- perturbations: bfloat16 [2, 64, 8, 128, 1024], P(None, 'ens', None, 'tile'), may hold values from -6 to 6
- level_sigma: float32 [8], replicated, may hold values from 0.5 to 2
- length_class: int32 [128, 1024], P('tile'), may hold values from 0 to 3
- courant_east: float32 [128, 1024], P('tile'), may hold values from -0.45 to 0.45
- courant_north: float32 [128, 1024], P('tile'), may hold values from -0.45 to 0.45
- obs_column: int32 [131072], P('tile'), may hold values from 0 to 8191
- obs_count: int32 [1024], P('tile'), may hold values from 0 to 128, as said below
- obs_value: float32 [131072], P('tile'), may hold values from -6 to 6
- obs_weight: float32 [131072], P('tile'), may hold values from 1 to 16
- obs_kernel: float32 [8, 131072], P(None, 'tile'), may hold values from 0.25 to 1.5
Outputs:
- grad_ens: float32 [64, 8, 128, 1024], P('ens', None, 'tile')
- grad_static: float32 [8, 128, 1024], P(None, 'tile')
- departures: float32 [131072], P('tile')
The draws below stay inside these ranges and needn't reach their ends.
Inputs may be any that keep to these rules, and one draw needn't show every extreme that they name: `obs_count`: for each owner d there is a largest count in its column: in every draw one owner strip gets exactly 128 slots from every holder; the counts of one holder sum to at most 4096.
All inputs are finite; a program needn't handle non-finite values.
Results may differ from the reference program's by a relative error of at most 0.0003.
Values sent between devices are 32-bit elements; how exact they have to be, the bound alone decides.
A program may use at most 64 MiB of HBM per device.

```python
import math
import jax
import jax.numpy as jnp
from jax import lax

LEV = 8
RY = 4
NX = 1024
NT = 2
NDIFF = 4
NCLASS = 4
CAP = 128
MEMBERS = 64
TILES = 32
NY = 128
CELLS = 4096
OBS_DEV = 4096
OBS = 131072


def draw_obs_count(key, part):
    keys = jax.random.split(jax.random.fold_in(key, 11), 3)
    quarter = CAP // 4
    ceiling = quarter * jax.random.randint(keys[0], (TILES,), 1, 5)
    counts = jax.random.randint(keys[1], (TILES, TILES), ceiling[None, :] // 2, ceiling[None, :] + 1)
    crowded = jax.random.randint(keys[2], (), 0, TILES)
    counts = jnp.where(jnp.arange(TILES)[None, :] == crowded, CAP, counts)
    return counts.reshape(TILES * TILES).astype(jnp.int32)


def draw_length_class(key, part):
    keys = jax.random.split(jax.random.fold_in(key, 23), 3)
    lower = jax.random.randint(keys[0], (NY * NX,), 0, NCLASS - 1)
    picker = jax.random.randint(keys[1], (NY * NX,), 0, 16)
    classes = jnp.where(picker == 0, lower, NCLASS - 1)
    planted = jax.random.randint(keys[2], (), 0, NY * NX)
    classes = jnp.where(jnp.arange(NY * NX) == planted, 0, classes)
    return classes.reshape(NY, NX).astype(jnp.int32)


def plant(values, key, low, high):
    longest = values.shape.index(max(values.shape))
    spots = []
    for shift in (0, 1):
        where = [jax.random.randint(jax.random.fold_in(key, axis), (), 0, length) for axis, length in enumerate(values.shape)]
        where[longest] = (where[longest] + shift) % values.shape[longest]
        spots.append(tuple(where))
    return values.at[spots[0]].set(low).at[spots[1]].set(high)


def level_of(key, extent, pieces, low, largest):
    factor_of = 1.0
    for dim, parts in pieces:
        heights = jax.random.uniform(jax.random.fold_in(jax.random.fold_in(key, 6), dim), (parts,), jnp.float32, low / len(pieces), largest / len(pieces))
        factor_of = factor_of * jnp.repeat(jnp.exp(heights), extent[dim] // parts).reshape((-1,) + (1,) * (len(extent) - 1 - dim))
    return factor_of


def scatter_about(stream_key, extent, width, bound, cuts=(), kind=jnp.bfloat16):
    drawn = width * jax.random.normal(stream_key, extent, jnp.float32)
    if cuts:
        drawn = drawn * level_of(stream_key, extent, cuts, -0.22, 0.18)
    return jnp.clip(drawn, -bound, bound).astype(kind)


def setup_inputs(seed: int = 0) -> dict:
    seeds = jax.random.split(jax.random.key(seed), 13)
    return {
        "ens_control": scatter_about(seeds[0], (MEMBERS, LEV, NY, NX), 1.0, 6.0, ((0, 8), (2, 32)), jnp.float32),
        "static_control": scatter_about(seeds[1], (LEV, NY, NX), 1.0, 6.0, ((1, 32),), jnp.float32),
        "perturbations": scatter_about(seeds[2], (NT, MEMBERS, LEV, NY, NX), 1.0, 6.0, ((1, 8), (3, 32))),
        "level_sigma": jnp.clip(jnp.exp(jax.random.uniform(seeds[3], (LEV,), jnp.float32, math.log(0.5), math.log(2.0))), 0.5, 2.0),
        "length_class": draw_length_class(jax.random.fold_in(seeds[12], 71), 0),
        "courant_east": jnp.clip(jax.random.uniform(seeds[5], (NY, NX), jnp.float32, -0.45, 0.45) * level_of(seeds[5], (NY, NX), ((0, 32),), -0.4, 0.0), -0.45, 0.45),
        "courant_north": jnp.clip(jax.random.uniform(seeds[6], (NY, NX), jnp.float32, -0.45, 0.45) * level_of(seeds[6], (NY, NX), ((0, 32),), -0.4, 0.0), -0.45, 0.45),
        "obs_column": plant(jax.random.randint(seeds[7], (OBS,), 0, NT * CELLS), jax.random.fold_in(seeds[7], 1), 0, (NT * CELLS) - 1).astype(jnp.int32),
        "obs_count": draw_obs_count(jax.random.fold_in(seeds[12], 71), 0),
        "obs_value": scatter_about(seeds[9], (OBS,), 1.0, 6.0, ((0, 32),), jnp.float32),
        "obs_weight": jnp.clip(jnp.exp(math.log(16.0) - 2.7725887 * jax.random.uniform(seeds[10], (OBS,), jnp.float32) ** level_of(seeds[10], (OBS,), ((0, 32),), -0.2, 0.2)), 1.0, 16.0),
        "obs_kernel": jnp.clip(jnp.exp(math.log(1.5) - 1.7917595 * jax.random.uniform(seeds[11], (LEV, OBS), jnp.float32) ** level_of(seeds[11], (LEV, OBS), ((1, 32),), -0.2, 0.2)), 0.25, 1.5),
    }


BETA_ENS = 0.8
BETA_STATIC = 0.6
DIFF_BASE = 0.06

def smooth(fields, diffusion):
    for sweep in range(NDIFF):
        weighted = diffusion * fields
        padded = jnp.pad(weighted, [(0, 0)] * (weighted.ndim - 2) + [(1, 1), (0, 0)])
        laplace = padded[..., 2:, :] + padded[..., :-2, :] + jnp.roll(weighted, 1, -1) + jnp.roll(weighted, -1, -1) - 4.0 * weighted
        fields = fields + diffusion * laplace
    return fields

def advect(fields, courant_east, courant_north):
    east_plus = jnp.maximum(courant_east, 0.0)
    east_minus = jnp.minimum(courant_east, 0.0)
    north_plus = jnp.maximum(courant_north, 0.0)
    north_minus = jnp.minimum(courant_north, 0.0)
    padded = jnp.pad(fields, ((0, 0), (1, 1), (0, 0)))
    result = fields - east_plus * (fields - jnp.roll(fields, 1, -1)) - east_minus * (jnp.roll(fields, -1, -1) - fields)
    return result - north_plus * (fields - padded[:, :-2]) - north_minus * (padded[:, 2:] - fields)

def adjoint_advect(fields, courant_east, courant_north):
    east_plus = jnp.maximum(courant_east, 0.0)
    east_minus = jnp.minimum(courant_east, 0.0)
    north_plus = jnp.maximum(courant_north, 0.0)
    north_minus = jnp.minimum(courant_north, 0.0)
    upper = jnp.pad(north_plus * fields, ((0, 0), (1, 1), (0, 0)))
    lower = jnp.pad(north_minus * fields, ((0, 0), (1, 1), (0, 0)))
    result = fields * (1.0 - east_plus + east_minus - north_plus + north_minus)
    result = result + jnp.roll(east_plus * fields, -1, -1) - jnp.roll(east_minus * fields, 1, -1)
    return result + upper[:, 2:] - lower[:, :-2]

def reference(ens_control, static_control, perturbations, level_sigma, length_class, courant_east, courant_north, obs_column, obs_count, obs_value, obs_weight, obs_kernel):
    diffusion = jnp.sqrt(DIFF_BASE * (length_class.astype(jnp.float32) + 1.0))
    members = ens_control.shape[0]
    factor = BETA_ENS / math.sqrt(members - 1)

    def add_member(running, member):
        smoothed = smooth(ens_control[member], diffusion)
        return (running + perturbations[:, member].astype(jnp.float32) * smoothed[None], member)
    initial = jnp.zeros((NT, LEV, NY, NX), jnp.float32)
    ens_sum = lax.scan(add_member, initial, jnp.arange(members, dtype=jnp.int32))[0]
    static_first = BETA_STATIC * level_sigma[:, None, None] * static_control
    static_second = advect(static_first, courant_east, courant_north)
    increment = factor * ens_sum + jnp.stack([static_first, static_second])
    counts = obs_count.reshape(TILES, TILES)
    block_end = jnp.cumsum(counts, axis=1)
    slots = jnp.arange(TILES * OBS_DEV, dtype=jnp.int32)
    holders = slots // OBS_DEV
    within = slots % OBS_DEV
    owners = lax.optimization_barrier(jnp.sum((within[:, None] >= block_end[holders]).astype(jnp.int32), axis=1))
    usable = owners < TILES
    owners = jnp.minimum(owners, TILES - 1)
    slot_time = obs_column // CELLS
    points = obs_column % CELLS
    flat_point = (owners * RY + points // NX) * NX + points % NX
    column = slot_time * (NY * NX) + flat_point
    columns = jnp.moveaxis(increment, 1, 0).reshape(LEV, NT * NY * NX)
    profile = columns[:, column]
    evolved = lax.optimization_barrier(jnp.sum(obs_kernel * profile, axis=0))
    departures = jnp.where(usable, obs_weight * (evolved - obs_value), jnp.zeros_like(evolved))
    adjoint = jnp.zeros((LEV, NT * NY * NX), jnp.float32).at[:, column].add(obs_kernel * departures[None])
    adjoint = jnp.moveaxis(adjoint.reshape(LEV, NT, NY, NX), 0, 1)
    grad_static = static_control + BETA_STATIC * level_sigma[:, None, None] * (adjoint[0] + adjoint_advect(adjoint[1], courant_east, courant_north))

    def member_grad(member):
        forcing = factor * lax.optimization_barrier(jnp.sum(perturbations[:, member].astype(jnp.float32) * adjoint, axis=0))
        return ens_control[member] + smooth(forcing, diffusion)
    grad_ens = lax.map(member_grad, jnp.arange(members, dtype=jnp.int32))
    return (grad_ens, grad_static, departures)
```

```python
import functools
import math

import jax
import jax.numpy as jnp
from jax import lax
from jax.experimental import pallas as pl
from jax.experimental.pallas import tpu as pltpu
from jax.sharding import PartitionSpec as P

NT = 2
NDIFF = 4
BETA_ENS = 0.8
BETA_STATIC = 0.6
DIFF_BASE = 0.06
LANES = 128
MESH = pl.DeviceIdType.MESH
F32 = jnp.float32
BF16 = jnp.bfloat16


def split3(x):
    a = x.astype(BF16)
    rest = x - a.astype(F32)
    b = rest.astype(BF16)
    c = (rest - b.astype(F32)).astype(BF16)
    return a, b, c


def left(x):
    return pltpu.roll(x, 1, 1)


def right(x):
    return pltpu.roll(x, x.shape[1] - 1, 1)


def kernel(
    factor,
    ens,
    tiles,
    ctl,
    stc,
    per,
    sigma,
    cls,
    east,
    north,
    ocol,
    ocnt,
    oval,
    owgt,
    oker,
    gens,
    gsta,
    gdep,
    okb,
    dif,
    dif_u,
    dif_d,
    dbc,
    dsq,
    fin,
    sta,
    sta_u,
    sta_d,
    stb,
    wnd_u,
    wnd_d,
    rcv_wu,
    rcv_wd,
    cc,
    cu,
    cd,
    pp,
    ff,
    fu,
    fd,
    wa,
    wb,
    acc,
    accb,
    rbuf,
    obs_s,
    obs_r,
    onehot,
    himask,
    adjb,
    abuf,
    adjf,
    depp,
    dbuf,
    deps,
    depr,
    s_pre,
    r_pre,
    s_c,
    r_c,
    s_f,
    r_f,
    s_obs,
    r_obs,
    s_rs,
    r_rs,
    s_ag,
    r_ag,
    s_dg,
    r_dg,
    s_w,
    r_w,
    s_dep,
    r_dep,
):
    members, lev, rows, width = ctl.shape
    hi_n = NT * rows
    e = lax.axis_index("ens")
    t = lax.axis_index("tile")
    up = lax.rem(t + tiles - 1, tiles)
    down = lax.rem(t + 1, tiles)
    first = t == 0
    last = t == tiles - 1

    def remote(src, dst, ssem, rsem, e_to, t_to):
        return pltpu.make_async_remote_copy(
            src_ref=src,
            dst_ref=dst,
            send_sem=ssem,
            recv_sem=rsem,
            device_id=(e_to, t_to),
            device_id_type=MESH,
        )

    def loop(n, body):
        def step(i, carry):
            body(i)
            return carry

        lax.fori_loop(0, n, step, 0)

    def peer_e(k):
        return lax.rem(e + k, ens)

    def peer_t(k):
        return lax.rem(t + k, tiles)

    barrier = pltpu.get_barrier_semaphore()
    loop(
        tiles - 1,
        lambda k: pl.semaphore_signal(
            barrier, inc=1, device_id=(e, peer_t(k + 1)), device_id_type=MESH
        ),
    )
    loop(
        ens - 1,
        lambda k: pl.semaphore_signal(
            barrier, inc=1, device_id=(peer_e(k + 1), t), device_id_type=MESH
        ),
    )
    dif[...] = jnp.sqrt(DIFF_BASE * (cls[...].astype(F32) + 1.0))
    sub = lax.broadcasted_iota(jnp.int32, (lev, width), 0)
    scale = jnp.zeros((lev, width), F32)
    for l in range(lev):
        scale = jnp.where(sub == l, BETA_STATIC * sigma[l], scale)
    for r in range(rows):
        sta[r] = scale * stc[:, r, :]
    pl.semaphore_wait(barrier, tiles - 1 + ens - 1)

    pre = [
        remote(dif, dif_u, s_pre.at[0], r_pre.at[0], e, down),
        remote(dif, dif_d, s_pre.at[1], r_pre.at[1], e, up),
        remote(sta.at[rows - 1], sta_u, s_pre.at[2], r_pre.at[2], e, down),
        remote(sta.at[0], sta_d, s_pre.at[3], r_pre.at[3], e, up),
    ]
    for copy in pre:
        copy.start()

    def halo(m, own, from_up, from_down, ssem, rsem):
        return (
            remote(own.at[m], from_up.at[m], ssem.at[0, m], rsem.at[0, m], e, down),
            remote(own.at[m], from_down.at[m], ssem.at[1, m], rsem.at[1, m], e, up),
        )

    def send_control(m):
        for r in range(rows):
            cc[m, r] = ctl[m, :, r, :]
        for copy in halo(m, cc, cu, cd, s_c, r_c):
            copy.start()

    loop(members, send_control)

    count = jnp.broadcast_to(ocnt[...].astype(F32), (tiles, tiles))
    d_sub = lax.broadcasted_iota(jnp.int32, (tiles, tiles), 0)
    d_lane = lax.broadcasted_iota(jnp.int32, (tiles, tiles), 1)
    count_col = jnp.sum(
        jnp.where(d_lane == d_sub, count, 0.0), axis=1, keepdims=True
    )
    start_col = jnp.sum(jnp.where(d_lane < d_sub, count, 0.0), axis=1, keepdims=True)
    start_row = jnp.sum(
        jnp.where(d_sub < d_lane, jnp.broadcast_to(count_col, (tiles, tiles)), 0.0),
        axis=0,
        keepdims=True,
    )
    begin = jnp.broadcast_to(start_col, (tiles, LANES)).astype(jnp.int32)
    shift = begin & (LANES - 1)
    lane = lax.broadcasted_iota(jnp.int32, (tiles, LANES), 1)
    usable = lane < jnp.broadcast_to(count_col, (tiles, LANES)).astype(jnp.int32)

    def turn(x, back):
        for bit in range(LANES.bit_length() - 1):
            by = LANES - (1 << bit) if back else 1 << bit
            x = jnp.where(shift & (1 << bit) != 0, pltpu.roll(x, by, 1), x)
        return x

    line_col = jnp.broadcast_to(start_col, (tiles, tiles)).astype(jnp.int32) // LANES
    pick = jnp.concatenate(
        [jnp.where(d_lane == line_col, 1.0, 0.0), jnp.where(d_lane == line_col + 1, 1.0, 0.0)],
        axis=0,
    ).astype(BF16)
    for b in range(tiles):
        okb[b] = oker[:, b * LANES : (b + 1) * LANES]
    for q in range(lev + 3):
        if q < lev:
            part = okb[:, q, :]
        else:
            part = (ocol, oval, owgt)[q - lev][...].astype(F32)
        two = sum(
            jnp.dot(pick, piece, preferred_element_type=F32) for piece in split3(part)
        )
        value = turn(jnp.where(lane >= shift, two[0:tiles], two[tiles : 2 * tiles]), True)
        if q == lev:
            value = jnp.where(usable, value, -1.0)
        obs_s[:, q, :] = value
    for q in range(lev + 3, 2 * lev):
        obs_s[:, q, :] = jnp.zeros((tiles, LANES), F32)

    def obs_copy(k):
        d = peer_t(k)
        return remote(obs_s.at[d], obs_r.at[t], s_obs.at[d], r_obs.at[t], e, d)

    loop(tiles - 1, lambda k: obs_copy(k + 1).start())
    obs_r[t] = obs_s[t]

    def spread(m):
        for s in range(NT):
            block = per[s, m].astype(F32)
            for r in range(rows):
                pp[s, m, r] = block[:, r, :]

    loop(members, spread)

    pre[0].wait_recv()
    pre[1].wait_recv()
    above = jnp.where(first, 0.0, dif_u[...])
    below = jnp.where(last, 0.0, dif_d[...])
    own = dif[...]
    total_rows = rows + 2 * NDIFF
    for i in range(total_rows):
        src = above if i < NDIFF else (own if i < NDIFF + rows else below)
        j = i if i < NDIFF else (i - NDIFF if i < NDIFF + rows else i - NDIFF - rows)
        line = jnp.broadcast_to(src[j : j + 1, :], (lev, width))
        dbc[i] = line
        dsq[i] = line * line
        if NDIFF <= i < NDIFF + rows:
            fin[i - NDIFF] = factor / line

    pre[2].wait_recv()
    pre[3].wait_recv()

    def winds(r):
        we = jnp.broadcast_to(east[r : r + 1, :], (lev, width))
        wn = jnp.broadcast_to(north[r : r + 1, :], (lev, width))
        return (
            jnp.maximum(we, 0.0),
            jnp.minimum(we, 0.0),
            jnp.maximum(wn, 0.0),
            jnp.minimum(wn, 0.0),
        )

    for r in range(rows):
        ep, em, np_, nm = winds(r)
        q = sta[r]
        above = sta[r - 1] if r else jnp.where(first, 0.0, sta_u[...])
        below = sta[r + 1] if r < rows - 1 else jnp.where(last, 0.0, sta_d[...])
        moved = q - ep * (q - left(q)) - em * (right(q) - q)
        moved = moved - np_ * (q - above) - nm * (below - q)
        for b in range(ens):
            stb[b, r] = q[:, b * LANES : (b + 1) * LANES]
            stb[b, rows + r] = moved[:, b * LANES : (b + 1) * LANES]

    def obs_wait(k):
        s = peer_t(k + 1)
        remote(obs_s.at[s], obs_r.at[s], s_obs.at[s], r_obs.at[s], e, s).wait_recv()

    loop(tiles - 1, obs_wait)
    pairs = tiles // 2

    def lines_of(g, i):
        return jnp.concatenate(
            [obs_r[2 * g, i : i + 1, :], obs_r[2 * g + 1, i : i + 1, :]], axis=1
        )

    lo_iota = lax.broadcasted_iota(jnp.int32, (LANES, 2 * LANES), 0)

    def hot(g):
        col = lines_of(g, lev).astype(jnp.int32)
        lo = col & (LANES - 1)
        block = (col // LANES) & (ens - 1)
        hi = col // width
        hi = jnp.where((col >= 0) & (block == e), hi, -1)
        himask[g] = jnp.broadcast_to(hi, (lev, 2 * LANES))
        onehot[g] = jnp.where(
            jnp.broadcast_to(lo, (LANES, 2 * LANES)) == lo_iota, 1.0, 0.0
        ).astype(BF16)

    loop(pairs, hot)

    def smooth(m, center, from_up, from_down):
        for i in range(total_rows):
            if i < NDIFF:
                line = from_up[m, i]
            elif i < NDIFF + rows:
                line = center[m, i - NDIFF]
            else:
                line = from_down[m, i - NDIFF - rows]
            wa[i] = dbc[i] * line
        src, dst = wa, wb
        for step in range(NDIFF):
            for i in range(step + 1, total_rows - 1 - step):
                w = src[i]
                lap = src[i + 1] + src[i - 1] + left(w) + right(w) - 4.0 * w
                dst[i] = w + dsq[i] * lap
            src, dst = dst, src
        return src

    for h in range(hi_n):
        acc[h] = jnp.zeros((lev, width), F32)

    def forward(m):
        for copy in halo(m, cc, cu, cd, s_c, r_c):
            copy.wait_recv()
        res = smooth(m, cc, cu, cd)
        for r in range(rows):
            w = res[NDIFF + r]
            for s in range(NT):
                acc[s * rows + r] += pp[s, m, r] * w

    loop(members, forward)

    for h in range(hi_n):
        value = acc[h] * fin[h % rows]
        for b in range(ens):
            accb[b, h] = value[:, b * LANES : (b + 1) * LANES]

    def rs_copy(k):
        to = peer_e(k)
        return remote(accb.at[to], rbuf.at[e], s_rs.at[to], r_rs.at[e], to, t)

    loop(ens - 1, lambda k: rs_copy(k + 1).start())

    def rs_wait(k):
        s = peer_e(k + 1)
        remote(accb.at[s], rbuf.at[s], s_rs.at[s], r_rs.at[s], s, t).wait_recv()

    loop(ens - 1, rs_wait)
    rbuf[e] = accb[e]
    parts = ([], [], [])
    for h in range(hi_n):
        value = stb[e, h]
        for b in range(ens):
            value = value + rbuf[b, h]
        for store, piece in zip(parts, split3(value)):
            store.append(piece)
    table = jnp.concatenate(parts[0] + parts[1] + parts[2], axis=0)
    points = hi_n * lev

    def observe(g, total):
        flat = jnp.dot(table, onehot[g], preferred_element_type=F32)
        flat = flat[0:points] + flat[points : 2 * points] + flat[2 * points : 3 * points]
        hi = himask[g]
        kern = jnp.concatenate(
            [obs_r[2 * g, 0:lev, :], obs_r[2 * g + 1, 0:lev, :]], axis=1
        )
        profile = jnp.zeros((lev, 2 * LANES), F32)
        for h in range(hi_n):
            profile = jnp.where(hi == h, flat[h * lev : (h + 1) * lev], profile)
        evolved = jnp.sum(kern * profile, axis=0, keepdims=True)
        dep = lines_of(g, lev + 2) * (evolved - lines_of(g, lev + 1))
        dep = jnp.where(hi[0:1] >= 0, dep, 0.0)
        depp[2 * g] = dep[:, 0:LANES]
        depp[2 * g + 1] = dep[:, LANES : 2 * LANES]
        push = kern * dep
        place = jnp.concatenate(
            [jnp.where(hi == h, push, 0.0) for h in range(hi_n)], axis=0
        )
        return total + lax.dot_general(
            jnp.concatenate(split3(place), axis=0),
            onehot[g],
            (((1,), (1,)), ((), ())),
            preferred_element_type=F32,
        )

    total = lax.fori_loop(0, pairs, observe, jnp.zeros((3 * points, LANES), F32))
    total = total[0:points] + total[points : 2 * points] + total[2 * points : 3 * points]
    for h in range(hi_n):
        adjb[h] = total[h * lev : (h + 1) * lev]

    def ag_copy(k):
        to = peer_e(k)
        return remote(adjb, abuf.at[e], s_ag.at[to], r_ag.at[e], to, t)

    def dg_copy(k):
        to = peer_e(k)
        return remote(depp, dbuf.at[e], s_dg.at[to], r_dg.at[e], to, t)

    loop(ens - 1, lambda k: ag_copy(k + 1).start())
    loop(ens - 1, lambda k: dg_copy(k + 1).start())
    abuf[e] = adjb[...]

    def ag_wait(k):
        s = peer_e(k + 1)
        remote(adjb, abuf.at[s], s_ag.at[s], r_ag.at[s], s, t).wait_recv()

    loop(ens - 1, ag_wait)
    for h in range(hi_n):
        adjf[h] = jnp.concatenate([abuf[b, h] for b in range(ens)], axis=1)

    def force(m):
        for r in range(rows):
            ff[m, r] = pp[0, m, r] * adjf[r] + pp[1, m, r] * adjf[rows + r]
        for copy in halo(m, ff, fu, fd, s_f, r_f):
            copy.start()

    loop(members, force)

    wnd_u[...] = winds(0)[2] * adjf[rows]
    wnd_d[...] = winds(rows - 1)[3] * adjf[2 * rows - 1]
    wind = [
        remote(wnd_d, rcv_wu, s_w.at[0], r_w.at[0], e, down),
        remote(wnd_u, rcv_wd, s_w.at[1], r_w.at[1], e, up),
    ]
    for copy in wind:
        copy.start()

    def dg_wait(k):
        s = peer_e(k + 1)
        remote(depp, dbuf.at[s], s_dg.at[s], r_dg.at[s], s, t).wait_recv()

    loop(ens - 1, dg_wait)
    dbuf[e] = depp[...]

    def gather_dep(s):
        value = dbuf[0, s]
        for b in range(1, ens):
            value = value + dbuf[b, s]
        deps[s] = value

    loop(tiles, gather_dep)

    def dep_copy(k):
        s = peer_t(k)
        return remote(deps.at[s], depr.at[t], s_dep.at[s], r_dep.at[t], e, s)

    loop(tiles - 1, lambda k: dep_copy(k + 1).start())
    depr[t] = deps[t]

    def backward(m):
        for copy in halo(m, ff, fu, fd, s_f, r_f):
            copy.wait_recv()
        res = smooth(m, ff, fu, fd)
        for r in range(rows):
            gens[m, :, r, :] = cc[m, r] + res[NDIFF + r] * fin[r]

    loop(members, backward)

    for copy in wind:
        copy.wait_recv()
    for r in range(rows):
        ep, em, np_, nm = winds(r)
        a = adjf[rows + r]
        if r < rows - 1:
            lower = winds(r + 1)[2] * adjf[rows + r + 1]
        else:
            lower = jnp.where(last, 0.0, rcv_wd[...])
        if r:
            upper = winds(r - 1)[3] * adjf[rows + r - 1]
        else:
            upper = jnp.where(first, 0.0, rcv_wu[...])
        moved = a * (1.0 - ep + em - np_ + nm) + right(ep * a) - left(em * a)
        moved = moved + lower - upper
        gsta[:, r, :] = stc[:, r, :] + scale * (adjf[r] + moved)

    def dep_wait(k):
        s = peer_t(k + 1)
        remote(deps.at[s], depr.at[s], s_dep.at[s], r_dep.at[s], e, s).wait_recv()

    loop(tiles - 1, dep_wait)
    line_row = jnp.broadcast_to(start_row, (tiles, tiles)).astype(jnp.int32) // LANES
    spread0 = jnp.where(d_sub == line_row, 1.0, 0.0).astype(BF16)
    spread1 = jnp.where(d_sub == line_row + 1, 1.0, 0.0).astype(BF16)
    value = turn(jnp.where(usable, depr[:, 0, :], 0.0), False)
    out = jnp.zeros((tiles, LANES), F32)
    for piece in split3(jnp.where(lane >= shift, value, 0.0)):
        out = out + jnp.dot(spread0, piece, preferred_element_type=F32)
    for piece in split3(jnp.where(lane < shift, value, 0.0)):
        out = out + jnp.dot(spread1, piece, preferred_element_type=F32)
    gdep[...] = out

    for copy in pre + wind:
        copy.wait_send()

    def sent(m):
        for copy in halo(m, cc, cu, cd, s_c, r_c) + halo(m, ff, fu, fd, s_f, r_f):
            copy.wait_send()

    loop(members, sent)

    def sent_t(k):
        obs_copy(k + 1).wait_send()
        dep_copy(k + 1).wait_send()

    loop(tiles - 1, sent_t)

    def sent_e(k):
        rs_copy(k + 1).wait_send()
        ag_copy(k + 1).wait_send()
        dg_copy(k + 1).wait_send()

    loop(ens - 1, sent_e)


def per_device(
    ens_control,
    static_control,
    perturbations,
    level_sigma,
    length_class,
    courant_east,
    courant_north,
    obs_column,
    obs_count,
    obs_value,
    obs_weight,
    obs_kernel,
):
    members, lev, rows, width = ens_control.shape
    ens = lax.axis_size("ens")
    tiles = lax.axis_size("tile")
    factor = BETA_ENS / math.sqrt(ens * members - 1)
    hi_n = NT * rows
    vmem = lambda *shape, dtype=F32: pltpu.VMEM(shape, dtype)
    dma = lambda *shape: pltpu.SemaphoreType.DMA(shape)
    line = (lev, width)
    total_rows = rows + 2 * NDIFF
    fields = (members, rows) + line
    scratch = [
        vmem(tiles, lev, LANES),
        vmem(rows, width),
        vmem(rows, width),
        vmem(rows, width),
        vmem(total_rows, *line),
        vmem(total_rows, *line),
        vmem(rows, *line),
        vmem(rows, *line),
        vmem(*line),
        vmem(*line),
        vmem(ens, hi_n, lev, LANES),
        vmem(*line),
        vmem(*line),
        vmem(*line),
        vmem(*line),
        vmem(*fields),
        vmem(*fields),
        vmem(*fields),
        vmem(NT, *fields),
        vmem(*fields),
        vmem(*fields),
        vmem(*fields),
        vmem(total_rows, *line),
        vmem(total_rows, *line),
        vmem(hi_n, *line),
        vmem(ens, hi_n, lev, LANES),
        vmem(ens, hi_n, lev, LANES),
        vmem(tiles, 2 * lev, LANES),
        vmem(tiles, 2 * lev, LANES),
        vmem(tiles // 2, LANES, 2 * LANES, dtype=BF16),
        vmem(tiles // 2, lev, 2 * LANES, dtype=jnp.int32),
        vmem(hi_n, lev, LANES),
        vmem(ens, hi_n, lev, LANES),
        vmem(hi_n, *line),
        vmem(tiles, 1, LANES),
        vmem(ens, tiles, 1, LANES),
        vmem(tiles, 1, LANES),
        vmem(tiles, 1, LANES),
        dma(4), dma(4),
        dma(2, members), dma(2, members),
        dma(2, members), dma(2, members),
        dma(tiles), dma(tiles),
        dma(ens), dma(ens),
        dma(ens), dma(ens),
        dma(ens), dma(ens),
        dma(2), dma(2),
        dma(tiles), dma(tiles),
    ]
    v = pl.BlockSpec(memory_space=pltpu.VMEM)
    s = pl.BlockSpec(memory_space=pltpu.SMEM)
    shape = jax.ShapeDtypeStruct
    grad_ens, grad_static, departures = pl.pallas_call(
        functools.partial(kernel, factor, ens, tiles),
        out_shape=(
            shape(ens_control.shape, F32),
            shape(static_control.shape, F32),
            shape((tiles, LANES), F32),
        ),
        in_specs=[v, v, v, s, v, v, v, v, v, v, v, v],
        out_specs=(v, v, v),
        scratch_shapes=scratch,
        name="gradient",
        compiler_params=pltpu.CompilerParams(
            collective_id=0, has_side_effects=True, vmem_limit_bytes=56 * 2**20
        ),
    )(
        ens_control,
        static_control,
        perturbations,
        level_sigma,
        length_class,
        courant_east,
        courant_north,
        obs_column.reshape(tiles, LANES),
        obs_count.reshape(1, tiles),
        obs_value.reshape(tiles, LANES),
        obs_weight.reshape(tiles, LANES),
        obs_kernel,
    )
    return (grad_ens, grad_static, departures.reshape(-1))


def solution(mesh):
    return jax.shard_map(
        per_device,
        mesh=mesh,
        in_specs=(
            P("ens", None, "tile", None),
            P(None, "tile", None),
            P(None, "ens", None, "tile", None),
            P(),
            P("tile", None),
            P("tile", None),
            P("tile", None),
            P("tile"),
            P("tile"),
            P("tile"),
            P("tile"),
            P(None, "tile"),
        ),
        out_specs=(P("ens", None, "tile", None), P(None, "tile", None), P("tile")),
        check_vma=False,
    )
```

```python
import functools
import math

import jax
import jax.numpy as jnp
from jax import lax
from jax.experimental import pallas as pl
from jax.experimental.pallas import tpu as pltpu
from jax.sharding import PartitionSpec as P

NT = 2
NDIFF = 4
BETA_ENS = 0.8
BETA_STATIC = 0.6
DIFF_BASE = 0.06
LANES = 128
MESH = pl.DeviceIdType.MESH
F32 = jnp.float32
BF16 = jnp.bfloat16


def split3(x):
    a = x.astype(BF16)
    rest = x - a.astype(F32)
    b = rest.astype(BF16)
    c = (rest - b.astype(F32)).astype(BF16)
    return a, b, c


def left(x):
    return pltpu.roll(x, 1, 1)


def right(x):
    return pltpu.roll(x, x.shape[1] - 1, 1)


def kernel(
    factor,
    ens,
    tiles,
    ctl_hbm,
    stc,
    per_hbm,
    sigma,
    cls,
    east,
    north,
    ocol,
    ocnt,
    oval,
    owgt,
    oker,
    gens_hbm,
    gsta,
    gdep,
    ctl,
    per,
    gens,
    s_in,
    s_out,
    okb,
    dif,
    dif_u,
    dif_d,
    dbc,
    dsq,
    fin,
    sta,
    sta_u,
    sta_d,
    stb,
    wnd_u,
    wnd_d,
    rcv_wu,
    rcv_wd,
    cc,
    cu,
    cd,
    pp,
    ff,
    fu,
    fd,
    wa,
    wb,
    acc,
    accb,
    rbuf,
    obs_s,
    obs_r,
    onehot,
    himask,
    adjb,
    abuf,
    adjf,
    depp,
    dbuf,
    deps,
    depr,
    s_pre,
    r_pre,
    s_c,
    r_c,
    s_f,
    r_f,
    s_obs,
    r_obs,
    s_rs,
    r_rs,
    s_ag,
    r_ag,
    s_dg,
    r_dg,
    s_w,
    r_w,
    s_dep,
    r_dep,
):
    members, lev, rows, width = ctl.shape
    load_ctl = pltpu.make_async_copy(ctl_hbm, ctl, s_in.at[0])
    load_per = pltpu.make_async_copy(per_hbm, per, s_in.at[1])
    load_ctl.start()
    load_per.start()
    hi_n = NT * rows
    e = lax.axis_index("ens")
    t = lax.axis_index("tile")
    up = lax.rem(t + tiles - 1, tiles)
    down = lax.rem(t + 1, tiles)
    first = t == 0
    last = t == tiles - 1

    def remote(src, dst, ssem, rsem, e_to, t_to):
        return pltpu.make_async_remote_copy(
            src_ref=src,
            dst_ref=dst,
            send_sem=ssem,
            recv_sem=rsem,
            device_id=(e_to, t_to),
            device_id_type=MESH,
        )

    def loop(n, body):
        def step(i, carry):
            body(i)
            return carry

        lax.fori_loop(0, n, step, 0)

    def peer_e(k):
        return lax.rem(e + k, ens)

    def peer_t(k):
        return lax.rem(t + k, tiles)

    barrier = pltpu.get_barrier_semaphore()
    loop(
        tiles - 1,
        lambda k: pl.semaphore_signal(
            barrier, inc=1, device_id=(e, peer_t(k + 1)), device_id_type=MESH
        ),
    )
    loop(
        ens - 1,
        lambda k: pl.semaphore_signal(
            barrier, inc=1, device_id=(peer_e(k + 1), t), device_id_type=MESH
        ),
    )
    dif[...] = jnp.sqrt(DIFF_BASE * (cls[...].astype(F32) + 1.0))
    sub = lax.broadcasted_iota(jnp.int32, (lev, width), 0)
    scale = jnp.zeros((lev, width), F32)
    for l in range(lev):
        scale = jnp.where(sub == l, BETA_STATIC * sigma[l], scale)
    for r in range(rows):
        sta[r] = scale * stc[:, r, :]
    load_ctl.wait()
    pl.semaphore_wait(barrier, tiles - 1 + ens - 1)

    pre = [
        remote(dif, dif_u, s_pre.at[0], r_pre.at[0], e, down),
        remote(dif, dif_d, s_pre.at[1], r_pre.at[1], e, up),
        remote(sta.at[rows - 1], sta_u, s_pre.at[2], r_pre.at[2], e, down),
        remote(sta.at[0], sta_d, s_pre.at[3], r_pre.at[3], e, up),
    ]
    for copy in pre:
        copy.start()

    def halo(m, own, from_up, from_down, ssem, rsem):
        return (
            remote(own.at[m], from_up.at[m], ssem.at[0, m], rsem.at[0, m], e, down),
            remote(own.at[m], from_down.at[m], ssem.at[1, m], rsem.at[1, m], e, up),
        )

    def send_control(m):
        for r in range(rows):
            cc[m, r] = ctl[m, :, r, :]
        for copy in halo(m, cc, cu, cd, s_c, r_c):
            copy.start()

    def control_part(low, high):
        lax.fori_loop(low, high, lambda m, c: (send_control(m), c)[1], 0)

    control_part(0, members // 2)

    count = jnp.broadcast_to(ocnt[...].astype(F32), (tiles, tiles))
    d_sub = lax.broadcasted_iota(jnp.int32, (tiles, tiles), 0)
    d_lane = lax.broadcasted_iota(jnp.int32, (tiles, tiles), 1)
    count_col = jnp.sum(
        jnp.where(d_lane == d_sub, count, 0.0), axis=1, keepdims=True
    )
    start_col = jnp.sum(jnp.where(d_lane < d_sub, count, 0.0), axis=1, keepdims=True)
    start_row = jnp.sum(
        jnp.where(d_sub < d_lane, jnp.broadcast_to(count_col, (tiles, tiles)), 0.0),
        axis=0,
        keepdims=True,
    )
    begin = jnp.broadcast_to(start_col, (tiles, LANES)).astype(jnp.int32)
    shift = begin & (LANES - 1)
    lane = lax.broadcasted_iota(jnp.int32, (tiles, LANES), 1)
    usable = lane < jnp.broadcast_to(count_col, (tiles, LANES)).astype(jnp.int32)

    def turn(x, back):
        for bit in range(LANES.bit_length() - 1):
            by = LANES - (1 << bit) if back else 1 << bit
            x = jnp.where(shift & (1 << bit) != 0, pltpu.roll(x, by, 1), x)
        return x

    line_col = jnp.broadcast_to(start_col, (tiles, tiles)).astype(jnp.int32) // LANES
    pick = jnp.concatenate(
        [jnp.where(d_lane == line_col, 1.0, 0.0), jnp.where(d_lane == line_col + 1, 1.0, 0.0)],
        axis=0,
    ).astype(BF16)
    for b in range(tiles):
        okb[b] = oker[:, b * LANES : (b + 1) * LANES]
    for q in range(lev + 3):
        if q < lev:
            part = okb[:, q, :]
        else:
            part = (ocol, oval, owgt)[q - lev][...].astype(F32)
        two = sum(
            jnp.dot(pick, piece, preferred_element_type=F32) for piece in split3(part)
        )
        value = turn(jnp.where(lane >= shift, two[0:tiles], two[tiles : 2 * tiles]), True)
        if q == lev:
            value = jnp.where(usable, value, -1.0)
        obs_s[:, q, :] = value
    for q in range(lev + 3, 2 * lev):
        obs_s[:, q, :] = jnp.zeros((tiles, LANES), F32)

    def obs_copy(k):
        d = peer_t(k)
        return remote(obs_s.at[d], obs_r.at[t], s_obs.at[d], r_obs.at[t], e, d)

    loop(tiles - 1, lambda k: obs_copy(k + 1).start())
    control_part(members // 2, members)
    obs_r[t] = obs_s[t]

    def spread(m):
        for s in range(NT):
            block = per[s, m].astype(F32)
            for r in range(rows):
                pp[s, m, r] = block[:, r, :]

    load_per.wait()
    loop(members, spread)

    pre[0].wait_recv()
    pre[1].wait_recv()
    above = jnp.where(first, 0.0, dif_u[...])
    below = jnp.where(last, 0.0, dif_d[...])
    own = dif[...]
    total_rows = rows + 2 * NDIFF
    for i in range(total_rows):
        src = above if i < NDIFF else (own if i < NDIFF + rows else below)
        j = i if i < NDIFF else (i - NDIFF if i < NDIFF + rows else i - NDIFF - rows)
        line = jnp.broadcast_to(src[j : j + 1, :], (lev, width))
        dbc[i] = line
        dsq[i] = line * line
        if NDIFF <= i < NDIFF + rows:
            fin[i - NDIFF] = factor / line

    pre[2].wait_recv()
    pre[3].wait_recv()

    def winds(r):
        we = jnp.broadcast_to(east[r : r + 1, :], (lev, width))
        wn = jnp.broadcast_to(north[r : r + 1, :], (lev, width))
        return (
            jnp.maximum(we, 0.0),
            jnp.minimum(we, 0.0),
            jnp.maximum(wn, 0.0),
            jnp.minimum(wn, 0.0),
        )

    for r in range(rows):
        ep, em, np_, nm = winds(r)
        q = sta[r]
        above = sta[r - 1] if r else jnp.where(first, 0.0, sta_u[...])
        below = sta[r + 1] if r < rows - 1 else jnp.where(last, 0.0, sta_d[...])
        moved = q - ep * (q - left(q)) - em * (right(q) - q)
        moved = moved - np_ * (q - above) - nm * (below - q)
        for b in range(ens):
            stb[b, r] = q[:, b * LANES : (b + 1) * LANES]
            stb[b, rows + r] = moved[:, b * LANES : (b + 1) * LANES]

    def smooth(m, center, from_up, from_down):
        for i in range(total_rows):
            if i < NDIFF:
                line = from_up[m, i]
            elif i < NDIFF + rows:
                line = center[m, i - NDIFF]
            else:
                line = from_down[m, i - NDIFF - rows]
            wa[i] = dbc[i] * line
        src, dst = wa, wb
        for step in range(NDIFF):
            for i in range(step + 1, total_rows - 1 - step):
                w = src[i]
                lap = src[i + 1] + src[i - 1] + left(w) + right(w) - 4.0 * w
                dst[i] = w + dsq[i] * lap
            src, dst = dst, src
        return src

    for h in range(hi_n):
        acc[h] = jnp.zeros((lev, width), F32)

    def forward(m):
        for copy in halo(m, cc, cu, cd, s_c, r_c):
            copy.wait_recv()
        res = smooth(m, cc, cu, cd)
        for r in range(rows):
            w = res[NDIFF + r]
            for s in range(NT):
                acc[s * rows + r] += pp[s, m, r] * w

    loop(members, forward)

    for h in range(hi_n):
        value = acc[h] * fin[h % rows]
        for b in range(ens):
            accb[b, h] = value[:, b * LANES : (b + 1) * LANES]

    def rs_copy(k):
        to = peer_e(k)
        return remote(accb.at[to], rbuf.at[e], s_rs.at[to], r_rs.at[e], to, t)

    loop(ens - 1, lambda k: rs_copy(k + 1).start())

    def obs_wait(k):
        s = peer_t(k + 1)
        remote(obs_s.at[s], obs_r.at[s], s_obs.at[s], r_obs.at[s], e, s).wait_recv()

    loop(tiles - 1, obs_wait)
    pairs = tiles // 2

    def lines_of(g, i):
        return jnp.concatenate(
            [obs_r[2 * g, i : i + 1, :], obs_r[2 * g + 1, i : i + 1, :]], axis=1
        )

    lo_iota = lax.broadcasted_iota(jnp.int32, (LANES, 2 * LANES), 0)

    def hot(g):
        col = lines_of(g, lev).astype(jnp.int32)
        lo = col & (LANES - 1)
        block = (col // LANES) & (ens - 1)
        hi = col // width
        hi = jnp.where((col >= 0) & (block == e), hi, -1)
        himask[g] = jnp.broadcast_to(hi, (lev, 2 * LANES))
        onehot[g] = jnp.where(
            jnp.broadcast_to(lo, (LANES, 2 * LANES)) == lo_iota, 1.0, 0.0
        ).astype(BF16)

    loop(pairs, hot)

    def rs_wait(k):
        s = peer_e(k + 1)
        remote(accb.at[s], rbuf.at[s], s_rs.at[s], r_rs.at[s], s, t).wait_recv()

    loop(ens - 1, rs_wait)
    rbuf[e] = accb[e]
    parts = ([], [], [])
    for h in range(hi_n):
        value = stb[e, h]
        for b in range(ens):
            value = value + rbuf[b, h]
        for store, piece in zip(parts, split3(value)):
            store.append(piece)
    table = jnp.concatenate(parts[0] + parts[1] + parts[2], axis=0)
    points = hi_n * lev

    def observe(g, total):
        flat = jnp.dot(table, onehot[g], preferred_element_type=F32)
        flat = flat[0:points] + flat[points : 2 * points] + flat[2 * points : 3 * points]
        hi = himask[g]
        kern = jnp.concatenate(
            [obs_r[2 * g, 0:lev, :], obs_r[2 * g + 1, 0:lev, :]], axis=1
        )
        profile = jnp.zeros((lev, 2 * LANES), F32)
        for h in range(hi_n):
            profile = jnp.where(hi == h, flat[h * lev : (h + 1) * lev], profile)
        evolved = jnp.sum(kern * profile, axis=0, keepdims=True)
        dep = lines_of(g, lev + 2) * (evolved - lines_of(g, lev + 1))
        dep = jnp.where(hi[0:1] >= 0, dep, 0.0)
        depp[2 * g] = dep[:, 0:LANES]
        depp[2 * g + 1] = dep[:, LANES : 2 * LANES]
        push = kern * dep
        place = jnp.concatenate(
            [jnp.where(hi == h, push, 0.0) for h in range(hi_n)], axis=0
        )
        return total + lax.dot_general(
            jnp.concatenate(split3(place), axis=0),
            onehot[g],
            (((1,), (1,)), ((), ())),
            preferred_element_type=F32,
        )

    total = lax.fori_loop(0, pairs, observe, jnp.zeros((3 * points, LANES), F32))
    total = total[0:points] + total[points : 2 * points] + total[2 * points : 3 * points]
    for h in range(hi_n):
        adjb[h] = total[h * lev : (h + 1) * lev]

    def ag_copy(k):
        to = peer_e(k)
        return remote(adjb, abuf.at[e], s_ag.at[to], r_ag.at[e], to, t)

    def dg_copy(k):
        to = peer_e(k)
        return remote(depp, dbuf.at[e], s_dg.at[to], r_dg.at[e], to, t)

    loop(ens - 1, lambda k: ag_copy(k + 1).start())
    loop(ens - 1, lambda k: dg_copy(k + 1).start())
    abuf[e] = adjb[...]

    def ag_wait(k):
        s = peer_e(k + 1)
        remote(adjb, abuf.at[s], s_ag.at[s], r_ag.at[s], s, t).wait_recv()

    loop(ens - 1, ag_wait)
    for h in range(hi_n):
        adjf[h] = jnp.concatenate([abuf[b, h] for b in range(ens)], axis=1)

    wnd_u[...] = winds(0)[2] * adjf[rows]
    wnd_d[...] = winds(rows - 1)[3] * adjf[2 * rows - 1]
    wind = [
        remote(wnd_d, rcv_wu, s_w.at[0], r_w.at[0], e, down),
        remote(wnd_u, rcv_wd, s_w.at[1], r_w.at[1], e, up),
    ]
    for copy in wind:
        copy.start()

    def force(m):
        for r in range(rows):
            ff[m, r] = pp[0, m, r] * adjf[r] + pp[1, m, r] * adjf[rows + r]
        for copy in halo(m, ff, fu, fd, s_f, r_f):
            copy.start()

    loop(members, force)

    def dg_wait(k):
        s = peer_e(k + 1)
        remote(depp, dbuf.at[s], s_dg.at[s], r_dg.at[s], s, t).wait_recv()

    loop(ens - 1, dg_wait)
    dbuf[e] = depp[...]

    def gather_dep(s):
        value = dbuf[0, s]
        for b in range(1, ens):
            value = value + dbuf[b, s]
        deps[s] = value

    loop(tiles, gather_dep)

    def dep_copy(k):
        s = peer_t(k)
        return remote(deps.at[s], depr.at[t], s_dep.at[s], r_dep.at[t], e, s)

    loop(tiles - 1, lambda k: dep_copy(k + 1).start())
    depr[t] = deps[t]

    for copy in wind:
        copy.wait_recv()
    for r in range(rows):
        ep, em, np_, nm = winds(r)
        a = adjf[rows + r]
        if r < rows - 1:
            lower = winds(r + 1)[2] * adjf[rows + r + 1]
        else:
            lower = jnp.where(last, 0.0, rcv_wd[...])
        if r:
            upper = winds(r - 1)[3] * adjf[rows + r - 1]
        else:
            upper = jnp.where(first, 0.0, rcv_wu[...])
        moved = a * (1.0 - ep + em - np_ + nm) + right(ep * a) - left(em * a)
        moved = moved + lower - upper
        gsta[:, r, :] = stc[:, r, :] + scale * (adjf[r] + moved)

    def store_of(m):
        return pltpu.make_async_copy(gens.at[m], gens_hbm.at[m], s_out.at[m])

    def backward(m):
        for copy in halo(m, ff, fu, fd, s_f, r_f):
            copy.wait_recv()
        res = smooth(m, ff, fu, fd)
        for r in range(rows):
            gens[m, :, r, :] = cc[m, r] + res[NDIFF + r] * fin[r]
        store_of(m).start()

    loop(members, backward)

    def dep_wait(k):
        s = peer_t(k + 1)
        remote(deps.at[s], depr.at[s], s_dep.at[s], r_dep.at[s], e, s).wait_recv()

    loop(tiles - 1, dep_wait)
    line_row = jnp.broadcast_to(start_row, (tiles, tiles)).astype(jnp.int32) // LANES
    spread0 = jnp.where(d_sub == line_row, 1.0, 0.0).astype(BF16)
    spread1 = jnp.where(d_sub == line_row + 1, 1.0, 0.0).astype(BF16)
    value = turn(jnp.where(usable, depr[:, 0, :], 0.0), False)
    out = jnp.zeros((tiles, LANES), F32)
    for piece in split3(jnp.where(lane >= shift, value, 0.0)):
        out = out + jnp.dot(spread0, piece, preferred_element_type=F32)
    for piece in split3(jnp.where(lane < shift, value, 0.0)):
        out = out + jnp.dot(spread1, piece, preferred_element_type=F32)
    gdep[...] = out

    loop(members, lambda m: store_of(m).wait())
    for copy in pre + wind:
        copy.wait_send()

    def sent(m):
        for copy in halo(m, cc, cu, cd, s_c, r_c) + halo(m, ff, fu, fd, s_f, r_f):
            copy.wait_send()

    loop(members, sent)

    def sent_t(k):
        obs_copy(k + 1).wait_send()
        dep_copy(k + 1).wait_send()

    loop(tiles - 1, sent_t)

    def sent_e(k):
        rs_copy(k + 1).wait_send()
        ag_copy(k + 1).wait_send()
        dg_copy(k + 1).wait_send()

    loop(ens - 1, sent_e)


def hand_over(x0, x1, x2, y0, y1, y2, sems):
    copies = [
        pltpu.make_async_copy(x, y, sems.at[i])
        for i, (x, y) in enumerate(((x0, y0), (x1, y1), (x2, y2)))
    ]
    for copy in copies:
        copy.start()
    for copy in copies:
        copy.wait()


def per_device(
    ens_control,
    static_control,
    perturbations,
    level_sigma,
    length_class,
    courant_east,
    courant_north,
    obs_column,
    obs_count,
    obs_value,
    obs_weight,
    obs_kernel,
):
    members, lev, rows, width = ens_control.shape
    ens = lax.axis_size("ens")
    tiles = lax.axis_size("tile")
    factor = BETA_ENS / math.sqrt(ens * members - 1)
    hi_n = NT * rows
    vmem = lambda *shape, dtype=F32: pltpu.VMEM(shape, dtype)
    dma = lambda *shape: pltpu.SemaphoreType.DMA(shape)
    line = (lev, width)
    total_rows = rows + 2 * NDIFF
    fields = (members, rows) + line
    scratch = [
        vmem(*ens_control.shape),
        vmem(*perturbations.shape, dtype=BF16),
        vmem(*ens_control.shape),
        dma(2),
        dma(members),
        vmem(tiles, lev, LANES),
        vmem(rows, width),
        vmem(rows, width),
        vmem(rows, width),
        vmem(total_rows, *line),
        vmem(total_rows, *line),
        vmem(rows, *line),
        vmem(rows, *line),
        vmem(*line),
        vmem(*line),
        vmem(ens, hi_n, lev, LANES),
        vmem(*line),
        vmem(*line),
        vmem(*line),
        vmem(*line),
        vmem(*fields),
        vmem(*fields),
        vmem(*fields),
        vmem(NT, *fields),
        vmem(*fields),
        vmem(*fields),
        vmem(*fields),
        vmem(total_rows, *line),
        vmem(total_rows, *line),
        vmem(hi_n, *line),
        vmem(ens, hi_n, lev, LANES),
        vmem(ens, hi_n, lev, LANES),
        vmem(tiles, 2 * lev, LANES),
        vmem(tiles, 2 * lev, LANES),
        vmem(tiles // 2, LANES, 2 * LANES, dtype=BF16),
        vmem(tiles // 2, lev, 2 * LANES, dtype=jnp.int32),
        vmem(hi_n, lev, LANES),
        vmem(ens, hi_n, lev, LANES),
        vmem(hi_n, *line),
        vmem(tiles, 1, LANES),
        vmem(ens, tiles, 1, LANES),
        vmem(tiles, 1, LANES),
        vmem(tiles, 1, LANES),
        dma(4), dma(4),
        dma(2, members), dma(2, members),
        dma(2, members), dma(2, members),
        dma(tiles), dma(tiles),
        dma(ens), dma(ens),
        dma(ens), dma(ens),
        dma(ens), dma(ens),
        dma(2), dma(2),
        dma(tiles), dma(tiles),
    ]
    v = pl.BlockSpec(memory_space=pltpu.VMEM)
    s = pl.BlockSpec(memory_space=pltpu.SMEM)
    a = pl.BlockSpec(memory_space=pl.ANY)
    shape = jax.ShapeDtypeStruct
    grad_ens, grad_static, departures = pl.pallas_call(
        functools.partial(kernel, factor, ens, tiles),
        out_shape=(
            shape(ens_control.shape, F32),
            shape(static_control.shape, F32),
            shape((tiles, LANES), F32),
        ),
        in_specs=[a, v, a, s, v, v, v, v, v, v, v, v],
        out_specs=(a, v, v),
        scratch_shapes=scratch,
        name="gradient",
        compiler_params=pltpu.CompilerParams(
            collective_id=0, has_side_effects=True, vmem_limit_bytes=56 * 2**20
        ),
    )(
        ens_control,
        static_control,
        perturbations,
        level_sigma,
        length_class,
        courant_east,
        courant_north,
        obs_column.reshape(tiles, LANES),
        obs_count.reshape(1, tiles),
        obs_value.reshape(tiles, LANES),
        obs_weight.reshape(tiles, LANES),
        obs_kernel,
    )
    grad_ens, grad_static, departures = pl.pallas_call(
        hand_over,
        out_shape=tuple(shape(x.shape, F32) for x in (grad_ens, grad_static, departures)),
        in_specs=[a, a, a],
        out_specs=(a, a, a),
        scratch_shapes=[dma(3)],
        name="results",
    )(grad_ens, grad_static, departures)
    return (grad_ens, grad_static, departures.reshape(-1))


def solution(mesh):
    return jax.shard_map(
        per_device,
        mesh=mesh,
        in_specs=(
            P("ens", None, "tile", None),
            P(None, "tile", None),
            P(None, "ens", None, "tile", None),
            P(),
            P("tile", None),
            P("tile", None),
            P("tile", None),
            P("tile"),
            P("tile"),
            P("tile"),
            P("tile"),
            P(None, "tile"),
        ),
        out_specs=(P("ens", None, "tile", None), P(None, "tile", None), P("tile")),
        check_vma=False,
    )
```

```python
import functools
import math

import jax
import jax.numpy as jnp
from jax import lax
from jax.experimental import pallas as pl
from jax.experimental.pallas import tpu as pltpu
from jax.sharding import PartitionSpec as P

NT = 2
NDIFF = 4
BETA_ENS = 0.8
BETA_STATIC = 0.6
DIFF_BASE = 0.06
LANES = 128
MESH = pl.DeviceIdType.MESH
F32 = jnp.float32
BF16 = jnp.bfloat16


def split3(x):
    a = x.astype(BF16)
    rest = x - a.astype(F32)
    b = rest.astype(BF16)
    c = (rest - b.astype(F32)).astype(BF16)
    return a, b, c


def left(x):
    return pltpu.roll(x, 1, 1)


def right(x):
    return pltpu.roll(x, x.shape[1] - 1, 1)


def kernel(
    factor,
    ens,
    tiles,
    ctl_hbm,
    stc,
    per_hbm,
    sigma,
    cls,
    east,
    north,
    ocol,
    ocnt,
    oval,
    owgt,
    oker,
    gens_hbm,
    gsta,
    gdep,
    ctl,
    per,
    gens,
    s_in,
    s_out,
    okb,
    dif,
    dif_u,
    dif_d,
    dbc,
    dsq,
    fin,
    sta,
    sta_u,
    sta_d,
    stb,
    wnd_u,
    wnd_d,
    rcv_wu,
    rcv_wd,
    cc,
    cu,
    cd,
    pp,
    ff,
    fu,
    fd,
    wa,
    wb,
    acc,
    accb,
    rbuf,
    obs_s,
    obs_r,
    onehot,
    himask,
    adjb,
    abuf,
    adjf,
    depp,
    dbuf,
    deps,
    depr,
    s_pre,
    r_pre,
    s_c,
    r_c,
    s_f,
    r_f,
    s_obs,
    r_obs,
    s_rs,
    r_rs,
    s_ag,
    r_ag,
    s_dg,
    r_dg,
    s_w,
    r_w,
    s_dep,
    r_dep,
):
    members, lev, rows, width = ctl.shape
    load_ctl = pltpu.make_async_copy(ctl_hbm, ctl, s_in.at[0])
    load_per = pltpu.make_async_copy(per_hbm, per, s_in.at[1])
    load_ctl.start()
    load_per.start()
    hi_n = NT * rows
    e = lax.axis_index("ens")
    t = lax.axis_index("tile")
    up = lax.rem(t + tiles - 1, tiles)
    down = lax.rem(t + 1, tiles)
    first = t == 0
    last = t == tiles - 1

    def remote(src, dst, ssem, rsem, e_to, t_to):
        return pltpu.make_async_remote_copy(
            src_ref=src,
            dst_ref=dst,
            send_sem=ssem,
            recv_sem=rsem,
            device_id=(e_to, t_to),
            device_id_type=MESH,
        )

    def loop(n, body):
        def step(i, carry):
            body(i)
            return carry

        lax.fori_loop(0, n, step, 0)

    def peer_e(k):
        return lax.rem(e + k, ens)

    def peer_t(k):
        return lax.rem(t + k, tiles)

    barrier = pltpu.get_barrier_semaphore()
    loop(
        tiles - 1,
        lambda k: pl.semaphore_signal(
            barrier, inc=1, device_id=(e, peer_t(k + 1)), device_id_type=MESH
        ),
    )
    loop(
        ens - 1,
        lambda k: pl.semaphore_signal(
            barrier, inc=1, device_id=(peer_e(k + 1), t), device_id_type=MESH
        ),
    )
    dif[...] = jnp.sqrt(DIFF_BASE * (cls[...].astype(F32) + 1.0))
    sub = lax.broadcasted_iota(jnp.int32, (lev, width), 0)
    scale = jnp.zeros((lev, width), F32)
    for l in range(lev):
        scale = jnp.where(sub == l, BETA_STATIC * sigma[l], scale)
    for r in range(rows):
        sta[r] = scale * stc[:, r, :]
    load_ctl.wait()
    pl.semaphore_wait(barrier, tiles - 1 + ens - 1)

    pre = [
        remote(dif, dif_u, s_pre.at[0], r_pre.at[0], e, down),
        remote(dif, dif_d, s_pre.at[1], r_pre.at[1], e, up),
        remote(sta.at[rows - 1], sta_u, s_pre.at[2], r_pre.at[2], e, down),
        remote(sta.at[0], sta_d, s_pre.at[3], r_pre.at[3], e, up),
    ]
    for copy in pre:
        copy.start()

    def halo(m, own, from_up, from_down, ssem, rsem):
        return (
            remote(own.at[m], from_up.at[m], ssem.at[0, m], rsem.at[0, m], e, down),
            remote(own.at[m], from_down.at[m], ssem.at[1, m], rsem.at[1, m], e, up),
        )

    def send_control(m):
        for r in range(rows):
            cc[m, r] = ctl[m, :, r, :]
        for copy in halo(m, cc, cu, cd, s_c, r_c):
            copy.start()

    def control_part(low, high):
        lax.fori_loop(low, high, lambda m, c: (send_control(m), c)[1], 0)

    control_part(0, members // 2)

    count = jnp.broadcast_to(ocnt[...].astype(F32), (tiles, tiles))
    d_sub = lax.broadcasted_iota(jnp.int32, (tiles, tiles), 0)
    d_lane = lax.broadcasted_iota(jnp.int32, (tiles, tiles), 1)
    count_col = jnp.sum(
        jnp.where(d_lane == d_sub, count, 0.0), axis=1, keepdims=True
    )
    start_col = jnp.sum(jnp.where(d_lane < d_sub, count, 0.0), axis=1, keepdims=True)
    start_row = jnp.sum(
        jnp.where(d_sub < d_lane, jnp.broadcast_to(count_col, (tiles, tiles)), 0.0),
        axis=0,
        keepdims=True,
    )
    begin = jnp.broadcast_to(start_col, (tiles, LANES)).astype(jnp.int32)
    shift = begin & (LANES - 1)
    lane = lax.broadcasted_iota(jnp.int32, (tiles, LANES), 1)
    usable = lane < jnp.broadcast_to(count_col, (tiles, LANES)).astype(jnp.int32)

    def turn(x, back):
        for bit in range(LANES.bit_length() - 1):
            by = LANES - (1 << bit) if back else 1 << bit
            x = jnp.where(shift & (1 << bit) != 0, pltpu.roll(x, by, 1), x)
        return x

    line_col = jnp.broadcast_to(start_col, (tiles, tiles)).astype(jnp.int32) // LANES
    pick = jnp.concatenate(
        [jnp.where(d_lane == line_col, 1.0, 0.0), jnp.where(d_lane == line_col + 1, 1.0, 0.0)],
        axis=0,
    ).astype(BF16)
    for b in range(tiles):
        okb[b] = oker[:, b * LANES : (b + 1) * LANES]
    for q in range(lev + 3):
        if q < lev:
            part = okb[:, q, :]
        else:
            part = (ocol, oval, owgt)[q - lev][...].astype(F32)
        two = sum(
            jnp.dot(pick, piece, preferred_element_type=F32) for piece in split3(part)
        )
        value = turn(jnp.where(lane >= shift, two[0:tiles], two[tiles : 2 * tiles]), True)
        if q == lev:
            value = jnp.where(usable, value, -1.0)
        obs_s[:, q, :] = value
    for q in range(lev + 3, 2 * lev):
        obs_s[:, q, :] = jnp.zeros((tiles, LANES), F32)

    def obs_copy(k):
        d = peer_t(k)
        return remote(obs_s.at[d], obs_r.at[t], s_obs.at[d], r_obs.at[t], e, d)

    loop(tiles - 1, lambda k: obs_copy(k + 1).start())
    control_part(members // 2, members)
    obs_r[t] = obs_s[t]

    def spread(m):
        for s in range(NT):
            block = per[s, m].astype(F32)
            for r in range(rows):
                pp[s, m, r] = block[:, r, :]

    load_per.wait()
    loop(members, spread)

    pre[0].wait_recv()
    pre[1].wait_recv()
    above = jnp.where(first, 0.0, dif_u[...])
    below = jnp.where(last, 0.0, dif_d[...])
    own = dif[...]
    total_rows = rows + 2 * NDIFF
    for i in range(total_rows):
        src = above if i < NDIFF else (own if i < NDIFF + rows else below)
        j = i if i < NDIFF else (i - NDIFF if i < NDIFF + rows else i - NDIFF - rows)
        line = jnp.broadcast_to(src[j : j + 1, :], (lev, width))
        dbc[i] = line
        dsq[i] = line * line
        if NDIFF <= i < NDIFF + rows:
            fin[i - NDIFF] = factor / line

    pre[2].wait_recv()
    pre[3].wait_recv()

    def winds(r):
        we = jnp.broadcast_to(east[r : r + 1, :], (lev, width))
        wn = jnp.broadcast_to(north[r : r + 1, :], (lev, width))
        return (
            jnp.maximum(we, 0.0),
            jnp.minimum(we, 0.0),
            jnp.maximum(wn, 0.0),
            jnp.minimum(wn, 0.0),
        )

    for r in range(rows):
        ep, em, np_, nm = winds(r)
        q = sta[r]
        above = sta[r - 1] if r else jnp.where(first, 0.0, sta_u[...])
        below = sta[r + 1] if r < rows - 1 else jnp.where(last, 0.0, sta_d[...])
        moved = q - ep * (q - left(q)) - em * (right(q) - q)
        moved = moved - np_ * (q - above) - nm * (below - q)
        for b in range(ens):
            stb[b, r] = q[:, b * LANES : (b + 1) * LANES]
            stb[b, rows + r] = moved[:, b * LANES : (b + 1) * LANES]

    def smooth(m, center, from_up, from_down):
        for i in range(total_rows):
            if i < NDIFF:
                line = from_up[m, i]
            elif i < NDIFF + rows:
                line = center[m, i - NDIFF]
            else:
                line = from_down[m, i - NDIFF - rows]
            wa[i] = dbc[i] * line
        src, dst = wa, wb
        for step in range(NDIFF):
            for i in range(step + 1, total_rows - 1 - step):
                w = src[i]
                lap = src[i + 1] + src[i - 1] + left(w) + right(w) - 4.0 * w
                dst[i] = w + dsq[i] * lap
            src, dst = dst, src
        return src

    for h in range(hi_n):
        acc[h] = jnp.zeros((lev, width), F32)

    def forward(m):
        for copy in halo(m, cc, cu, cd, s_c, r_c):
            copy.wait_recv()
        res = smooth(m, cc, cu, cd)
        for r in range(rows):
            w = res[NDIFF + r]
            for s in range(NT):
                acc[s * rows + r] += pp[s, m, r] * w

    loop(members, forward)

    for h in range(hi_n):
        value = acc[h] * fin[h % rows]
        for b in range(ens):
            accb[b, h] = value[:, b * LANES : (b + 1) * LANES]

    def rs_copy(k):
        to = peer_e(k)
        return remote(accb.at[to], rbuf.at[e], s_rs.at[to], r_rs.at[e], to, t)

    loop(ens - 1, lambda k: rs_copy(k + 1).start())

    def obs_wait(k):
        s = peer_t(k + 1)
        remote(obs_s.at[s], obs_r.at[s], s_obs.at[s], r_obs.at[s], e, s).wait_recv()

    loop(tiles - 1, obs_wait)
    pairs = tiles // 2

    def lines_of(g, i):
        return jnp.concatenate(
            [obs_r[2 * g, i : i + 1, :], obs_r[2 * g + 1, i : i + 1, :]], axis=1
        )

    lo_iota = lax.broadcasted_iota(jnp.int32, (LANES, 2 * LANES), 0)

    def hot(g):
        col = lines_of(g, lev).astype(jnp.int32)
        lo = col & (LANES - 1)
        block = (col // LANES) & (ens - 1)
        hi = col // width
        hi = jnp.where((col >= 0) & (block == e), hi, -1)
        himask[g] = jnp.broadcast_to(hi, (lev, 2 * LANES))
        onehot[g] = jnp.where(
            jnp.broadcast_to(lo, (LANES, 2 * LANES)) == lo_iota, 1.0, 0.0
        ).astype(BF16)

    loop(pairs, hot)

    def rs_wait(k):
        s = peer_e(k + 1)
        remote(accb.at[s], rbuf.at[s], s_rs.at[s], r_rs.at[s], s, t).wait_recv()

    loop(ens - 1, rs_wait)
    rbuf[e] = accb[e]
    parts = ([], [], [])
    for h in range(hi_n):
        value = stb[e, h]
        for b in range(ens):
            value = value + rbuf[b, h]
        for store, piece in zip(parts, split3(value)):
            store.append(piece)
    table = jnp.concatenate(parts[0] + parts[1] + parts[2], axis=0)
    points = hi_n * lev

    def observe(g, total):
        flat = jnp.dot(table, onehot[g], preferred_element_type=F32)
        flat = flat[0:points] + flat[points : 2 * points] + flat[2 * points : 3 * points]
        hi = himask[g]
        kern = jnp.concatenate(
            [obs_r[2 * g, 0:lev, :], obs_r[2 * g + 1, 0:lev, :]], axis=1
        )
        profile = jnp.zeros((lev, 2 * LANES), F32)
        for h in range(hi_n):
            profile = jnp.where(hi == h, flat[h * lev : (h + 1) * lev], profile)
        evolved = jnp.sum(kern * profile, axis=0, keepdims=True)
        dep = lines_of(g, lev + 2) * (evolved - lines_of(g, lev + 1))
        dep = jnp.where(hi[0:1] >= 0, dep, 0.0)
        depp[2 * g] = dep[:, 0:LANES]
        depp[2 * g + 1] = dep[:, LANES : 2 * LANES]
        push = kern * dep
        place = jnp.concatenate(
            [jnp.where(hi == h, push, 0.0) for h in range(hi_n)], axis=0
        )
        return total + lax.dot_general(
            jnp.concatenate(split3(place), axis=0),
            onehot[g],
            (((1,), (1,)), ((), ())),
            preferred_element_type=F32,
        )

    total = lax.fori_loop(0, pairs, observe, jnp.zeros((3 * points, LANES), F32))
    total = total[0:points] + total[points : 2 * points] + total[2 * points : 3 * points]
    for h in range(hi_n):
        adjb[h] = total[h * lev : (h + 1) * lev]

    def ag_copy(k):
        to = peer_e(k)
        return remote(adjb, abuf.at[e], s_ag.at[to], r_ag.at[e], to, t)

    def dg_copy(k):
        to = peer_e(k)
        return remote(depp, dbuf.at[e], s_dg.at[to], r_dg.at[e], to, t)

    loop(ens - 1, lambda k: ag_copy(k + 1).start())
    loop(ens - 1, lambda k: dg_copy(k + 1).start())
    abuf[e] = adjb[...]

    def ag_wait(k):
        s = peer_e(k + 1)
        remote(adjb, abuf.at[s], s_ag.at[s], r_ag.at[s], s, t).wait_recv()

    loop(ens - 1, ag_wait)
    for h in range(hi_n):
        adjf[h] = jnp.concatenate([abuf[b, h] for b in range(ens)], axis=1)

    wnd_u[...] = winds(0)[2] * adjf[rows]
    wnd_d[...] = winds(rows - 1)[3] * adjf[2 * rows - 1]
    wind = [
        remote(wnd_d, rcv_wu, s_w.at[0], r_w.at[0], e, down),
        remote(wnd_u, rcv_wd, s_w.at[1], r_w.at[1], e, up),
    ]
    for copy in wind:
        copy.start()

    def force(m):
        for r in range(rows):
            ff[m, r] = pp[0, m, r] * adjf[r] + pp[1, m, r] * adjf[rows + r]
        for copy in halo(m, ff, fu, fd, s_f, r_f):
            copy.start()

    loop(members, force)

    def dg_wait(k):
        s = peer_e(k + 1)
        remote(depp, dbuf.at[s], s_dg.at[s], r_dg.at[s], s, t).wait_recv()

    loop(ens - 1, dg_wait)
    dbuf[e] = depp[...]

    def gather_dep(s):
        value = dbuf[0, s]
        for b in range(1, ens):
            value = value + dbuf[b, s]
        deps[s] = value

    loop(tiles, gather_dep)

    def dep_copy(k):
        s = peer_t(k)
        return remote(deps.at[s], depr.at[t], s_dep.at[s], r_dep.at[t], e, s)

    loop(tiles - 1, lambda k: dep_copy(k + 1).start())
    depr[t] = deps[t]

    for copy in wind:
        copy.wait_recv()
    for r in range(rows):
        ep, em, np_, nm = winds(r)
        a = adjf[rows + r]
        if r < rows - 1:
            lower = winds(r + 1)[2] * adjf[rows + r + 1]
        else:
            lower = jnp.where(last, 0.0, rcv_wd[...])
        if r:
            upper = winds(r - 1)[3] * adjf[rows + r - 1]
        else:
            upper = jnp.where(first, 0.0, rcv_wu[...])
        moved = a * (1.0 - ep + em - np_ + nm) + right(ep * a) - left(em * a)
        moved = moved + lower - upper
        gsta[:, r, :] = stc[:, r, :] + scale * (adjf[r] + moved)

    def store_of(m):
        return pltpu.make_async_copy(gens.at[m], gens_hbm.at[m], s_out.at[m])

    def backward(m):
        for copy in halo(m, ff, fu, fd, s_f, r_f):
            copy.wait_recv()
        res = smooth(m, ff, fu, fd)
        for r in range(rows):
            gens[m, :, r, :] = cc[m, r] + res[NDIFF + r] * fin[r]
        store_of(m).start()

    loop(members, backward)

    def dep_wait(k):
        s = peer_t(k + 1)
        remote(deps.at[s], depr.at[s], s_dep.at[s], r_dep.at[s], e, s).wait_recv()

    loop(tiles - 1, dep_wait)
    line_row = jnp.broadcast_to(start_row, (tiles, tiles)).astype(jnp.int32) // LANES
    spread0 = jnp.where(d_sub == line_row, 1.0, 0.0).astype(BF16)
    spread1 = jnp.where(d_sub == line_row + 1, 1.0, 0.0).astype(BF16)
    value = turn(jnp.where(usable, depr[:, 0, :], 0.0), False)
    out = jnp.zeros((tiles, LANES), F32)
    for piece in split3(jnp.where(lane >= shift, value, 0.0)):
        out = out + jnp.dot(spread0, piece, preferred_element_type=F32)
    for piece in split3(jnp.where(lane < shift, value, 0.0)):
        out = out + jnp.dot(spread1, piece, preferred_element_type=F32)
    gdep[...] = out

    loop(members, lambda m: store_of(m).wait())
    for copy in pre + wind:
        copy.wait_send()

    def sent(m):
        for copy in halo(m, cc, cu, cd, s_c, r_c) + halo(m, ff, fu, fd, s_f, r_f):
            copy.wait_send()

    loop(members, sent)

    def sent_t(k):
        obs_copy(k + 1).wait_send()
        dep_copy(k + 1).wait_send()

    loop(tiles - 1, sent_t)

    def sent_e(k):
        rs_copy(k + 1).wait_send()
        ag_copy(k + 1).wait_send()
        dg_copy(k + 1).wait_send()

    loop(ens - 1, sent_e)


def hand_over(x0, x1, x2, y0, y1, y2, b0, b1, b2, s_in, s_out):
    members = x0.shape[0]
    triples = [(x0.at[m], b0.at[m], y0.at[m]) for m in range(members)]
    triples += [(x1, b1, y1), (x2, b2, y2)]
    come = [
        pltpu.make_async_copy(x, b, s_in.at[i]) for i, (x, b, y) in enumerate(triples)
    ]
    go = [
        pltpu.make_async_copy(b, y, s_out.at[i]) for i, (x, b, y) in enumerate(triples)
    ]
    for copy in come:
        copy.start()
    for a, b in zip(come, go):
        a.wait()
        b.start()
    for copy in go:
        copy.wait()


def per_device(
    ens_control,
    static_control,
    perturbations,
    level_sigma,
    length_class,
    courant_east,
    courant_north,
    obs_column,
    obs_count,
    obs_value,
    obs_weight,
    obs_kernel,
):
    members, lev, rows, width = ens_control.shape
    ens = lax.axis_size("ens")
    tiles = lax.axis_size("tile")
    factor = BETA_ENS / math.sqrt(ens * members - 1)
    hi_n = NT * rows
    vmem = lambda *shape, dtype=F32: pltpu.VMEM(shape, dtype)
    dma = lambda *shape: pltpu.SemaphoreType.DMA(shape)
    line = (lev, width)
    total_rows = rows + 2 * NDIFF
    fields = (members, rows) + line
    scratch = [
        vmem(*ens_control.shape),
        vmem(*perturbations.shape, dtype=BF16),
        vmem(*ens_control.shape),
        dma(2),
        dma(members),
        vmem(tiles, lev, LANES),
        vmem(rows, width),
        vmem(rows, width),
        vmem(rows, width),
        vmem(total_rows, *line),
        vmem(total_rows, *line),
        vmem(rows, *line),
        vmem(rows, *line),
        vmem(*line),
        vmem(*line),
        vmem(ens, hi_n, lev, LANES),
        vmem(*line),
        vmem(*line),
        vmem(*line),
        vmem(*line),
        vmem(*fields),
        vmem(*fields),
        vmem(*fields),
        vmem(NT, *fields),
        vmem(*fields),
        vmem(*fields),
        vmem(*fields),
        vmem(total_rows, *line),
        vmem(total_rows, *line),
        vmem(hi_n, *line),
        vmem(ens, hi_n, lev, LANES),
        vmem(ens, hi_n, lev, LANES),
        vmem(tiles, 2 * lev, LANES),
        vmem(tiles, 2 * lev, LANES),
        vmem(tiles // 2, LANES, 2 * LANES, dtype=BF16),
        vmem(tiles // 2, lev, 2 * LANES, dtype=jnp.int32),
        vmem(hi_n, lev, LANES),
        vmem(ens, hi_n, lev, LANES),
        vmem(hi_n, *line),
        vmem(tiles, 1, LANES),
        vmem(ens, tiles, 1, LANES),
        vmem(tiles, 1, LANES),
        vmem(tiles, 1, LANES),
        dma(4), dma(4),
        dma(2, members), dma(2, members),
        dma(2, members), dma(2, members),
        dma(tiles), dma(tiles),
        dma(ens), dma(ens),
        dma(ens), dma(ens),
        dma(ens), dma(ens),
        dma(2), dma(2),
        dma(tiles), dma(tiles),
    ]
    v = pl.BlockSpec(memory_space=pltpu.VMEM)
    s = pl.BlockSpec(memory_space=pltpu.SMEM)
    a = pl.BlockSpec(memory_space=pl.ANY)
    shape = jax.ShapeDtypeStruct
    grad_ens, grad_static, departures = pl.pallas_call(
        functools.partial(kernel, factor, ens, tiles),
        out_shape=(
            shape(ens_control.shape, F32),
            shape(static_control.shape, F32),
            shape((tiles, LANES), F32),
        ),
        in_specs=[a, v, a, s, v, v, v, v, v, v, v, v],
        out_specs=(a, v, v),
        scratch_shapes=scratch,
        name="gradient",
        compiler_params=pltpu.CompilerParams(
            collective_id=0, has_side_effects=True, vmem_limit_bytes=56 * 2**20
        ),
    )(
        ens_control,
        static_control,
        perturbations,
        level_sigma,
        length_class,
        courant_east,
        courant_north,
        obs_column.reshape(tiles, LANES),
        obs_count.reshape(1, tiles),
        obs_value.reshape(tiles, LANES),
        obs_weight.reshape(tiles, LANES),
        obs_kernel,
    )
    grad_ens, grad_static, departures = pl.pallas_call(
        hand_over,
        out_shape=tuple(shape(x.shape, F32) for x in (grad_ens, grad_static, departures)),
        in_specs=[a, a, a],
        out_specs=(a, a, a),
        scratch_shapes=[
            vmem(*x.shape) for x in (grad_ens, grad_static, departures)
        ]
        + [dma(members + 2), dma(members + 2)],
        name="results",
    )(grad_ens, grad_static, departures)
    return (grad_ens, grad_static, departures.reshape(-1))


def solution(mesh):
    return jax.shard_map(
        per_device,
        mesh=mesh,
        in_specs=(
            P("ens", None, "tile", None),
            P(None, "tile", None),
            P(None, "ens", None, "tile", None),
            P(),
            P("tile", None),
            P("tile", None),
            P("tile", None),
            P("tile"),
            P("tile"),
            P("tile"),
            P("tile"),
            P(None, "tile"),
        ),
        out_specs=(P("ens", None, "tile", None), P(None, "tile", None), P("tile")),
        check_vma=False,
    )
```

```python
import functools
import math

import jax
import jax.numpy as jnp
from jax import lax
from jax.experimental import pallas as pl
from jax.experimental.pallas import tpu as pltpu
from jax.sharding import PartitionSpec as P

NT = 2
NDIFF = 4
BETA_ENS = 0.8
BETA_STATIC = 0.6
DIFF_BASE = 0.06
LANES = 128
MESH = pl.DeviceIdType.MESH
F32 = jnp.float32
BF16 = jnp.bfloat16


def split3(x):
    a = x.astype(BF16)
    rest = x - a.astype(F32)
    b = rest.astype(BF16)
    c = (rest - b.astype(F32)).astype(BF16)
    return a, b, c


def split2(x):
    a = x.astype(BF16).astype(F32)
    return a, x - a


def left(x):
    return pltpu.roll(x, 1, 1)


def right(x):
    return pltpu.roll(x, x.shape[1] - 1, 1)


def kernel(
    factor,
    ens,
    tiles,
    ctl_hbm,
    stc,
    per_hbm,
    sigma,
    cls,
    east,
    north,
    ocol,
    ocnt,
    oval,
    owgt,
    oker,
    gens_hbm,
    gsta,
    gdep,
    ctl,
    per,
    gens,
    s_in,
    s_out,
    okb,
    dif,
    dif_u,
    dif_d,
    dbc,
    dsq,
    fin,
    sta,
    sta_u,
    sta_d,
    stb,
    wnd_u,
    wnd_d,
    rcv_wu,
    rcv_wd,
    cc,
    cu,
    cd,
    pp,
    ff,
    fu,
    fd,
    wa,
    wb,
    acc,
    accb,
    rbuf,
    obs_s,
    obs_r,
    onehot,
    himask,
    okern,
    oaux,
    fe,
    eu,
    ed,
    pk,
    pk_u,
    pk_d,
    adjb,
    abuf,
    adjf,
    depp,
    dbuf,
    deps,
    depr,
    s_pre,
    r_pre,
    s_c,
    r_c,
    s_f,
    r_f,
    s_obs,
    r_obs,
    s_rs,
    r_rs,
    s_ag,
    r_ag,
    s_dg,
    r_dg,
    s_w,
    r_w,
    s_dep,
    r_dep,
    s_pk,
    r_pk,
):
    members, lev, rows, width = ctl.shape
    load_ctl = pltpu.make_async_copy(ctl_hbm, ctl, s_in.at[0])
    load_per = pltpu.make_async_copy(per_hbm, per, s_in.at[1])
    load_ctl.start()
    load_per.start()
    hi_n = NT * rows
    e = lax.axis_index("ens")
    t = lax.axis_index("tile")
    up = lax.rem(t + tiles - 1, tiles)
    down = lax.rem(t + 1, tiles)
    first = t == 0
    last = t == tiles - 1

    def remote(src, dst, ssem, rsem, e_to, t_to):
        return pltpu.make_async_remote_copy(
            src_ref=src,
            dst_ref=dst,
            send_sem=ssem,
            recv_sem=rsem,
            device_id=(e_to, t_to),
            device_id_type=MESH,
        )

    def loop(n, body):
        def step(i, carry):
            body(i)
            return carry

        lax.fori_loop(0, n, step, 0)

    def peer_e(k):
        return lax.rem(e + k, ens)

    def peer_t(k):
        return lax.rem(t + k, tiles)

    barrier = pltpu.get_barrier_semaphore()
    loop(
        tiles - 1,
        lambda k: pl.semaphore_signal(
            barrier, inc=1, device_id=(e, peer_t(k + 1)), device_id_type=MESH
        ),
    )
    loop(
        ens - 1,
        lambda k: pl.semaphore_signal(
            barrier, inc=1, device_id=(peer_e(k + 1), t), device_id_type=MESH
        ),
    )
    dif[...] = jnp.sqrt(DIFF_BASE * (cls[...].astype(F32) + 1.0))
    sub = lax.broadcasted_iota(jnp.int32, (lev, width), 0)
    scale = jnp.zeros((lev, width), F32)
    for l in range(lev):
        scale = jnp.where(sub == l, BETA_STATIC * sigma[l], scale)
    for r in range(rows):
        sta[r] = scale * stc[:, r, :]
    load_ctl.wait()
    pl.semaphore_wait(barrier, tiles - 1 + ens - 1)

    pre = [
        remote(dif, dif_u, s_pre.at[0], r_pre.at[0], e, down),
        remote(dif, dif_d, s_pre.at[1], r_pre.at[1], e, up),
        remote(sta.at[rows - 1], sta_u, s_pre.at[2], r_pre.at[2], e, down),
        remote(sta.at[0], sta_d, s_pre.at[3], r_pre.at[3], e, up),
    ]
    for copy in pre:
        copy.start()

    half = width // 2
    nb = half // LANES
    edge = NDIFF

    def halo(m, part, own, from_up, from_down, ssem, rsem):
        cols = pl.ds(part * half, half)
        src = own.at[m, :, :, cols]
        return (
            remote(
                src, from_up.at[m, :, :, cols], ssem.at[0, part, m], rsem.at[0, part, m], e, down
            ),
            remote(
                src, from_down.at[m, :, :, cols], ssem.at[1, part, m], rsem.at[1, part, m], e, up
            ),
        )

    def send_control(m):
        for r in range(rows):
            cc[m, r] = ctl[m, :, r, :]
        for copy in halo(m, 0, cc, cu, cd, s_c, r_c):
            copy.start()

    loop(members, send_control)

    count = jnp.broadcast_to(ocnt[...].astype(F32), (tiles, tiles))
    d_sub = lax.broadcasted_iota(jnp.int32, (tiles, tiles), 0)
    d_lane = lax.broadcasted_iota(jnp.int32, (tiles, tiles), 1)
    count_col = jnp.sum(
        jnp.where(d_lane == d_sub, count, 0.0), axis=1, keepdims=True
    )
    start_col = jnp.sum(jnp.where(d_lane < d_sub, count, 0.0), axis=1, keepdims=True)
    start_row = jnp.sum(
        jnp.where(d_sub < d_lane, jnp.broadcast_to(count_col, (tiles, tiles)), 0.0),
        axis=0,
        keepdims=True,
    )
    begin = jnp.broadcast_to(start_col, (tiles, LANES)).astype(jnp.int32)
    shift = begin & (LANES - 1)
    lane = lax.broadcasted_iota(jnp.int32, (tiles, LANES), 1)
    usable = lane < jnp.broadcast_to(count_col, (tiles, LANES)).astype(jnp.int32)

    def turn(x, back):
        for bit in range(LANES.bit_length() - 1):
            by = LANES - (1 << bit) if back else 1 << bit
            x = jnp.where(shift & (1 << bit) != 0, pltpu.roll(x, by, 1), x)
        return x

    line_col = jnp.broadcast_to(start_col, (tiles, tiles)).astype(jnp.int32) // LANES
    pick = jnp.concatenate(
        [jnp.where(d_lane == line_col, 1.0, 0.0), jnp.where(d_lane == line_col + 1, 1.0, 0.0)],
        axis=0,
    ).astype(BF16)
    for b in range(tiles):
        okb[b] = oker[:, b * LANES : (b + 1) * LANES]
    for q in range(lev + 3):
        if q < lev:
            part = okb[:, q, :]
        else:
            part = (ocol, oval, owgt)[q - lev][...].astype(F32)
        two = sum(
            jnp.dot(pick, piece, preferred_element_type=F32) for piece in split3(part)
        )
        value = turn(jnp.where(lane >= shift, two[0:tiles], two[tiles : 2 * tiles]), True)
        if q == lev:
            value = jnp.where(usable, value, -1.0)
        obs_s[:, q, :] = value
    for q in range(lev + 3, 2 * lev):
        obs_s[:, q, :] = jnp.zeros((tiles, LANES), F32)

    def obs_copy(k):
        d = peer_t(k)
        return remote(obs_s.at[d], obs_r.at[t], s_obs.at[d], r_obs.at[t], e, d)

    loop(tiles - 1, lambda k: obs_copy(k + 1).start())

    def send_second(m):
        for copy in halo(m, 1, cc, cu, cd, s_c, r_c):
            copy.start()

    loop(members, send_second)
    obs_r[t] = obs_s[t]

    def spread(m):
        for s in range(NT):
            block = per[s, m].astype(F32)
            for r in range(rows):
                pp[s, m, r] = block[:, r, :]

    load_per.wait()
    loop(members, spread)

    pre[0].wait_recv()
    pre[1].wait_recv()
    above = jnp.where(first, 0.0, dif_u[...])
    below = jnp.where(last, 0.0, dif_d[...])
    own = dif[...]
    total_rows = rows + 2 * NDIFF
    for i in range(total_rows):
        src = above if i < NDIFF else (own if i < NDIFF + rows else below)
        j = i if i < NDIFF else (i - NDIFF if i < NDIFF + rows else i - NDIFF - rows)
        line = jnp.broadcast_to(src[j : j + 1, :], (lev, width))
        dbc[i, :, 0:width] = line
        dsq[i, :, 0:width] = line * line
        dbc[i, :, width:] = line[:, 0:LANES]
        dsq[i, :, width:] = line[:, 0:LANES] * line[:, 0:LANES]
        if NDIFF <= i < NDIFF + rows:
            fin[i - NDIFF, :, 0:width] = factor / line
            fin[i - NDIFF, :, width:] = factor / line[:, 0:LANES]

    lane_u = lax.broadcasted_iota(jnp.int32, (lev, LANES), 1)

    def tile_of(x, b):
        return x[:, b * LANES : (b + 1) * LANES]

    def seam(head, tail):
        return jnp.where(
            lane_u < edge, head, jnp.where(lane_u >= LANES - edge, tail, 0.0)
        )

    pre[2].wait_recv()
    pre[3].wait_recv()

    def winds(r):
        we = jnp.broadcast_to(east[r : r + 1, :], (lev, width))
        wn = jnp.broadcast_to(north[r : r + 1, :], (lev, width))
        return (
            jnp.maximum(we, 0.0),
            jnp.minimum(we, 0.0),
            jnp.maximum(wn, 0.0),
            jnp.minimum(wn, 0.0),
        )

    for r in range(rows):
        ep, em, np_, nm = winds(r)
        q = sta[r]
        above = sta[r - 1] if r else jnp.where(first, 0.0, sta_u[...])
        below = sta[r + 1] if r < rows - 1 else jnp.where(last, 0.0, sta_d[...])
        moved = q - ep * (q - left(q)) - em * (right(q) - q)
        moved = moved - np_ * (q - above) - nm * (below - q)
        for s, value in enumerate((q, moved)):
            for b in range(nb):
                stb[s * nb + b, r] = tile_of(value, b)
                stb[s * nb + b, rows + r] = tile_of(value, nb + b)
            stb[s * rows + r, 2 * rows] = seam(tile_of(value, 0), tile_of(value, nb - 1))

    window = ((0, half), (half - LANES, width + LANES))

    def band(ref, part, *at):
        if part == 0:
            return ref[(*at, slice(None), slice(0, half))]
        return jnp.concatenate(
            [
                ref[(*at, slice(None), slice(half - LANES, width))],
                ref[(*at, slice(None), slice(0, LANES))],
            ],
            axis=1,
        )

    def band_e(ref, eref, m, r):
        fix = eref[m, r]
        return jnp.concatenate(
            [
                jnp.where(lane_u >= LANES - edge, fix, ref[m, r, :, half - LANES : half]),
                ref[m, r, :, half:width],
                jnp.where(lane_u < edge, fix, ref[m, r, :, 0:LANES]),
            ],
            axis=1,
        )

    def smooth(part, lines):
        a, b = window[part]
        n = b - a
        for i in range(total_rows):
            wa[i, :, 0:n] = dbc[i, :, a:b] * lines(i)
        src, dst = wa, wb
        for step in range(NDIFF):
            for i in range(step + 1, total_rows - 1 - step):
                w = src[i, :, 0:n]
                lap = src[i + 1, :, 0:n] + src[i - 1, :, 0:n]
                lap = lap + left(w) + right(w) - 4.0 * w
                dst[i, :, 0:n] = w + dsq[i, :, a:b] * lap
            src, dst = dst, src
        return [src[NDIFF + r, :, 0:n] for r in range(rows)]

    def source_of(i, refs):
        if i < NDIFF:
            return refs[0], i
        if i < NDIFF + rows:
            return refs[1], i - NDIFF
        return refs[2], i - NDIFF - rows

    def forward(part, m):
        for copy in halo(m, part, cc, cu, cd, s_c, r_c):
            copy.wait_recv()

        def lines(i):
            ref, r = source_of(i, (cu, cc, cd))
            return band(ref, part, m, r)

        n = window[part][1] - window[part][0]
        res = smooth(part, lines)
        for r in range(rows):
            for s in range(NT):
                h = s * rows + r
                acc[h, :, 0:n] = acc[h, :, 0:n] + band(pp, part, s, m, r) * res[r]

    ranges = ((0, rows), (rows, rows + 1))

    def clear():
        for h in range(hi_n):
            acc[h] = jnp.zeros(acc.shape[1:], F32)

    def rs_copy(part, k):
        to = peer_e(k)
        first_u, count_u = ranges[part]
        at = pl.ds(first_u, count_u)
        return remote(
            accb.at[to, at], rbuf.at[e, at], s_rs.at[part, to], r_rs.at[part, e], to, t
        )

    def rs_start(part):
        a, b = window[part]
        for s in range(NT):
            for r in range(rows):
                h = s * rows + r
                value = acc[h, :, 0 : b - a] * fin[r, :, a:b]
                for j in range(nb):
                    accb[s * nb + j, part * rows + r] = tile_of(value, j + part)
                if part:
                    accb[h, 2 * rows] = seam(tile_of(value, nb + 1), tile_of(value, 0))
        loop(ens - 1, lambda k: rs_copy(part, k + 1).start())

    def rs_wait(part):
        first_u, count_u = ranges[part]
        at = pl.ds(first_u, count_u)

        def one(k):
            s = peer_e(k + 1)
            remote(
                accb.at[s, at], rbuf.at[s, at], s_rs.at[part, s], r_rs.at[part, s], s, t
            ).wait_recv()

        loop(ens - 1, one)
        for u in range(first_u, first_u + count_u):
            rbuf[e, u] = accb[e, u]

    group = min(ens, tiles)
    chunks = tiles // group

    def obs_wait(k):
        s = peer_t(k + 1)
        remote(obs_s.at[s], obs_r.at[s], s_obs.at[s], r_obs.at[s], e, s).wait_recv()

    def lines_of(g, i, n=1):
        return jnp.concatenate(
            [obs_r[group * g + j, i : i + n, :] for j in range(group)], axis=1
        )

    lo_iota = lax.broadcasted_iota(jnp.int32, (LANES, group * LANES), 0)
    my_tile = lax.rem(e, nb)
    my_time = e // nb

    def hot(g):
        col = lines_of(g, lev).astype(jnp.int32)
        lo = col & (LANES - 1)
        block = (col // LANES) & (2 * nb - 1)
        hi = col // width
        row = hi & (rows - 1)
        seams = ((block == 0) & (lo < edge)) | ((block == nb - 1) & (lo >= LANES - edge))
        mine = ((block & (nb - 1)) == my_tile) & (hi // rows == my_time)
        unit = jnp.where(mine, jnp.where(block >= nb, rows + row, row), -1)
        unit = jnp.where(seams, jnp.where(hi == e, 2 * rows, -1), unit)
        unit = jnp.where(col >= 0, unit, -1)
        himask[g] = jnp.broadcast_to(unit, (lev, group * LANES))
        okern[g] = lines_of(g, 0, lev)
        oaux[g, 0:1, :] = lines_of(g, lev + 1)
        oaux[g, 1:2, :] = lines_of(g, lev + 2)
        onehot[g] = jnp.where(
            jnp.broadcast_to(lo, (LANES, group * LANES)) == lo_iota, 1.0, 0.0
        ).astype(BF16)

    def observe(part):
        first_u, count_u = ranges[part]
        points = count_u * lev
        values = []
        for u in range(first_u, first_u + count_u):
            value = stb[e, u]
            for b in range(ens):
                value = value + rbuf[b, u]
            values.append(value)
        table = jnp.concatenate(split2(jnp.concatenate(values, axis=0)), axis=0)
        table = table.astype(BF16)
        total = jnp.zeros((2 * points, LANES), F32)
        for g in range(chunks):
            hi = himask[g]
            kern = okern[g]
            flat = jnp.dot(table, onehot[g], preferred_element_type=F32)
            profile = jnp.zeros(kern.shape, F32)
            for j in range(count_u):
                value = flat[j * lev : (j + 1) * lev]
                value = value + flat[points + j * lev : points + (j + 1) * lev]
                profile = jnp.where(hi == first_u + j, value, profile)
            evolved = jnp.sum(kern * profile, axis=0, keepdims=True)
            dep = oaux[g, 1:2, :] * (evolved - oaux[g, 0:1, :])
            inside = (hi[0:1] >= first_u) & (hi[0:1] < first_u + count_u)
            dep = jnp.where(inside, dep, 0.0)
            for j in range(group):
                piece = dep[:, j * LANES : (j + 1) * LANES]
                depp[group * g + j] = piece if part == 0 else depp[group * g + j] + piece
            push = kern * dep
            place = jnp.concatenate(
                [jnp.where(hi == first_u + j, push, 0.0) for j in range(count_u)], axis=0
            )
            place = jnp.concatenate(split2(place), axis=0).astype(BF16)
            total = total + lax.dot_general(
                place, onehot[g], (((1,), (1,)), ((), ())), preferred_element_type=F32
            )
        total = total[0:points] + total[points : 2 * points]
        for j in range(count_u):
            adjb[first_u + j] = total[j * lev : (j + 1) * lev]
            abuf[e, first_u + j] = total[j * lev : (j + 1) * lev]
        loop(ens - 1, lambda k: ag_copy(part, k + 1).start())

    def ag_copy(part, k):
        to = peer_e(k)
        at = pl.ds(*ranges[part])
        return remote(
            adjb.at[at], abuf.at[e, at], s_ag.at[part, to], r_ag.at[part, e], to, t
        )

    def ag_wait(part):
        at = pl.ds(*ranges[part])

        def one(k):
            s = peer_e(k + 1)
            remote(
                adjb.at[at], abuf.at[s, at], s_ag.at[part, s], r_ag.at[part, s], s, t
            ).wait_recv()

        loop(ens - 1, one)
        for s in range(NT):
            for r in range(rows):
                adjf[s * rows + r, :, part * half : (part + 1) * half] = jnp.concatenate(
                    [abuf[s * nb + b, part * rows + r] for b in range(nb)], axis=1
                )

    def dg_copy(k):
        to = peer_e(k)
        return remote(depp, dbuf.at[e], s_dg.at[to], r_dg.at[e], to, t)

    def force(part, m):
        a, b = part * half, (part + 1) * half
        for r in range(rows):
            ff[m, r, :, a:b] = (
                pp[0, m, r, :, a:b] * adjf[r, :, a:b]
                + pp[1, m, r, :, a:b] * adjf[rows + r, :, a:b]
            )
        for copy in halo(m, part, ff, fu, fd, s_f, r_f):
            copy.start()

    def force_seams(m):
        for r in range(rows):
            head = (
                pp[0, m, r, :, 0:LANES] * abuf[r, 2 * rows]
                + pp[1, m, r, :, 0:LANES] * abuf[rows + r, 2 * rows]
            )
            tail = (
                pp[0, m, r, :, half - LANES : half] * abuf[r, 2 * rows]
                + pp[1, m, r, :, half - LANES : half] * abuf[rows + r, 2 * rows]
            )
            fe[m, r] = seam(head, tail)

    def backward_first(m):
        for copy in halo(m, 0, ff, fu, fd, s_f, r_f):
            copy.wait_recv()

        def lines(i):
            ref, r = source_of(i, (fu, ff, fd))
            return ref[m, r, :, 0:half]

        res = smooth(0, lines)
        for r in range(rows):
            gens[m, :, r, 0:half] = cc[m, r, :, 0:half] + res[r] * fin[r, :, 0:half]

    def store_of(m):
        return pltpu.make_async_copy(gens.at[m], gens_hbm.at[m], s_out.at[m])

    def backward_second(m):
        for copy in halo(m, 1, ff, fu, fd, s_f, r_f):
            copy.wait_recv()

        def lines(i):
            (ref, eref), r = source_of(i, ((fu, eu), (ff, fe), (fd, ed)))
            return band_e(ref, eref, m, r)

        res = smooth(1, lines)
        a, b = window[1]
        for r in range(rows):
            value = res[r] * fin[r, :, a:b] + band(cc, 1, m, r)
            gens[m, :, r, half:width] = value[:, LANES : LANES + half]
            gens[m, :, r, half - LANES : half] = jnp.where(
                lane_u >= LANES - 2 * edge, value[:, 0:LANES], gens[m, :, r, half - LANES : half]
            )
            gens[m, :, r, 0:LANES] = jnp.where(
                lane_u < 2 * edge, value[:, LANES + half :], gens[m, :, r, 0:LANES]
            )
        store_of(m).start()

    clear()
    loop(members, functools.partial(forward, 0))
    rs_start(0)
    clear()
    loop(tiles - 1, obs_wait)
    for g in range(chunks):
        hot(g)
    rs_wait(0)
    observe(0)
    loop(members, functools.partial(forward, 1))
    rs_start(1)
    ag_wait(0)
    loop(members, functools.partial(force, 0))
    rs_wait(1)
    observe(1)
    loop(ens - 1, lambda k: dg_copy(k + 1).start())
    early = members // 4
    loop(early, backward_first)
    ag_wait(1)
    for h in range(hi_n):
        fix = abuf[h, 2 * rows]
        adjf[h, :, 0:LANES] = adjf[h, :, 0:LANES] + jnp.where(lane_u < edge, fix, 0.0)
        adjf[h, :, half - LANES : half] = adjf[h, :, half - LANES : half] + jnp.where(
            lane_u >= LANES - edge, fix, 0.0
        )

    loop(members, force_seams)
    each = 2 * edge
    for r in range(rows):
        value = jnp.zeros((lev, LANES), F32)
        for m in range(members):
            spot = (lane_u >= m * each) & (lane_u < (m + 1) * each)
            value = jnp.where(spot, pltpu.roll(fe[m, r], edge + m * each, 1), value)
        pk[r] = value
    seams = [
        remote(pk, pk_u, s_pk.at[0], r_pk.at[0], e, down),
        remote(pk, pk_d, s_pk.at[1], r_pk.at[1], e, up),
    ]
    for copy in seams:
        copy.start()
    wnd_u[...] = winds(0)[2] * adjf[rows]
    wnd_d[...] = winds(rows - 1)[3] * adjf[2 * rows - 1]
    wind = [
        remote(wnd_d, rcv_wu, s_w.at[0], r_w.at[0], e, down),
        remote(wnd_u, rcv_wd, s_w.at[1], r_w.at[1], e, up),
    ]
    for copy in wind:
        copy.start()

    loop(members, functools.partial(force, 1))

    def dg_wait(k):
        s = peer_e(k + 1)
        remote(depp, dbuf.at[s], s_dg.at[s], r_dg.at[s], s, t).wait_recv()

    loop(ens - 1, dg_wait)
    dbuf[e] = depp[...]

    def gather_dep(s):
        value = dbuf[0, s]
        for b in range(1, ens):
            value = value + dbuf[b, s]
        deps[s] = value

    loop(tiles, gather_dep)

    def dep_copy(k):
        s = peer_t(k)
        return remote(deps.at[s], depr.at[t], s_dep.at[s], r_dep.at[t], e, s)

    loop(tiles - 1, lambda k: dep_copy(k + 1).start())
    depr[t] = deps[t]

    for copy in wind:
        copy.wait_recv()
    for r in range(rows):
        ep, em, np_, nm = winds(r)
        a = adjf[rows + r]
        if r < rows - 1:
            lower = winds(r + 1)[2] * adjf[rows + r + 1]
        else:
            lower = jnp.where(last, 0.0, rcv_wd[...])
        if r:
            upper = winds(r - 1)[3] * adjf[rows + r - 1]
        else:
            upper = jnp.where(first, 0.0, rcv_wu[...])
        moved = a * (1.0 - ep + em - np_ + nm) + right(ep * a) - left(em * a)
        moved = moved + lower - upper
        gsta[:, r, :] = stc[:, r, :] + scale * (adjf[r] + moved)

    lax.fori_loop(early, members, lambda m, c: (backward_first(m), c)[1], 0)
    for copy in seams:
        copy.wait_recv()
    for m in range(members):
        for r in range(rows):
            by = LANES - edge - m * each
            eu[m, r] = pltpu.roll(pk_u[r], by, 1)
            ed[m, r] = pltpu.roll(pk_d[r], by, 1)
    loop(members, backward_second)

    def dep_wait(k):
        s = peer_t(k + 1)
        remote(deps.at[s], depr.at[s], s_dep.at[s], r_dep.at[s], e, s).wait_recv()

    loop(tiles - 1, dep_wait)
    line_row = jnp.broadcast_to(start_row, (tiles, tiles)).astype(jnp.int32) // LANES
    spread0 = jnp.where(d_sub == line_row, 1.0, 0.0).astype(BF16)
    spread1 = jnp.where(d_sub == line_row + 1, 1.0, 0.0).astype(BF16)
    value = turn(jnp.where(usable, depr[:, 0, :], 0.0), False)
    out = jnp.zeros((tiles, LANES), F32)
    for piece in split3(jnp.where(lane >= shift, value, 0.0)):
        out = out + jnp.dot(spread0, piece, preferred_element_type=F32)
    for piece in split3(jnp.where(lane < shift, value, 0.0)):
        out = out + jnp.dot(spread1, piece, preferred_element_type=F32)
    gdep[...] = out

    loop(members, lambda m: store_of(m).wait())
    for copy in pre + wind + seams:
        copy.wait_send()

    def sent(m):
        for part in range(2):
            for copy in halo(m, part, cc, cu, cd, s_c, r_c):
                copy.wait_send()
            for copy in halo(m, part, ff, fu, fd, s_f, r_f):
                copy.wait_send()

    loop(members, sent)

    def sent_t(k):
        obs_copy(k + 1).wait_send()
        dep_copy(k + 1).wait_send()

    loop(tiles - 1, sent_t)

    def sent_e(k):
        for part in range(2):
            rs_copy(part, k + 1).wait_send()
            ag_copy(part, k + 1).wait_send()
        dg_copy(k + 1).wait_send()

    loop(ens - 1, sent_e)


def hand_over(x0, x1, x2, y0, y1, y2, b0, b1, b2, s_in, s_out):
    members = x0.shape[0]
    triples = [(x0.at[m], b0.at[m], y0.at[m]) for m in range(members)]
    triples += [(x1, b1, y1), (x2, b2, y2)]
    come = [
        pltpu.make_async_copy(x, b, s_in.at[i]) for i, (x, b, y) in enumerate(triples)
    ]
    go = [
        pltpu.make_async_copy(b, y, s_out.at[i]) for i, (x, b, y) in enumerate(triples)
    ]
    for copy in come:
        copy.start()
    for a, b in zip(come, go):
        a.wait()
        b.start()
    for copy in go:
        copy.wait()


def per_device(
    ens_control,
    static_control,
    perturbations,
    level_sigma,
    length_class,
    courant_east,
    courant_north,
    obs_column,
    obs_count,
    obs_value,
    obs_weight,
    obs_kernel,
):
    members, lev, rows, width = ens_control.shape
    ens = lax.axis_size("ens")
    tiles = lax.axis_size("tile")
    factor = BETA_ENS / math.sqrt(ens * members - 1)
    hi_n = NT * rows
    vmem = lambda *shape, dtype=F32: pltpu.VMEM(shape, dtype)
    dma = lambda *shape: pltpu.SemaphoreType.DMA(shape)
    line = (lev, width)
    wide = width + LANES
    band = width // 2 + 2 * LANES
    units = 2 * rows + 1
    chunks = max(1, tiles // ens)
    slots = min(ens, tiles) * LANES
    total_rows = rows + 2 * NDIFF
    fields = (members, rows) + line
    scratch = [
        vmem(*ens_control.shape),
        vmem(*perturbations.shape, dtype=BF16),
        vmem(*ens_control.shape),
        dma(2),
        dma(members),
        vmem(tiles, lev, LANES),
        vmem(rows, width),
        vmem(rows, width),
        vmem(rows, width),
        vmem(total_rows, lev, wide),
        vmem(total_rows, lev, wide),
        vmem(rows, lev, wide),
        vmem(rows, *line),
        vmem(*line),
        vmem(*line),
        vmem(ens, units, lev, LANES),
        vmem(*line),
        vmem(*line),
        vmem(*line),
        vmem(*line),
        vmem(*fields),
        vmem(*fields),
        vmem(*fields),
        vmem(NT, *fields),
        vmem(*fields),
        vmem(*fields),
        vmem(*fields),
        vmem(total_rows, lev, band),
        vmem(total_rows, lev, band),
        vmem(hi_n, lev, band),
        vmem(ens, units, lev, LANES),
        vmem(ens, units, lev, LANES),
        vmem(tiles, 2 * lev, LANES),
        vmem(tiles, 2 * lev, LANES),
        vmem(chunks, LANES, slots, dtype=BF16),
        vmem(chunks, lev, slots, dtype=jnp.int32),
        vmem(chunks, lev, slots),
        vmem(chunks, lev, slots),
        vmem(members, rows, lev, LANES),
        vmem(members, rows, lev, LANES),
        vmem(members, rows, lev, LANES),
        vmem(rows, lev, LANES),
        vmem(rows, lev, LANES),
        vmem(rows, lev, LANES),
        vmem(units, lev, LANES),
        vmem(ens, units, lev, LANES),
        vmem(hi_n, *line),
        vmem(tiles, 1, LANES),
        vmem(ens, tiles, 1, LANES),
        vmem(tiles, 1, LANES),
        vmem(tiles, 1, LANES),
        dma(4), dma(4),
        dma(2, 2, members), dma(2, 2, members),
        dma(2, 2, members), dma(2, 2, members),
        dma(tiles), dma(tiles),
        dma(2, ens), dma(2, ens),
        dma(2, ens), dma(2, ens),
        dma(ens), dma(ens),
        dma(2), dma(2),
        dma(tiles), dma(tiles),
        dma(2), dma(2),
    ]
    v = pl.BlockSpec(memory_space=pltpu.VMEM)
    s = pl.BlockSpec(memory_space=pltpu.SMEM)
    a = pl.BlockSpec(memory_space=pl.ANY)
    shape = jax.ShapeDtypeStruct
    grad_ens, grad_static, departures = pl.pallas_call(
        functools.partial(kernel, factor, ens, tiles),
        out_shape=(
            shape(ens_control.shape, F32),
            shape(static_control.shape, F32),
            shape((tiles, LANES), F32),
        ),
        in_specs=[a, v, a, s, v, v, v, v, v, v, v, v],
        out_specs=(a, v, v),
        scratch_shapes=scratch,
        name="gradient",
        compiler_params=pltpu.CompilerParams(
            collective_id=0, has_side_effects=True, vmem_limit_bytes=56 * 2**20
        ),
    )(
        ens_control,
        static_control,
        perturbations,
        level_sigma,
        length_class,
        courant_east,
        courant_north,
        obs_column.reshape(tiles, LANES),
        obs_count.reshape(1, tiles),
        obs_value.reshape(tiles, LANES),
        obs_weight.reshape(tiles, LANES),
        obs_kernel,
    )
    grad_ens, grad_static, departures = pl.pallas_call(
        hand_over,
        out_shape=tuple(shape(x.shape, F32) for x in (grad_ens, grad_static, departures)),
        in_specs=[a, a, a],
        out_specs=(a, a, a),
        scratch_shapes=[
            vmem(*x.shape) for x in (grad_ens, grad_static, departures)
        ]
        + [dma(members + 2), dma(members + 2)],
        name="results",
    )(grad_ens, grad_static, departures)
    return (grad_ens, grad_static, departures.reshape(-1))


def solution(mesh):
    return jax.shard_map(
        per_device,
        mesh=mesh,
        in_specs=(
            P("ens", None, "tile", None),
            P(None, "tile", None),
            P(None, "ens", None, "tile", None),
            P(),
            P("tile", None),
            P("tile", None),
            P("tile", None),
            P("tile"),
            P("tile"),
            P("tile"),
            P("tile"),
            P(None, "tile"),
        ),
        out_specs=(P("ens", None, "tile", None), P(None, "tile", None), P("tile")),
        check_vma=False,
    )
```

```python
import functools
import math

import jax
import jax.numpy as jnp
from jax import lax
from jax.experimental import pallas as pl
from jax.experimental.pallas import tpu as pltpu
from jax.sharding import PartitionSpec as P

NT = 2
NDIFF = 4
BETA_ENS = 0.8
BETA_STATIC = 0.6
DIFF_BASE = 0.06
LANES = 128
MESH = pl.DeviceIdType.MESH
F32 = jnp.float32
BF16 = jnp.bfloat16


def split3(x):
    a = x.astype(BF16)
    rest = x - a.astype(F32)
    b = rest.astype(BF16)
    c = (rest - b.astype(F32)).astype(BF16)
    return a, b, c


def split2(x):
    a = x.astype(BF16).astype(F32)
    return a, x - a


def left(x):
    return pltpu.roll(x, 1, 1)


def right(x):
    return pltpu.roll(x, x.shape[1] - 1, 1)


def kernel(
    factor,
    ens,
    tiles,
    ctl_hbm,
    stc,
    per_hbm,
    sigma,
    cls,
    east,
    north,
    ocol,
    ocnt,
    oval,
    owgt,
    oker,
    gens_hbm,
    gsta,
    gdep,
    ctl,
    per,
    gens,
    s_in,
    s_out,
    okb,
    dif,
    dif_u,
    dif_d,
    dbc,
    dsq,
    fin,
    sta,
    sta_u,
    sta_d,
    stb,
    wnd_u,
    wnd_d,
    rcv_wu,
    rcv_wd,
    cc,
    cu,
    cd,
    pp,
    ff,
    fu,
    fd,
    wa,
    wb,
    acc,
    accb,
    rbuf,
    xs,
    xr,
    obs_s,
    obs_r,
    onehot,
    himask,
    okern,
    oaux,
    fe,
    eu,
    ed,
    pk,
    pk_u,
    pk_d,
    adjb,
    abuf,
    adjf,
    depp,
    depx,
    dx,
    dbuf,
    deps,
    depr,
    depf,
    s_pre,
    r_pre,
    s_c,
    r_c,
    s_f,
    r_f,
    s_obs,
    r_obs,
    s_rs,
    r_rs,
    s_ag,
    r_ag,
    s_dg,
    r_dg,
    s_w,
    r_w,
    s_dep,
    r_dep,
    s_pk,
    r_pk,
    s_o2,
    r_o2,
    s_rx,
    r_rx,
    s_ax,
    r_ax,
    s_dx,
    r_dx,
    s_d2,
    r_d2,
):
    members, lev, rows, width = ctl.shape
    load_ctl = pltpu.make_async_copy(ctl_hbm, ctl, s_in.at[0])
    load_per = pltpu.make_async_copy(per_hbm, per, s_in.at[1])
    load_ctl.start()
    load_per.start()
    hi_n = NT * rows
    e = lax.axis_index("ens")
    t = lax.axis_index("tile")
    ny = ens // 2
    y = e // 2
    xl = lax.rem(e, 2)
    partner = 2 * y + 1 - xl
    group = tiles // ny
    kin = lax.rem(y - lax.rem(t, ny) + ny, ny)
    line_t = t // ny
    up = lax.rem(t + tiles - 1, tiles)
    down = lax.rem(t + 1, tiles)
    first = t == 0
    last = t == tiles - 1

    def remote(src, dst, ssem, rsem, e_to, t_to):
        return pltpu.make_async_remote_copy(
            src_ref=src,
            dst_ref=dst,
            send_sem=ssem,
            recv_sem=rsem,
            device_id=(e_to, t_to),
            device_id_type=MESH,
        )

    def loop(n, body):
        def step(i, carry):
            body(i)
            return carry

        lax.fori_loop(0, n, step, 0)

    def span(low, high, body):
        def step(i, carry):
            body(i)
            return carry

        lax.fori_loop(low, high, step, 0)

    def peer_y(k):
        return lax.rem(y + k, ny)

    def each_y(body):
        span(1, ny, lambda k: body(peer_y(k)))

    def each_kin(body):
        def one(j):
            pl.when(j * ny + kin != t)(lambda: body(j, j * ny + kin))

        loop(group, one)

    barrier = pltpu.get_barrier_semaphore()

    def greet(e_to, t_to):
        pl.semaphore_signal(barrier, inc=1, device_id=(e_to, t_to), device_id_type=MESH)

    greet(e, up)
    greet(e, down)
    each_kin(lambda j, d: greet(e, d))
    each_y(lambda b: greet(2 * b + xl, t))
    greet(partner, t)
    alone = jnp.where(kin == lax.rem(t, ny), 1, 0)
    dif[...] = jnp.sqrt(DIFF_BASE * (cls[...].astype(F32) + 1.0))
    sub = lax.broadcasted_iota(jnp.int32, (lev, width), 0)
    scale = jnp.zeros((lev, width), F32)
    for l in range(lev):
        scale = jnp.where(sub == l, BETA_STATIC * sigma[l], scale)
    for r in range(rows):
        sta[r] = scale * stc[:, r, :]
    load_ctl.wait()
    pl.semaphore_wait(barrier, 2 + group - alone + ny)

    pre = [
        remote(dif, dif_u, s_pre.at[0], r_pre.at[0], e, down),
        remote(dif, dif_d, s_pre.at[1], r_pre.at[1], e, up),
        remote(sta.at[rows - 1], sta_u, s_pre.at[2], r_pre.at[2], e, down),
        remote(sta.at[0], sta_d, s_pre.at[3], r_pre.at[3], e, up),
    ]
    for copy in pre:
        copy.start()

    half = width // 2
    nb = half // LANES
    edge = NDIFF

    def halo(m, part, own, from_up, from_down, ssem, rsem):
        src = own.at[m, part]
        return (
            remote(src, from_up.at[m, part], ssem.at[0, part, m], rsem.at[0, part, m], e, down),
            remote(src, from_down.at[m, part], ssem.at[1, part, m], rsem.at[1, part, m], e, up),
        )

    def send_control(m):
        for r in range(rows):
            for part in range(2):
                cc[m, part, r] = ctl[m, :, r, part * half : (part + 1) * half]
        for copy in halo(m, 0, cc, cu, cd, s_c, r_c):
            copy.start()

    ahead = members // 4
    span(0, ahead, send_control)

    count = jnp.broadcast_to(ocnt[...].astype(F32), (tiles, tiles))
    d_sub = lax.broadcasted_iota(jnp.int32, (tiles, tiles), 0)
    d_lane = lax.broadcasted_iota(jnp.int32, (tiles, tiles), 1)
    count_col = jnp.sum(
        jnp.where(d_lane == d_sub, count, 0.0), axis=1, keepdims=True
    )
    start_col = jnp.sum(jnp.where(d_lane < d_sub, count, 0.0), axis=1, keepdims=True)
    start_row = jnp.sum(
        jnp.where(d_sub < d_lane, jnp.broadcast_to(count_col, (tiles, tiles)), 0.0),
        axis=0,
        keepdims=True,
    )
    def places(start_of, count_of):
        shape = (start_of.shape[0], LANES)
        begin = jnp.broadcast_to(start_of, shape).astype(jnp.int32)
        lane = lax.broadcasted_iota(jnp.int32, shape, 1)
        usable = lane < jnp.broadcast_to(count_of, shape).astype(jnp.int32)
        return lane, begin & (LANES - 1), usable

    def turn(x, shift, back):
        for bit in range(LANES.bit_length() - 1):
            by = LANES - (1 << bit) if back else 1 << bit
            x = jnp.where(shift & (1 << bit) != 0, pltpu.roll(x, by, 1), x)
        return x

    kin_count = jnp.broadcast_to(ocnt[...].astype(F32), (group, tiles))
    kin_sub = lax.broadcasted_iota(jnp.int32, (group, tiles), 0) * ny + kin
    kin_lane = lax.broadcasted_iota(jnp.int32, (group, tiles), 1)
    kin_start = jnp.sum(
        jnp.where(kin_lane < kin_sub, kin_count, 0.0), axis=1, keepdims=True
    )
    kin_own = jnp.sum(
        jnp.where(kin_lane == kin_sub, kin_count, 0.0), axis=1, keepdims=True
    )
    lane, shift, usable = places(kin_start, kin_own)
    line_col = jnp.broadcast_to(kin_start, (group, tiles)).astype(jnp.int32) // LANES
    pick = jnp.concatenate(
        [
            jnp.where(kin_lane == line_col, 1.0, 0.0),
            jnp.where(kin_lane == line_col + 1, 1.0, 0.0),
        ],
        axis=0,
    ).astype(BF16)
    for b in range(tiles):
        okb[b] = oker[:, b * LANES : (b + 1) * LANES]
    for q in range(lev + 3):
        if q < lev:
            part = okb[:, q, :]
        else:
            part = (ocol, oval, owgt)[q - lev][...].astype(F32)
        two = sum(
            jnp.dot(pick, piece, preferred_element_type=F32) for piece in split3(part)
        )
        value = jnp.where(lane >= shift, two[0:group], two[group : 2 * group])
        value = turn(value, shift, True)
        if q == lev:
            value = jnp.where(usable, value, -1.0)
        obs_s[:, q, :] = value
    for q in range(lev + 3, 2 * lev):
        obs_s[:, q, :] = jnp.zeros((group, LANES), F32)

    def obs_copy(j, d):
        return remote(
            obs_s.at[j], obs_r.at[y, line_t], s_obs.at[j], r_obs.at[line_t], e, d
        )

    each_kin(lambda j, d: obs_copy(j, d).start())

    @pl.when(alone == 1)
    def _():
        obs_r[y, line_t] = obs_s[line_t]

    span(ahead, members, send_control)

    def send_second(m):
        for copy in halo(m, 1, cc, cu, cd, s_c, r_c):
            copy.start()

    def obs_on(b):
        return remote(obs_r.at[y], obs_r.at[y], s_o2.at[b], r_o2.at[y], 2 * b + xl, t)

    def obs_mid():
        each_kin(
            lambda j, d: remote(
                obs_s.at[j], obs_r.at[y, j], s_obs.at[j], r_obs.at[j], e, d
            ).wait_recv()
        )
        each_y(lambda b: obs_on(b).start())

    def obs_wait():
        each_y(
            lambda b: remote(
                obs_r.at[b], obs_r.at[b], s_o2.at[b], r_o2.at[b], 2 * b + xl, t
            ).wait_recv()
        )

    def spread(m):
        for s in range(NT):
            block = per[s, m].astype(F32)
            for r in range(rows):
                pp[s, m, r] = block[:, r, :]

    load_per.wait()
    loop(members, spread)

    pre[0].wait_recv()
    pre[1].wait_recv()
    above = jnp.where(first, 0.0, dif_u[...])
    below = jnp.where(last, 0.0, dif_d[...])
    own = dif[...]
    total_rows = rows + 2 * NDIFF
    for i in range(total_rows):
        src = above if i < NDIFF else (own if i < NDIFF + rows else below)
        j = i if i < NDIFF else (i - NDIFF if i < NDIFF + rows else i - NDIFF - rows)
        line = jnp.broadcast_to(src[j : j + 1, :], (lev, width))
        dbc[i, :, 0:width] = line
        dsq[i, :, 0:width] = line * line
        dbc[i, :, width:] = line[:, 0:LANES]
        dsq[i, :, width:] = line[:, 0:LANES] * line[:, 0:LANES]
        if NDIFF <= i < NDIFF + rows:
            fin[i - NDIFF, :, 0:width] = factor / line
            fin[i - NDIFF, :, width:] = factor / line[:, 0:LANES]

    lane_u = lax.broadcasted_iota(jnp.int32, (lev, LANES), 1)

    def tile_of(x, b):
        return x[:, b * LANES : (b + 1) * LANES]

    def seam(head, tail):
        return jnp.where(
            lane_u < edge, head, jnp.where(lane_u >= LANES - edge, tail, 0.0)
        )

    pre[2].wait_recv()
    pre[3].wait_recv()

    def winds(r):
        we = jnp.broadcast_to(east[r : r + 1, :], (lev, width))
        wn = jnp.broadcast_to(north[r : r + 1, :], (lev, width))
        return (
            jnp.maximum(we, 0.0),
            jnp.minimum(we, 0.0),
            jnp.maximum(wn, 0.0),
            jnp.minimum(wn, 0.0),
        )

    for r in range(rows):
        ep, em, np_, nm = winds(r)
        q = sta[r]
        above = sta[r - 1] if r else jnp.where(first, 0.0, sta_u[...])
        below = sta[r + 1] if r < rows - 1 else jnp.where(last, 0.0, sta_d[...])
        moved = q - ep * (q - left(q)) - em * (right(q) - q)
        moved = moved - np_ * (q - above) - nm * (below - q)
        for s, value in enumerate((q, moved)):
            for b in range(nb):
                stb[s * nb + b, r] = tile_of(value, b)
                stb[s * nb + b, rows + r] = tile_of(value, nb + b)
            stb[s * rows + r, 2 * rows] = seam(tile_of(value, 0), tile_of(value, nb - 1))

    window = ((0, half), (half - LANES, width + LANES))

    def band(ref, part, m, r):
        if part == 0:
            return ref[m, 0, r]
        return jnp.concatenate(
            [
                ref[m, 0, r, :, half - LANES : half],
                ref[m, 1, r],
                ref[m, 0, r, :, 0:LANES],
            ],
            axis=1,
        )

    def band_p(s, part, m, r):
        if part == 0:
            return pp[s, m, r, :, 0:half]
        return jnp.concatenate(
            [pp[s, m, r, :, half - LANES : width], pp[s, m, r, :, 0:LANES]], axis=1
        )

    def band_e(ref, eref, m, r):
        fix = eref[m, r]
        return jnp.concatenate(
            [
                jnp.where(lane_u >= LANES - edge, fix, ref[m, 0, r, :, half - LANES : half]),
                ref[m, 1, r],
                jnp.where(lane_u < edge, fix, ref[m, 0, r, :, 0:LANES]),
            ],
            axis=1,
        )

    def smooth(part, lines):
        a, b = window[part]
        n = b - a
        for i in range(total_rows):
            wa[i, :, 0:n] = dbc[i, :, a:b] * lines(i)
        src, dst = wa, wb
        for step in range(NDIFF):
            for i in range(step + 1, total_rows - 1 - step):
                w = src[i, :, 0:n]
                lap = src[i + 1, :, 0:n] + src[i - 1, :, 0:n]
                lap = lap + left(w) + right(w) - 4.0 * w
                dst[i, :, 0:n] = w + dsq[i, :, a:b] * lap
            src, dst = dst, src
        return [src[NDIFF + r, :, 0:n] for r in range(rows)]

    def source_of(i, refs):
        if i < NDIFF:
            return refs[0], i
        if i < NDIFF + rows:
            return refs[1], i - NDIFF
        return refs[2], i - NDIFF - rows

    def forward(part, m):
        for copy in halo(m, part, cc, cu, cd, s_c, r_c):
            copy.wait_recv()

        def lines(i):
            ref, r = source_of(i, (cu, cc, cd))
            return band(ref, part, m, r)

        n = window[part][1] - window[part][0]
        res = smooth(part, lines)
        for r in range(rows):
            for s in range(NT):
                h = s * rows + r
                acc[h, :, 0:n] = acc[h, :, 0:n] + band_p(s, part, m, r) * res[r]

    ranges = ((0, rows), (rows, rows + 1))

    def clear():
        for h in range(hi_n):
            acc[h] = jnp.zeros(acc.shape[1:], F32)

    def rs_copy(part, b):
        at = pl.ds(*ranges[part])
        return remote(
            accb.at[pl.ds(2 * b, 2), at],
            rbuf.at[y, :, at],
            s_rs.at[part, b],
            r_rs.at[part, y],
            2 * b + xl,
            t,
        )

    def rx_copy(part):
        at = pl.ds(*ranges[part])
        return remote(xs.at[at], xr.at[at], s_rx.at[part], r_rx.at[part], partner, t)

    def rs_start(part):
        a, b = window[part]
        for s in range(NT):
            for r in range(rows):
                h = s * rows + r
                value = acc[h, :, 0 : b - a] * fin[r, :, a:b]
                for j in range(nb):
                    accb[s * nb + j, part * rows + r] = tile_of(value, j + part)
                if part:
                    accb[h, 2 * rows] = seam(tile_of(value, nb + 1), tile_of(value, 0))
        each_y(lambda b: rs_copy(part, b).start())

    def rs_mid(part):
        first_u, count_u = ranges[part]
        at = pl.ds(first_u, count_u)
        each_y(
            lambda b: remote(
                accb.at[pl.ds(2 * b, 2), at],
                rbuf.at[b, :, at],
                s_rs.at[part, b],
                r_rs.at[part, b],
                2 * b + xl,
                t,
            ).wait_recv()
        )
        for u in range(first_u, first_u + count_u):
            for x in range(2):
                rbuf[y, x, u] = accb[2 * y + x, u]
            value = rbuf[0, 1 - xl, u]
            for b in range(1, ny):
                value = value + rbuf[b, 1 - xl, u]
            xs[u] = value
        rx_copy(part).start()

    chunks = ny

    def lines_of(g, i, n=1):
        return jnp.concatenate(
            [obs_r[g, j, i : i + n, :] for j in range(group)], axis=1
        )

    lo_iota = lax.broadcasted_iota(jnp.int32, (LANES, group * LANES), 0)
    my_tile = lax.rem(e, nb)
    my_time = e // nb

    def hot(g):
        col = lines_of(g, lev).astype(jnp.int32)
        lo = col & (LANES - 1)
        block = (col // LANES) & (2 * nb - 1)
        hi = col // width
        row = hi & (rows - 1)
        seams = ((block == 0) & (lo < edge)) | ((block == nb - 1) & (lo >= LANES - edge))
        mine = ((block & (nb - 1)) == my_tile) & (hi // rows == my_time)
        unit = jnp.where(mine, jnp.where(block >= nb, rows + row, row), -1)
        unit = jnp.where(seams, jnp.where(hi == e, 2 * rows, -1), unit)
        unit = jnp.where(col >= 0, unit, -1)
        himask[g] = jnp.broadcast_to(unit, (lev, group * LANES))
        okern[g] = lines_of(g, 0, lev)
        oaux[g, 0:1, :] = lines_of(g, lev + 1)
        oaux[g, 1:2, :] = lines_of(g, lev + 2)
        onehot[g] = jnp.where(
            jnp.broadcast_to(lo, (LANES, group * LANES)) == lo_iota, 1.0, 0.0
        ).astype(BF16)

    def observe(part):
        first_u, count_u = ranges[part]
        points = count_u * lev
        rx_copy(part).wait_recv()
        values = []
        for u in range(first_u, first_u + count_u):
            value = stb[e, u] + xr[u]
            for b in range(ny):
                value = value + rbuf[b, xl, u]
            values.append(value)
        table = jnp.concatenate(split2(jnp.concatenate(values, axis=0)), axis=0)
        table = table.astype(BF16)
        total = jnp.zeros((2 * points, LANES), F32)
        for g in range(chunks):
            hi = himask[g]
            kern = okern[g]
            flat = jnp.dot(table, onehot[g], preferred_element_type=F32)
            profile = jnp.zeros(kern.shape, F32)
            for j in range(count_u):
                value = flat[j * lev : (j + 1) * lev]
                value = value + flat[points + j * lev : points + (j + 1) * lev]
                profile = jnp.where(hi == first_u + j, value, profile)
            evolved = jnp.sum(kern * profile, axis=0, keepdims=True)
            dep = oaux[g, 1:2, :] * (evolved - oaux[g, 0:1, :])
            inside = (hi[0:1] >= first_u) & (hi[0:1] < first_u + count_u)
            dep = jnp.where(inside, dep, 0.0)
            for j in range(group):
                piece = dep[:, j * LANES : (j + 1) * LANES]
                depp[g, j] = piece if part == 0 else depp[g, j] + piece
            push = kern * dep
            place = jnp.concatenate(
                [jnp.where(hi == first_u + j, push, 0.0) for j in range(count_u)], axis=0
            )
            place = jnp.concatenate(split2(place), axis=0).astype(BF16)
            total = total + lax.dot_general(
                place, onehot[g], (((1,), (1,)), ((), ())), preferred_element_type=F32
            )
        total = total[0:points] + total[points : 2 * points]
        for j in range(count_u):
            adjb[first_u + j] = total[j * lev : (j + 1) * lev]
            abuf[e, first_u + j] = total[j * lev : (j + 1) * lev]
        ax_copy(part).start()

    def ax_copy(part):
        at = pl.ds(*ranges[part])
        return remote(
            adjb.at[at], abuf.at[e, at], s_ax.at[part], r_ax.at[part], partner, t
        )

    def ag_copy(part, b):
        here = abuf.at[pl.ds(2 * y, 2), pl.ds(*ranges[part])]
        return remote(here, here, s_ag.at[part, b], r_ag.at[part, y], 2 * b + xl, t)

    def ag_mid(part):
        at = pl.ds(*ranges[part])
        remote(
            adjb.at[at], abuf.at[partner, at], s_ax.at[part], r_ax.at[part], partner, t
        ).wait_recv()
        each_y(lambda b: ag_copy(part, b).start())

    def ag_wait(part):
        def one(b):
            there = abuf.at[pl.ds(2 * b, 2), pl.ds(*ranges[part])]
            remote(
                there, there, s_ag.at[part, b], r_ag.at[part, b], 2 * b + xl, t
            ).wait_recv()

        each_y(one)
        for s in range(NT):
            for r in range(rows):
                adjf[s * rows + r, :, part * half : (part + 1) * half] = jnp.concatenate(
                    [abuf[s * nb + b, part * rows + r] for b in range(nb)], axis=1
                )

    dx_copy = remote(depp, dx, s_dx.at[0], r_dx.at[0], partner, t)

    def dg_copy(b):
        return remote(depx, dbuf.at[y], s_dg.at[b], r_dg.at[y], 2 * b + xl, t)

    def dg_mid():
        dx_copy.wait_recv()
        depx[...] = depp[...] + dx[...]
        each_y(lambda b: dg_copy(b).start())

    def force(part, m):
        a, b = part * half, (part + 1) * half
        for r in range(rows):
            ff[m, part, r] = (
                pp[0, m, r, :, a:b] * adjf[r, :, a:b]
                + pp[1, m, r, :, a:b] * adjf[rows + r, :, a:b]
            )
        for copy in halo(m, part, ff, fu, fd, s_f, r_f):
            copy.start()

    def force_seams(m):
        for r in range(rows):
            head = (
                pp[0, m, r, :, 0:LANES] * abuf[r, 2 * rows]
                + pp[1, m, r, :, 0:LANES] * abuf[rows + r, 2 * rows]
            )
            tail = (
                pp[0, m, r, :, half - LANES : half] * abuf[r, 2 * rows]
                + pp[1, m, r, :, half - LANES : half] * abuf[rows + r, 2 * rows]
            )
            fe[m, r] = seam(head, tail)

    def backward_first(m):
        for copy in halo(m, 0, ff, fu, fd, s_f, r_f):
            copy.wait_recv()

        def lines(i):
            ref, r = source_of(i, (fu, ff, fd))
            return ref[m, 0, r]

        res = smooth(0, lines)
        for r in range(rows):
            gens[m, :, r, 0:half] = cc[m, 0, r] + res[r] * fin[r, :, 0:half]

    def store_of(m):
        return pltpu.make_async_copy(gens.at[m], gens_hbm.at[m], s_out.at[m])

    def backward_second(m):
        for copy in halo(m, 1, ff, fu, fd, s_f, r_f):
            copy.wait_recv()

        def lines(i):
            (ref, eref), r = source_of(i, ((fu, eu), (ff, fe), (fd, ed)))
            return band_e(ref, eref, m, r)

        res = smooth(1, lines)
        a, b = window[1]
        for r in range(rows):
            value = res[r] * fin[r, :, a:b] + band(cc, 1, m, r)
            gens[m, :, r, half:width] = value[:, LANES : LANES + half]
            gens[m, :, r, half - LANES : half] = jnp.where(
                lane_u >= LANES - 2 * edge, value[:, 0:LANES], gens[m, :, r, half - LANES : half]
            )
            gens[m, :, r, 0:LANES] = jnp.where(
                lane_u < 2 * edge, value[:, LANES + half :], gens[m, :, r, 0:LANES]
            )
        store_of(m).start()

    q1, q2 = members // 4, members * 5 // 8
    clear()
    span(0, members - q1, functools.partial(forward, 0))
    obs_mid()
    span(0, q1, send_second)
    span(members - q1, members, functools.partial(forward, 0))
    rs_start(0)
    span(q1, q1 + 1, send_second)
    clear()
    obs_wait()
    for g in range(chunks):
        hot(g)
    rs_mid(0)
    span(q1 + 1, q2, send_second)
    observe(0)
    span(q2, q2 + 1, send_second)
    span(0, q1, functools.partial(forward, 1))
    ag_mid(0)
    span(q2 + 1, members, send_second)
    span(q1, q2, functools.partial(forward, 1))
    ag_wait(0)
    span(0, q1, functools.partial(force, 0))
    span(q2, members, functools.partial(forward, 1))
    rs_start(1)
    span(q1, q1 + 1, functools.partial(force, 0))
    rs_mid(1)
    span(q1 + 1, q2, functools.partial(force, 0))
    observe(1)
    dx_copy.start()
    span(q2, q2 + 1, functools.partial(force, 0))
    ag_mid(1)
    dg_mid()
    span(q2 + 1, members, functools.partial(force, 0))
    early = members // 4
    loop(early, backward_first)
    ag_wait(1)
    for h in range(hi_n):
        fix = abuf[h, 2 * rows]
        adjf[h, :, 0:LANES] = adjf[h, :, 0:LANES] + jnp.where(lane_u < edge, fix, 0.0)
        adjf[h, :, half - LANES : half] = adjf[h, :, half - LANES : half] + jnp.where(
            lane_u >= LANES - edge, fix, 0.0
        )

    loop(members, force_seams)
    each = 2 * edge
    for r in range(rows):
        value = jnp.zeros((lev, LANES), F32)
        for m in range(members):
            spot = (lane_u >= m * each) & (lane_u < (m + 1) * each)
            value = jnp.where(spot, pltpu.roll(fe[m, r], edge + m * each, 1), value)
        pk[r] = value
    seams = [
        remote(pk, pk_u, s_pk.at[0], r_pk.at[0], e, down),
        remote(pk, pk_d, s_pk.at[1], r_pk.at[1], e, up),
    ]
    for copy in seams:
        copy.start()
    wnd_u[...] = winds(0)[2] * adjf[rows]
    wnd_d[...] = winds(rows - 1)[3] * adjf[2 * rows - 1]
    wind = [
        remote(wnd_d, rcv_wu, s_w.at[0], r_w.at[0], e, down),
        remote(wnd_u, rcv_wd, s_w.at[1], r_w.at[1], e, up),
    ]
    for copy in wind:
        copy.start()

    span(0, q1, functools.partial(force, 1))

    each_y(
        lambda b: remote(
            depx, dbuf.at[b], s_dg.at[b], r_dg.at[b], 2 * b + xl, t
        ).wait_recv()
    )
    dbuf[y] = depx[...]
    value = dbuf[0]
    for b in range(1, ny):
        value = value + dbuf[b]
    deps[...] = value

    def dep_copy(j, s):
        return remote(
            deps.at[y, j], depr.at[y, line_t], s_dep.at[j], r_dep.at[line_t], e, s
        )

    each_kin(lambda j, s: dep_copy(j, s).start())

    @pl.when(alone == 1)
    def _():
        depr[y, line_t] = deps[y, line_t]

    span(q1, q2, functools.partial(force, 1))
    each_kin(
        lambda j, s: remote(
            deps.at[y, j], depr.at[y, j], s_dep.at[j], r_dep.at[j], e, s
        ).wait_recv()
    )

    def dep_on(b):
        return remote(depr.at[y], depr.at[y], s_d2.at[b], r_d2.at[y], 2 * b + xl, t)

    each_y(lambda b: dep_on(b).start())
    span(q2, members, functools.partial(force, 1))

    for copy in wind:
        copy.wait_recv()
    for r in range(rows):
        ep, em, np_, nm = winds(r)
        a = adjf[rows + r]
        if r < rows - 1:
            lower = winds(r + 1)[2] * adjf[rows + r + 1]
        else:
            lower = jnp.where(last, 0.0, rcv_wd[...])
        if r:
            upper = winds(r - 1)[3] * adjf[rows + r - 1]
        else:
            upper = jnp.where(first, 0.0, rcv_wu[...])
        moved = a * (1.0 - ep + em - np_ + nm) + right(ep * a) - left(em * a)
        moved = moved + lower - upper
        gsta[:, r, :] = stc[:, r, :] + scale * (adjf[r] + moved)

    lax.fori_loop(early, members, lambda m, c: (backward_first(m), c)[1], 0)
    for copy in seams:
        copy.wait_recv()
    for m in range(members):
        for r in range(rows):
            by = LANES - edge - m * each
            eu[m, r] = pltpu.roll(pk_u[r], by, 1)
            ed[m, r] = pltpu.roll(pk_d[r], by, 1)
    loop(members, backward_second)

    each_y(
        lambda b: remote(
            depr.at[b], depr.at[b], s_d2.at[b], r_d2.at[b], 2 * b + xl, t
        ).wait_recv()
    )
    for d in range(tiles):
        depf[d : d + 1, :] = depr[lax.rem(t + d, ny), d // ny]
    lane, shift, usable = places(start_col, count_col)
    line_row = jnp.broadcast_to(start_row, (tiles, tiles)).astype(jnp.int32) // LANES
    spread0 = jnp.where(d_sub == line_row, 1.0, 0.0).astype(BF16)
    spread1 = jnp.where(d_sub == line_row + 1, 1.0, 0.0).astype(BF16)
    value = turn(jnp.where(usable, depf[...], 0.0), shift, False)
    out = jnp.zeros((tiles, LANES), F32)
    for piece in split3(jnp.where(lane >= shift, value, 0.0)):
        out = out + jnp.dot(spread0, piece, preferred_element_type=F32)
    for piece in split3(jnp.where(lane < shift, value, 0.0)):
        out = out + jnp.dot(spread1, piece, preferred_element_type=F32)
    gdep[...] = out

    loop(members, lambda m: store_of(m).wait())
    for copy in pre + wind + seams:
        copy.wait_send()

    def sent(m):
        for part in range(2):
            for copy in halo(m, part, cc, cu, cd, s_c, r_c):
                copy.wait_send()
            for copy in halo(m, part, ff, fu, fd, s_f, r_f):
                copy.wait_send()

    loop(members, sent)

    each_kin(lambda j, d: obs_copy(j, d).wait_send())
    each_kin(lambda j, d: dep_copy(j, d).wait_send())
    dx_copy.wait_send()
    for part in range(2):
        rx_copy(part).wait_send()
        ax_copy(part).wait_send()

    def sent_y(b):
        obs_on(b).wait_send()
        dep_on(b).wait_send()
        dg_copy(b).wait_send()
        for part in range(2):
            rs_copy(part, b).wait_send()
            ag_copy(part, b).wait_send()

    each_y(sent_y)


def hand_over(x0, x1, x2, y0, y1, y2, b0, b1, b2, s_in, s_out):
    members = x0.shape[0]
    triples = [(x0.at[m], b0.at[m], y0.at[m]) for m in range(members)]
    triples += [(x1, b1, y1), (x2, b2, y2)]
    come = [
        pltpu.make_async_copy(x, b, s_in.at[i]) for i, (x, b, y) in enumerate(triples)
    ]
    go = [
        pltpu.make_async_copy(b, y, s_out.at[i]) for i, (x, b, y) in enumerate(triples)
    ]
    for copy in come:
        copy.start()
    for a, b in zip(come, go):
        a.wait()
        b.start()
    for copy in go:
        copy.wait()


def per_device(
    ens_control,
    static_control,
    perturbations,
    level_sigma,
    length_class,
    courant_east,
    courant_north,
    obs_column,
    obs_count,
    obs_value,
    obs_weight,
    obs_kernel,
):
    members, lev, rows, width = ens_control.shape
    ens = lax.axis_size("ens")
    tiles = lax.axis_size("tile")
    factor = BETA_ENS / math.sqrt(ens * members - 1)
    hi_n = NT * rows
    vmem = lambda *shape, dtype=F32: pltpu.VMEM(shape, dtype)
    dma = lambda *shape: pltpu.SemaphoreType.DMA(shape)
    line = (lev, width)
    wide = width + LANES
    band = width // 2 + 2 * LANES
    units = 2 * rows + 1
    ny = ens // 2
    group = tiles // ny
    chunks = ny
    slots = group * LANES
    total_rows = rows + 2 * NDIFF
    fields = (members, rows) + line
    halves = (members, 2, rows, lev, width // 2)
    scratch = [
        vmem(*ens_control.shape),
        vmem(*perturbations.shape, dtype=BF16),
        vmem(*ens_control.shape),
        dma(2),
        dma(members),
        vmem(tiles, lev, LANES),
        vmem(rows, width),
        vmem(rows, width),
        vmem(rows, width),
        vmem(total_rows, lev, wide),
        vmem(total_rows, lev, wide),
        vmem(rows, lev, wide),
        vmem(rows, *line),
        vmem(*line),
        vmem(*line),
        vmem(ens, units, lev, LANES),
        vmem(*line),
        vmem(*line),
        vmem(*line),
        vmem(*line),
        vmem(*halves),
        vmem(*halves),
        vmem(*halves),
        vmem(NT, *fields),
        vmem(*halves),
        vmem(*halves),
        vmem(*halves),
        vmem(total_rows, lev, band),
        vmem(total_rows, lev, band),
        vmem(hi_n, lev, band),
        vmem(ens, units, lev, LANES),
        vmem(ny, 2, units, lev, LANES),
        vmem(units, lev, LANES),
        vmem(units, lev, LANES),
        vmem(group, 2 * lev, LANES),
        vmem(ny, group, 2 * lev, LANES),
        vmem(chunks, LANES, slots, dtype=BF16),
        vmem(chunks, lev, slots, dtype=jnp.int32),
        vmem(chunks, lev, slots),
        vmem(chunks, lev, slots),
        vmem(members, rows, lev, LANES),
        vmem(members, rows, lev, LANES),
        vmem(members, rows, lev, LANES),
        vmem(rows, lev, LANES),
        vmem(rows, lev, LANES),
        vmem(rows, lev, LANES),
        vmem(units, lev, LANES),
        vmem(ens, units, lev, LANES),
        vmem(hi_n, *line),
        vmem(ny, group, 1, LANES),
        vmem(ny, group, 1, LANES),
        vmem(ny, group, 1, LANES),
        vmem(ny, ny, group, 1, LANES),
        vmem(ny, group, 1, LANES),
        vmem(ny, group, 1, LANES),
        vmem(tiles, LANES),
        dma(4), dma(4),
        dma(2, 2, members), dma(2, 2, members),
        dma(2, 2, members), dma(2, 2, members),
        dma(group), dma(group),
        dma(2, ny), dma(2, ny),
        dma(2, ny), dma(2, ny),
        dma(ny), dma(ny),
        dma(2), dma(2),
        dma(group), dma(group),
        dma(2), dma(2),
        dma(ny), dma(ny),
        dma(2), dma(2),
        dma(2), dma(2),
        dma(1), dma(1),
        dma(ny), dma(ny),
    ]
    v = pl.BlockSpec(memory_space=pltpu.VMEM)
    s = pl.BlockSpec(memory_space=pltpu.SMEM)
    a = pl.BlockSpec(memory_space=pl.ANY)
    shape = jax.ShapeDtypeStruct
    grad_ens, grad_static, departures = pl.pallas_call(
        functools.partial(kernel, factor, ens, tiles),
        out_shape=(
            shape(ens_control.shape, F32),
            shape(static_control.shape, F32),
            shape((tiles, LANES), F32),
        ),
        in_specs=[a, v, a, s, v, v, v, v, v, v, v, v],
        out_specs=(a, v, v),
        scratch_shapes=scratch,
        name="gradient",
        compiler_params=pltpu.CompilerParams(
            collective_id=0, has_side_effects=True, vmem_limit_bytes=56 * 2**20
        ),
    )(
        ens_control,
        static_control,
        perturbations,
        level_sigma,
        length_class,
        courant_east,
        courant_north,
        obs_column.reshape(tiles, LANES),
        obs_count.reshape(1, tiles),
        obs_value.reshape(tiles, LANES),
        obs_weight.reshape(tiles, LANES),
        obs_kernel,
    )
    grad_ens, grad_static, departures = pl.pallas_call(
        hand_over,
        out_shape=tuple(shape(x.shape, F32) for x in (grad_ens, grad_static, departures)),
        in_specs=[a, a, a],
        out_specs=(a, a, a),
        scratch_shapes=[
            vmem(*x.shape) for x in (grad_ens, grad_static, departures)
        ]
        + [dma(members + 2), dma(members + 2)],
        name="results",
    )(grad_ens, grad_static, departures)
    return (grad_ens, grad_static, departures.reshape(-1))


def solution(mesh):
    return jax.shard_map(
        per_device,
        mesh=mesh,
        in_specs=(
            P("ens", None, "tile", None),
            P(None, "tile", None),
            P(None, "ens", None, "tile", None),
            P(),
            P("tile", None),
            P("tile", None),
            P("tile", None),
            P("tile"),
            P("tile"),
            P("tile"),
            P("tile"),
            P(None, "tile"),
        ),
        out_specs=(P("ens", None, "tile", None), P(None, "tile", None), P("tile")),
        check_vma=False,
    )
```

```python
import functools
import math

import jax
import jax.numpy as jnp
from jax import lax
from jax.experimental import pallas as pl
from jax.experimental.pallas import tpu as pltpu
from jax.sharding import PartitionSpec as P

NT = 2
NDIFF = 4
BETA_ENS = 0.8
BETA_STATIC = 0.6
DIFF_BASE = 0.06
LANES = 128
MESH = pl.DeviceIdType.MESH
F32 = jnp.float32
BF16 = jnp.bfloat16


def split3(x):
    a = x.astype(BF16)
    rest = x - a.astype(F32)
    b = rest.astype(BF16)
    c = (rest - b.astype(F32)).astype(BF16)
    return a, b, c


def split2(x):
    a = x.astype(BF16).astype(F32)
    return a, x - a


def left(x):
    return pltpu.roll(x, 1, 1)


def right(x):
    return pltpu.roll(x, x.shape[1] - 1, 1)


def kernel(
    factor,
    ens,
    tiles,
    ctl_hbm,
    stc,
    per_hbm,
    sigma,
    cls,
    east,
    north,
    ocol,
    ocnt,
    oval,
    owgt,
    oker,
    gens_hbm,
    gsta,
    gdep,
    ctl,
    per,
    gens,
    s_in,
    s_out,
    okb,
    dif,
    dif_u,
    dif_d,
    dbc,
    dsq,
    fin,
    sta,
    sta_u,
    sta_d,
    stb,
    wnd_u,
    wnd_d,
    rcv_wu,
    rcv_wd,
    cc,
    cu,
    cd,
    pp,
    ff,
    fu,
    fd,
    wa,
    wb,
    acc,
    accb,
    rbuf,
    obs_s,
    obs_r,
    onehot,
    himask,
    okern,
    oaux,
    adjb,
    abuf,
    adjf,
    depp,
    depx,
    dx,
    dbuf,
    deps,
    depr,
    depf,
    s_pre,
    r_pre,
    s_c,
    r_c,
    s_f,
    r_f,
    s_obs,
    r_obs,
    s_rs,
    r_rs,
    s_ag,
    r_ag,
    s_dg,
    r_dg,
    s_w,
    r_w,
    s_dep,
    r_dep,
    s_o2,
    r_o2,
    s_dx,
    r_dx,
    s_d2,
    r_d2,
):
    members, lev, rows, width = ctl.shape
    load_ctl = pltpu.make_async_copy(ctl_hbm, ctl, s_in.at[0])
    load_per = pltpu.make_async_copy(per_hbm, per, s_in.at[1])
    load_ctl.start()
    load_per.start()
    hi_n = NT * rows
    e = lax.axis_index("ens")
    t = lax.axis_index("tile")
    ny = ens // 2
    y = e // 2
    xl = lax.rem(e, 2)
    partner = 2 * y + 1 - xl
    group = tiles // ny
    kin = lax.rem(y - lax.rem(t, ny) + ny, ny)
    line_t = t // ny
    up = lax.rem(t + tiles - 1, tiles)
    down = lax.rem(t + 1, tiles)
    first = t == 0
    last = t == tiles - 1

    def remote(src, dst, ssem, rsem, e_to, t_to):
        return pltpu.make_async_remote_copy(
            src_ref=src,
            dst_ref=dst,
            send_sem=ssem,
            recv_sem=rsem,
            device_id=(e_to, t_to),
            device_id_type=MESH,
        )

    def loop(n, body):
        def step(i, carry):
            body(i)
            return carry

        lax.fori_loop(0, n, step, 0)

    def span(low, high, body):
        def step(i, carry):
            body(i)
            return carry

        lax.fori_loop(low, high, step, 0)

    def each_e(body):
        span(1, ens, lambda k: body(lax.rem(e + k, ens)))

    def peer_y(k):
        return lax.rem(y + k, ny)

    def each_y(body):
        span(1, ny, lambda k: body(peer_y(k)))

    def each_kin(body):
        def one(j):
            pl.when(j * ny + kin != t)(lambda: body(j, j * ny + kin))

        loop(group, one)

    barrier = pltpu.get_barrier_semaphore()

    def greet(e_to, t_to):
        pl.semaphore_signal(barrier, inc=1, device_id=(e_to, t_to), device_id_type=MESH)

    greet(e, up)
    greet(e, down)
    each_kin(lambda j, d: greet(e, d))
    each_e(lambda b: greet(b, t))
    alone = jnp.where(kin == lax.rem(t, ny), 1, 0)
    dif[...] = jnp.sqrt(DIFF_BASE * (cls[...].astype(F32) + 1.0))
    sub = lax.broadcasted_iota(jnp.int32, (lev, width), 0)
    scale = jnp.zeros((lev, width), F32)
    for l in range(lev):
        scale = jnp.where(sub == l, BETA_STATIC * sigma[l], scale)
    for r in range(rows):
        sta[r] = scale * stc[:, r, :]
    load_ctl.wait()
    pl.semaphore_wait(barrier, 2 + group - alone + ens - 1)

    pre = [
        remote(dif, dif_u, s_pre.at[0], r_pre.at[0], e, down),
        remote(dif, dif_d, s_pre.at[1], r_pre.at[1], e, up),
        remote(sta.at[rows - 1], sta_u, s_pre.at[2], r_pre.at[2], e, down),
        remote(sta.at[0], sta_d, s_pre.at[3], r_pre.at[3], e, up),
    ]
    for copy in pre:
        copy.start()

    def halo(m, own, from_up, from_down, ssem, rsem):
        src = own.at[m]
        return (
            remote(src, from_up.at[m], ssem.at[0, m], rsem.at[0, m], e, down),
            remote(src, from_down.at[m], ssem.at[1, m], rsem.at[1, m], e, up),
        )

    def send_control(m):
        for r in range(rows):
            cc[m, r] = ctl[m, :, r, :]
        for copy in halo(m, cc, cu, cd, s_c, r_c):
            copy.start()

    ahead = members // 4
    span(0, ahead, send_control)

    count = jnp.broadcast_to(ocnt[...].astype(F32), (tiles, tiles))
    d_sub = lax.broadcasted_iota(jnp.int32, (tiles, tiles), 0)
    d_lane = lax.broadcasted_iota(jnp.int32, (tiles, tiles), 1)
    count_col = jnp.sum(
        jnp.where(d_lane == d_sub, count, 0.0), axis=1, keepdims=True
    )
    start_col = jnp.sum(jnp.where(d_lane < d_sub, count, 0.0), axis=1, keepdims=True)
    start_row = jnp.sum(
        jnp.where(d_sub < d_lane, jnp.broadcast_to(count_col, (tiles, tiles)), 0.0),
        axis=0,
        keepdims=True,
    )
    def places(start_of, count_of):
        shape = (start_of.shape[0], LANES)
        begin = jnp.broadcast_to(start_of, shape).astype(jnp.int32)
        lane = lax.broadcasted_iota(jnp.int32, shape, 1)
        usable = lane < jnp.broadcast_to(count_of, shape).astype(jnp.int32)
        return lane, begin & (LANES - 1), usable

    def turn(x, shift, back):
        for bit in range(LANES.bit_length() - 1):
            by = LANES - (1 << bit) if back else 1 << bit
            x = jnp.where(shift & (1 << bit) != 0, pltpu.roll(x, by, 1), x)
        return x

    kin_count = jnp.broadcast_to(ocnt[...].astype(F32), (group, tiles))
    kin_sub = lax.broadcasted_iota(jnp.int32, (group, tiles), 0) * ny + kin
    kin_lane = lax.broadcasted_iota(jnp.int32, (group, tiles), 1)
    kin_start = jnp.sum(
        jnp.where(kin_lane < kin_sub, kin_count, 0.0), axis=1, keepdims=True
    )
    kin_own = jnp.sum(
        jnp.where(kin_lane == kin_sub, kin_count, 0.0), axis=1, keepdims=True
    )
    lane, shift, usable = places(kin_start, kin_own)
    line_col = jnp.broadcast_to(kin_start, (group, tiles)).astype(jnp.int32) // LANES
    pick = jnp.concatenate(
        [
            jnp.where(kin_lane == line_col, 1.0, 0.0),
            jnp.where(kin_lane == line_col + 1, 1.0, 0.0),
        ],
        axis=0,
    ).astype(BF16)
    for b in range(tiles):
        okb[b] = oker[:, b * LANES : (b + 1) * LANES]
    for q in range(lev + 3):
        if q < lev:
            part = okb[:, q, :]
        else:
            part = (ocol, oval, owgt)[q - lev][...].astype(F32)
        two = sum(
            jnp.dot(pick, piece, preferred_element_type=F32) for piece in split3(part)
        )
        value = jnp.where(lane >= shift, two[0:group], two[group : 2 * group])
        value = turn(value, shift, True)
        if q == lev:
            value = jnp.where(usable, value, -1.0)
        obs_s[:, q, :] = value
    for q in range(lev + 3, 2 * lev):
        obs_s[:, q, :] = jnp.zeros((group, LANES), F32)

    def obs_copy(j, d):
        return remote(
            obs_s.at[j], obs_r.at[y, line_t], s_obs.at[j], r_obs.at[line_t], e, d
        )

    each_kin(lambda j, d: obs_copy(j, d).start())

    @pl.when(alone == 1)
    def _():
        obs_r[y, line_t] = obs_s[line_t]

    span(ahead, members, send_control)

    def obs_on(b):
        return remote(obs_r.at[y], obs_r.at[y], s_o2.at[b], r_o2.at[y], 2 * b + xl, t)

    def obs_mid():
        each_kin(
            lambda j, d: remote(
                obs_s.at[j], obs_r.at[y, j], s_obs.at[j], r_obs.at[j], e, d
            ).wait_recv()
        )
        each_y(lambda b: obs_on(b).start())

    def obs_wait():
        each_y(
            lambda b: remote(
                obs_r.at[b], obs_r.at[b], s_o2.at[b], r_o2.at[b], 2 * b + xl, t
            ).wait_recv()
        )

    def spread(m):
        for s in range(NT):
            block = per[s, m].astype(F32)
            for r in range(rows):
                pp[s, m, r] = block[:, r, :]

    load_per.wait()
    loop(members, spread)

    pre[0].wait_recv()
    pre[1].wait_recv()
    above = jnp.where(first, 0.0, dif_u[...])
    below = jnp.where(last, 0.0, dif_d[...])
    own = dif[...]
    total_rows = rows + 2 * NDIFF
    for i in range(total_rows):
        src = above if i < NDIFF else (own if i < NDIFF + rows else below)
        j = i if i < NDIFF else (i - NDIFF if i < NDIFF + rows else i - NDIFF - rows)
        line = jnp.broadcast_to(src[j : j + 1, :], (lev, width))
        dbc[i] = line
        dsq[i] = line * line
        if NDIFF <= i < NDIFF + rows:
            fin[i - NDIFF] = factor / line

    def tile_of(x, b):
        return x[:, b * LANES : (b + 1) * LANES]

    pre[2].wait_recv()
    pre[3].wait_recv()

    def winds(r):
        we = jnp.broadcast_to(east[r : r + 1, :], (lev, width))
        wn = jnp.broadcast_to(north[r : r + 1, :], (lev, width))
        return (
            jnp.maximum(we, 0.0),
            jnp.minimum(we, 0.0),
            jnp.maximum(wn, 0.0),
            jnp.minimum(wn, 0.0),
        )

    for r in range(rows):
        ep, em, np_, nm = winds(r)
        q = sta[r]
        above = sta[r - 1] if r else jnp.where(first, 0.0, sta_u[...])
        below = sta[r + 1] if r < rows - 1 else jnp.where(last, 0.0, sta_d[...])
        moved = q - ep * (q - left(q)) - em * (right(q) - q)
        moved = moved - np_ * (q - above) - nm * (below - q)
        for b in range(ens):
            stb[b, r] = tile_of(q, b)
            stb[b, rows + r] = tile_of(moved, b)

    def smooth(m, refs):
        for i in range(total_rows):
            ref, r = source_of(i, refs)
            wa[i] = dbc[i] * ref[m, r]
        src, dst = wa, wb
        for step in range(NDIFF):
            for i in range(step + 1, total_rows - 1 - step):
                w = src[i]
                lap = src[i + 1] + src[i - 1] + left(w) + right(w) - 4.0 * w
                dst[i] = w + dsq[i] * lap
            src, dst = dst, src
        return [src[NDIFF + r] for r in range(rows)]

    def source_of(i, refs):
        if i < NDIFF:
            return refs[0], i
        if i < NDIFF + rows:
            return refs[1], i - NDIFF
        return refs[2], i - NDIFF - rows

    def forward(m):
        for copy in halo(m, cc, cu, cd, s_c, r_c):
            copy.wait_recv()
        res = smooth(m, (cu, cc, cd))
        for r in range(rows):
            for s in range(NT):
                acc[s * rows + r] += pp[s, m, r] * res[r]

    def rs_copy(b):
        return remote(accb.at[b], rbuf.at[e], s_rs.at[b], r_rs.at[e], b, t)

    def rs_start():
        for h in range(hi_n):
            value = acc[h] * fin[h % rows]
            for b in range(ens):
                accb[b, h] = tile_of(value, b)
        each_e(lambda b: rs_copy(b).start())

    def rs_wait():
        each_e(
            lambda b: remote(
                accb.at[b], rbuf.at[b], s_rs.at[b], r_rs.at[b], b, t
            ).wait_recv()
        )
        rbuf[e] = accb[e]

    chunks = ny

    def lines_of(g, i, n=1):
        return jnp.concatenate(
            [obs_r[g, j, i : i + n, :] for j in range(group)], axis=1
        )

    lo_iota = lax.broadcasted_iota(jnp.int32, (LANES, group * LANES), 0)

    def hot(g):
        col = lines_of(g, lev).astype(jnp.int32)
        lo = col & (LANES - 1)
        block = (col // LANES) & (ens - 1)
        unit = jnp.where((col >= 0) & (block == e), col // width, -1)
        himask[g] = jnp.broadcast_to(unit, (lev, group * LANES))
        okern[g] = lines_of(g, 0, lev)
        oaux[g, 0:1, :] = lines_of(g, lev + 1)
        oaux[g, 1:2, :] = lines_of(g, lev + 2)
        onehot[g] = jnp.where(
            jnp.broadcast_to(lo, (LANES, group * LANES)) == lo_iota, 1.0, 0.0
        ).astype(BF16)

    def observe():
        points = hi_n * lev
        values = []
        for u in range(hi_n):
            value = stb[e, u]
            for b in range(ens):
                value = value + rbuf[b, u]
            values.append(value)
        table = jnp.concatenate(split2(jnp.concatenate(values, axis=0)), axis=0)
        table = table.astype(BF16)
        total = jnp.zeros((2 * points, LANES), F32)
        for g in range(chunks):
            hi = himask[g]
            kern = okern[g]
            flat = jnp.dot(table, onehot[g], preferred_element_type=F32)
            profile = jnp.zeros(kern.shape, F32)
            for j in range(hi_n):
                value = flat[j * lev : (j + 1) * lev]
                value = value + flat[points + j * lev : points + (j + 1) * lev]
                profile = jnp.where(hi == j, value, profile)
            evolved = jnp.sum(kern * profile, axis=0, keepdims=True)
            dep = oaux[g, 1:2, :] * (evolved - oaux[g, 0:1, :])
            dep = jnp.where(hi[0:1] >= 0, dep, 0.0)
            for j in range(group):
                depp[g, j] = tile_of(dep, j)
            push = kern * dep
            place = jnp.concatenate(
                [jnp.where(hi == j, push, 0.0) for j in range(hi_n)], axis=0
            )
            place = jnp.concatenate(split2(place), axis=0).astype(BF16)
            total = total + lax.dot_general(
                place, onehot[g], (((1,), (1,)), ((), ())), preferred_element_type=F32
            )
        total = total[0:points] + total[points : 2 * points]
        for j in range(hi_n):
            adjb[j] = total[j * lev : (j + 1) * lev]
            abuf[e, j] = total[j * lev : (j + 1) * lev]
        each_e(lambda b: ag_copy(b).start())

    def ag_copy(b):
        return remote(adjb, abuf.at[e], s_ag.at[b], r_ag.at[e], b, t)

    def ag_wait():
        each_e(
            lambda b: remote(
                adjb, abuf.at[b], s_ag.at[b], r_ag.at[b], b, t
            ).wait_recv()
        )
        for h in range(hi_n):
            adjf[h] = jnp.concatenate([abuf[b, h] for b in range(ens)], axis=1)

    dx_copy = remote(depp, dx, s_dx.at[0], r_dx.at[0], partner, t)

    def dg_copy(b):
        return remote(depx, dbuf.at[y], s_dg.at[b], r_dg.at[y], 2 * b + xl, t)

    def dg_mid():
        dx_copy.wait_recv()
        depx[...] = depp[...] + dx[...]
        each_y(lambda b: dg_copy(b).start())

    def force(m):
        for r in range(rows):
            ff[m, r] = pp[0, m, r] * adjf[r] + pp[1, m, r] * adjf[rows + r]
        for copy in halo(m, ff, fu, fd, s_f, r_f):
            copy.start()

    def store_of(m):
        return pltpu.make_async_copy(gens.at[m], gens_hbm.at[m], s_out.at[m])

    def backward(m):
        for copy in halo(m, ff, fu, fd, s_f, r_f):
            copy.wait_recv()
        res = smooth(m, (fu, ff, fd))
        for r in range(rows):
            gens[m, :, r, :] = cc[m, r] + res[r] * fin[r]
        store_of(m).start()

    for h in range(hi_n):
        acc[h] = jnp.zeros((lev, width), F32)
    span(0, members // 2, forward)
    obs_mid()
    span(members // 2, members, forward)
    rs_start()
    obs_wait()
    for g in range(chunks):
        hot(g)
    rs_wait()
    observe()
    dx_copy.start()
    ag_wait()
    wnd_u[...] = winds(0)[2] * adjf[rows]
    wnd_d[...] = winds(rows - 1)[3] * adjf[2 * rows - 1]
    wind = [
        remote(wnd_d, rcv_wu, s_w.at[0], r_w.at[0], e, down),
        remote(wnd_u, rcv_wd, s_w.at[1], r_w.at[1], e, up),
    ]
    q1, q2 = members // 4, members * 5 // 8
    span(0, 1, force)
    for copy in wind:
        copy.start()
    dg_mid()
    span(1, q1, force)

    each_y(
        lambda b: remote(
            depx, dbuf.at[b], s_dg.at[b], r_dg.at[b], 2 * b + xl, t
        ).wait_recv()
    )
    dbuf[y] = depx[...]
    value = dbuf[0]
    for b in range(1, ny):
        value = value + dbuf[b]
    deps[...] = value

    def dep_copy(j, s):
        return remote(
            deps.at[y, j], depr.at[y, line_t], s_dep.at[j], r_dep.at[line_t], e, s
        )

    each_kin(lambda j, s: dep_copy(j, s).start())

    @pl.when(alone == 1)
    def _():
        depr[y, line_t] = deps[y, line_t]

    span(q1, q2, force)
    each_kin(
        lambda j, s: remote(
            deps.at[y, j], depr.at[y, j], s_dep.at[j], r_dep.at[j], e, s
        ).wait_recv()
    )

    def dep_on(b):
        return remote(depr.at[y], depr.at[y], s_d2.at[b], r_d2.at[y], 2 * b + xl, t)

    each_y(lambda b: dep_on(b).start())
    span(q2, members, force)

    for copy in wind:
        copy.wait_recv()
    for r in range(rows):
        ep, em, np_, nm = winds(r)
        a = adjf[rows + r]
        if r < rows - 1:
            lower = winds(r + 1)[2] * adjf[rows + r + 1]
        else:
            lower = jnp.where(last, 0.0, rcv_wd[...])
        if r:
            upper = winds(r - 1)[3] * adjf[rows + r - 1]
        else:
            upper = jnp.where(first, 0.0, rcv_wu[...])
        moved = a * (1.0 - ep + em - np_ + nm) + right(ep * a) - left(em * a)
        moved = moved + lower - upper
        gsta[:, r, :] = stc[:, r, :] + scale * (adjf[r] + moved)

    span(0, q2, backward)

    each_y(
        lambda b: remote(
            depr.at[b], depr.at[b], s_d2.at[b], r_d2.at[b], 2 * b + xl, t
        ).wait_recv()
    )
    for d in range(tiles):
        depf[d : d + 1, :] = depr[lax.rem(t + d, ny), d // ny]
    lane, shift, usable = places(start_col, count_col)
    line_row = jnp.broadcast_to(start_row, (tiles, tiles)).astype(jnp.int32) // LANES
    spread0 = jnp.where(d_sub == line_row, 1.0, 0.0).astype(BF16)
    spread1 = jnp.where(d_sub == line_row + 1, 1.0, 0.0).astype(BF16)
    value = turn(jnp.where(usable, depf[...], 0.0), shift, False)
    out = jnp.zeros((tiles, LANES), F32)
    for piece in split3(jnp.where(lane >= shift, value, 0.0)):
        out = out + jnp.dot(spread0, piece, preferred_element_type=F32)
    for piece in split3(jnp.where(lane < shift, value, 0.0)):
        out = out + jnp.dot(spread1, piece, preferred_element_type=F32)
    gdep[...] = out
    span(q2, members, backward)

    loop(members, lambda m: store_of(m).wait())
    for copy in pre + wind:
        copy.wait_send()

    def sent(m):
        for copy in halo(m, cc, cu, cd, s_c, r_c) + halo(m, ff, fu, fd, s_f, r_f):
            copy.wait_send()

    loop(members, sent)

    each_kin(lambda j, d: obs_copy(j, d).wait_send())
    each_kin(lambda j, d: dep_copy(j, d).wait_send())
    dx_copy.wait_send()
    def sent_y(b):
        obs_on(b).wait_send()
        dep_on(b).wait_send()
        dg_copy(b).wait_send()

    each_y(sent_y)
    each_e(lambda b: rs_copy(b).wait_send())
    each_e(lambda b: ag_copy(b).wait_send())


def hand_over(x0, x1, x2, y0, y1, y2, b0, b1, b2, s_in, s_out):
    members = x0.shape[0]
    triples = [(x0.at[m], b0.at[m], y0.at[m]) for m in range(members)]
    triples += [(x1, b1, y1), (x2, b2, y2)]
    come = [
        pltpu.make_async_copy(x, b, s_in.at[i]) for i, (x, b, y) in enumerate(triples)
    ]
    go = [
        pltpu.make_async_copy(b, y, s_out.at[i]) for i, (x, b, y) in enumerate(triples)
    ]
    for copy in come:
        copy.start()
    for a, b in zip(come, go):
        a.wait()
        b.start()
    for copy in go:
        copy.wait()


def per_device(
    ens_control,
    static_control,
    perturbations,
    level_sigma,
    length_class,
    courant_east,
    courant_north,
    obs_column,
    obs_count,
    obs_value,
    obs_weight,
    obs_kernel,
):
    members, lev, rows, width = ens_control.shape
    ens = lax.axis_size("ens")
    tiles = lax.axis_size("tile")
    factor = BETA_ENS / math.sqrt(ens * members - 1)
    hi_n = NT * rows
    vmem = lambda *shape, dtype=F32: pltpu.VMEM(shape, dtype)
    dma = lambda *shape: pltpu.SemaphoreType.DMA(shape)
    line = (lev, width)
    ny = ens // 2
    group = tiles // ny
    chunks = ny
    slots = group * LANES
    total_rows = rows + 2 * NDIFF
    fields = (members, rows) + line
    scratch = [
        vmem(*ens_control.shape),
        vmem(*perturbations.shape, dtype=BF16),
        vmem(*ens_control.shape),
        dma(2),
        dma(members),
        vmem(tiles, lev, LANES),
        vmem(rows, width),
        vmem(rows, width),
        vmem(rows, width),
        vmem(total_rows, lev, width),
        vmem(total_rows, lev, width),
        vmem(rows, lev, width),
        vmem(rows, *line),
        vmem(*line),
        vmem(*line),
        vmem(ens, hi_n, lev, LANES),
        vmem(*line),
        vmem(*line),
        vmem(*line),
        vmem(*line),
        vmem(*fields),
        vmem(*fields),
        vmem(*fields),
        vmem(NT, *fields),
        vmem(*fields),
        vmem(*fields),
        vmem(*fields),
        vmem(total_rows, lev, width),
        vmem(total_rows, lev, width),
        vmem(hi_n, lev, width),
        vmem(ens, hi_n, lev, LANES),
        vmem(ens, hi_n, lev, LANES),
        vmem(group, 2 * lev, LANES),
        vmem(ny, group, 2 * lev, LANES),
        vmem(chunks, LANES, slots, dtype=BF16),
        vmem(chunks, lev, slots, dtype=jnp.int32),
        vmem(chunks, lev, slots),
        vmem(chunks, lev, slots),
        vmem(hi_n, lev, LANES),
        vmem(ens, hi_n, lev, LANES),
        vmem(hi_n, *line),
        vmem(ny, group, 1, LANES),
        vmem(ny, group, 1, LANES),
        vmem(ny, group, 1, LANES),
        vmem(ny, ny, group, 1, LANES),
        vmem(ny, group, 1, LANES),
        vmem(ny, group, 1, LANES),
        vmem(tiles, LANES),
        dma(4), dma(4),
        dma(2, members), dma(2, members),
        dma(2, members), dma(2, members),
        dma(group), dma(group),
        dma(ens), dma(ens),
        dma(ens), dma(ens),
        dma(ny), dma(ny),
        dma(2), dma(2),
        dma(group), dma(group),
        dma(ny), dma(ny),
        dma(1), dma(1),
        dma(ny), dma(ny),
    ]
    v = pl.BlockSpec(memory_space=pltpu.VMEM)
    s = pl.BlockSpec(memory_space=pltpu.SMEM)
    a = pl.BlockSpec(memory_space=pl.ANY)
    shape = jax.ShapeDtypeStruct
    grad_ens, grad_static, departures = pl.pallas_call(
        functools.partial(kernel, factor, ens, tiles),
        out_shape=(
            shape(ens_control.shape, F32),
            shape(static_control.shape, F32),
            shape((tiles, LANES), F32),
        ),
        in_specs=[a, v, a, s, v, v, v, v, v, v, v, v],
        out_specs=(a, v, v),
        scratch_shapes=scratch,
        name="gradient",
        compiler_params=pltpu.CompilerParams(
            collective_id=0, has_side_effects=True, vmem_limit_bytes=56 * 2**20
        ),
    )(
        ens_control,
        static_control,
        perturbations,
        level_sigma,
        length_class,
        courant_east,
        courant_north,
        obs_column.reshape(tiles, LANES),
        obs_count.reshape(1, tiles),
        obs_value.reshape(tiles, LANES),
        obs_weight.reshape(tiles, LANES),
        obs_kernel,
    )
    grad_ens, grad_static, departures = pl.pallas_call(
        hand_over,
        out_shape=tuple(shape(x.shape, F32) for x in (grad_ens, grad_static, departures)),
        in_specs=[a, a, a],
        out_specs=(a, a, a),
        scratch_shapes=[
            vmem(*x.shape) for x in (grad_ens, grad_static, departures)
        ]
        + [dma(members + 2), dma(members + 2)],
        name="results",
    )(grad_ens, grad_static, departures)
    return (grad_ens, grad_static, departures.reshape(-1))


def solution(mesh):
    return jax.shard_map(
        per_device,
        mesh=mesh,
        in_specs=(
            P("ens", None, "tile", None),
            P(None, "tile", None),
            P(None, "ens", None, "tile", None),
            P(),
            P("tile", None),
            P("tile", None),
            P("tile", None),
            P("tile"),
            P("tile"),
            P("tile"),
            P("tile"),
            P(None, "tile"),
        ),
        out_specs=(P("ens", None, "tile", None), P(None, "tile", None), P("tile")),
        check_vma=False,
    )
```

```python
import functools
import math

import jax
import jax.numpy as jnp
from jax import lax
from jax.experimental import pallas as pl
from jax.experimental.pallas import tpu as pltpu
from jax.sharding import PartitionSpec as P

NT = 2
NDIFF = 4
BETA_ENS = 0.8
BETA_STATIC = 0.6
DIFF_BASE = 0.06
LANES = 128
MESH = pl.DeviceIdType.MESH
F32 = jnp.float32
BF16 = jnp.bfloat16


def split3(x):
    a = x.astype(BF16)
    rest = x - a.astype(F32)
    b = rest.astype(BF16)
    c = (rest - b.astype(F32)).astype(BF16)
    return a, b, c


def split2(x):
    a = x.astype(BF16).astype(F32)
    return a, x - a


def left(x):
    return pltpu.roll(x, 1, 1)


def right(x):
    return pltpu.roll(x, x.shape[1] - 1, 1)


def kernel(
    factor,
    ens,
    tiles,
    ctl_hbm,
    stc,
    per_hbm,
    sigma,
    cls,
    east,
    north,
    ocol,
    ocnt,
    oval,
    owgt,
    oker,
    gens_hbm,
    gsta,
    gdep,
    ctl,
    per,
    gens,
    s_in,
    s_out,
    okb,
    dif,
    dif_u,
    dif_d,
    dbc,
    dsq,
    fin,
    sta,
    sta_u,
    sta_d,
    stb,
    wnd_u,
    wnd_d,
    rcv_wu,
    rcv_wd,
    cc,
    cu,
    cd,
    pp,
    ff,
    fu,
    fd,
    wa,
    wb,
    acc,
    accb,
    rbuf,
    obs_s,
    obs_r,
    onehot,
    himask,
    okern,
    oaux,
    adjb,
    abuf,
    adjf,
    depp,
    depx,
    dx,
    dbuf,
    deps,
    depr,
    depf,
    s_pre,
    r_pre,
    s_c,
    r_c,
    s_f,
    r_f,
    s_obs,
    r_obs,
    s_rs,
    r_rs,
    s_ag,
    r_ag,
    s_dg,
    r_dg,
    s_w,
    r_w,
    s_dep,
    r_dep,
    s_o2,
    r_o2,
    s_dx,
    r_dx,
    s_d2,
    r_d2,
):
    members, lev, rows, width = ctl.shape
    load_ctl = pltpu.make_async_copy(ctl_hbm, ctl, s_in.at[0])
    load_per = pltpu.make_async_copy(per_hbm, per, s_in.at[1])
    load_ctl.start()
    load_per.start()
    hi_n = NT * rows
    e = lax.axis_index("ens")
    t = lax.axis_index("tile")
    ny = ens // 2
    y = e // 2
    xl = lax.rem(e, 2)
    partner = 2 * y + 1 - xl
    group = tiles // ny
    kin = lax.rem(y - lax.rem(t, ny) + ny, ny)
    line_t = t // ny
    up = lax.rem(t + tiles - 1, tiles)
    down = lax.rem(t + 1, tiles)
    first = t == 0
    last = t == tiles - 1

    def remote(src, dst, ssem, rsem, e_to, t_to):
        return pltpu.make_async_remote_copy(
            src_ref=src,
            dst_ref=dst,
            send_sem=ssem,
            recv_sem=rsem,
            device_id=(e_to, t_to),
            device_id_type=MESH,
        )

    def loop(n, body):
        def step(i, carry):
            body(i)
            return carry

        lax.fori_loop(0, n, step, 0)

    def span(low, high, body):
        def step(i, carry):
            body(i)
            return carry

        lax.fori_loop(low, high, step, 0)

    def each_e(body):
        span(1, ens, lambda k: body(lax.rem(e + k, ens)))

    def peer_y(k):
        return lax.rem(y + k, ny)

    def each_y(body):
        span(1, ny, lambda k: body(peer_y(k)))

    def each_kin(body):
        def one(j):
            pl.when(j * ny + kin != t)(lambda: body(j, j * ny + kin))

        loop(group, one)

    barrier = pltpu.get_barrier_semaphore()

    def greet(e_to, t_to):
        pl.semaphore_signal(barrier, inc=1, device_id=(e_to, t_to), device_id_type=MESH)

    greet(e, up)
    greet(e, down)
    each_kin(lambda j, d: greet(e, d))
    each_e(lambda b: greet(b, t))
    alone = jnp.where(kin == lax.rem(t, ny), 1, 0)
    dif[...] = jnp.sqrt(DIFF_BASE * (cls[...].astype(F32) + 1.0))
    sub = lax.broadcasted_iota(jnp.int32, (lev, width), 0)
    scale = jnp.zeros((lev, width), F32)
    for l in range(lev):
        scale = jnp.where(sub == l, BETA_STATIC * sigma[l], scale)
    for r in range(rows):
        sta[r] = scale * stc[:, r, :]
    load_ctl.wait()
    pl.semaphore_wait(barrier, 2 + group - alone + ens - 1)

    pre = [
        remote(dif, dif_u, s_pre.at[0], r_pre.at[0], e, down),
        remote(dif, dif_d, s_pre.at[1], r_pre.at[1], e, up),
        remote(sta.at[rows - 1], sta_u, s_pre.at[2], r_pre.at[2], e, down),
        remote(sta.at[0], sta_d, s_pre.at[3], r_pre.at[3], e, up),
    ]
    for copy in pre:
        copy.start()

    def halo(m, own, from_up, from_down, ssem, rsem):
        src = own.at[m]
        return (
            remote(src, from_up.at[m], ssem.at[0, m], rsem.at[0, m], e, down),
            remote(src, from_down.at[m], ssem.at[1, m], rsem.at[1, m], e, up),
        )

    def send_control(m):
        for r in range(rows):
            cc[m, r] = ctl[m, :, r, :]
        for copy in halo(m, cc, cu, cd, s_c, r_c):
            copy.start()

    ahead = members // 4
    span(0, ahead, send_control)

    count = jnp.broadcast_to(ocnt[...].astype(F32), (tiles, tiles))
    d_sub = lax.broadcasted_iota(jnp.int32, (tiles, tiles), 0)
    d_lane = lax.broadcasted_iota(jnp.int32, (tiles, tiles), 1)
    count_col = jnp.sum(
        jnp.where(d_lane == d_sub, count, 0.0), axis=1, keepdims=True
    )
    start_col = jnp.sum(jnp.where(d_lane < d_sub, count, 0.0), axis=1, keepdims=True)
    start_row = jnp.sum(
        jnp.where(d_sub < d_lane, jnp.broadcast_to(count_col, (tiles, tiles)), 0.0),
        axis=0,
        keepdims=True,
    )
    def places(start_of, count_of):
        shape = (start_of.shape[0], LANES)
        begin = jnp.broadcast_to(start_of, shape).astype(jnp.int32)
        lane = lax.broadcasted_iota(jnp.int32, shape, 1)
        usable = lane < jnp.broadcast_to(count_of, shape).astype(jnp.int32)
        return lane, begin & (LANES - 1), usable

    def turn(x, shift, back):
        for bit in range(LANES.bit_length() - 1):
            by = LANES - (1 << bit) if back else 1 << bit
            x = jnp.where(shift & (1 << bit) != 0, pltpu.roll(x, by, 1), x)
        return x

    kin_count = jnp.broadcast_to(ocnt[...].astype(F32), (group, tiles))
    kin_sub = lax.broadcasted_iota(jnp.int32, (group, tiles), 0) * ny + kin
    kin_lane = lax.broadcasted_iota(jnp.int32, (group, tiles), 1)
    kin_start = jnp.sum(
        jnp.where(kin_lane < kin_sub, kin_count, 0.0), axis=1, keepdims=True
    )
    kin_own = jnp.sum(
        jnp.where(kin_lane == kin_sub, kin_count, 0.0), axis=1, keepdims=True
    )
    lane, shift, usable = places(kin_start, kin_own)
    line_col = jnp.broadcast_to(kin_start, (group, tiles)).astype(jnp.int32) // LANES
    pick = jnp.concatenate(
        [
            jnp.where(kin_lane == line_col, 1.0, 0.0),
            jnp.where(kin_lane == line_col + 1, 1.0, 0.0),
        ],
        axis=0,
    ).astype(BF16)
    for b in range(tiles):
        okb[b] = oker[:, b * LANES : (b + 1) * LANES]
    for q in range(lev + 3):
        if q < lev:
            part = okb[:, q, :]
        else:
            part = (ocol, oval, owgt)[q - lev][...].astype(F32)
        two = sum(
            jnp.dot(pick, piece, preferred_element_type=F32) for piece in split3(part)
        )
        value = jnp.where(lane >= shift, two[0:group], two[group : 2 * group])
        value = turn(value, shift, True)
        if q == lev:
            value = jnp.where(usable, value, -1.0)
        obs_s[:, q, :] = value
    for q in range(lev + 3, 2 * lev):
        obs_s[:, q, :] = jnp.zeros((group, LANES), F32)

    def obs_copy(j, d):
        return remote(
            obs_s.at[j], obs_r.at[y, line_t], s_obs.at[j], r_obs.at[line_t], e, d
        )

    each_kin(lambda j, d: obs_copy(j, d).start())

    @pl.when(alone == 1)
    def _():
        obs_r[y, line_t] = obs_s[line_t]

    span(ahead, members, send_control)

    def obs_on(b):
        return remote(obs_r.at[y], obs_r.at[y], s_o2.at[b], r_o2.at[y], 2 * b + xl, t)

    def obs_mid():
        each_kin(
            lambda j, d: remote(
                obs_s.at[j], obs_r.at[y, j], s_obs.at[j], r_obs.at[j], e, d
            ).wait_recv()
        )
        each_y(lambda b: obs_on(b).start())

    def obs_wait():
        each_y(
            lambda b: remote(
                obs_r.at[b], obs_r.at[b], s_o2.at[b], r_o2.at[b], 2 * b + xl, t
            ).wait_recv()
        )

    def spread(m):
        for s in range(NT):
            block = per[s, m].astype(F32)
            for r in range(rows):
                pp[s, m, r] = block[:, r, :]

    load_per.wait()
    loop(members, spread)

    pre[0].wait_recv()
    pre[1].wait_recv()
    above = jnp.where(first, 0.0, dif_u[...])
    below = jnp.where(last, 0.0, dif_d[...])
    own = dif[...]
    total_rows = rows + 2 * NDIFF
    for i in range(total_rows):
        src = above if i < NDIFF else (own if i < NDIFF + rows else below)
        j = i if i < NDIFF else (i - NDIFF if i < NDIFF + rows else i - NDIFF - rows)
        line = jnp.broadcast_to(src[j : j + 1, :], (lev, width))
        dbc[i] = line
        dsq[i] = line * line
        if NDIFF <= i < NDIFF + rows:
            fin[i - NDIFF] = factor / line

    def tile_of(x, b):
        return x[:, b * LANES : (b + 1) * LANES]

    pre[2].wait_recv()
    pre[3].wait_recv()

    def winds(r):
        we = jnp.broadcast_to(east[r : r + 1, :], (lev, width))
        wn = jnp.broadcast_to(north[r : r + 1, :], (lev, width))
        return (
            jnp.maximum(we, 0.0),
            jnp.minimum(we, 0.0),
            jnp.maximum(wn, 0.0),
            jnp.minimum(wn, 0.0),
        )

    for r in range(rows):
        ep, em, np_, nm = winds(r)
        q = sta[r]
        above = sta[r - 1] if r else jnp.where(first, 0.0, sta_u[...])
        below = sta[r + 1] if r < rows - 1 else jnp.where(last, 0.0, sta_d[...])
        moved = q - ep * (q - left(q)) - em * (right(q) - q)
        moved = moved - np_ * (q - above) - nm * (below - q)
        for b in range(ens):
            stb[b, r] = tile_of(q, b)
            stb[b, rows + r] = tile_of(moved, b)

    def smooth(m, refs):
        for i in range(total_rows):
            ref, r = source_of(i, refs)
            wa[i] = dbc[i] * ref[m, r]
        src, dst = wa, wb
        for step in range(NDIFF):
            for i in range(step + 1, total_rows - 1 - step):
                w = src[i]
                lap = src[i + 1] + src[i - 1] + left(w) + right(w) - 4.0 * w
                dst[i] = w + dsq[i] * lap
            src, dst = dst, src
        return [src[NDIFF + r] for r in range(rows)]

    def source_of(i, refs):
        if i < NDIFF:
            return refs[0], i
        if i < NDIFF + rows:
            return refs[1], i - NDIFF
        return refs[2], i - NDIFF - rows

    def forward(m):
        for copy in halo(m, cc, cu, cd, s_c, r_c):
            copy.wait_recv()
        res = smooth(m, (cu, cc, cd))
        for r in range(rows):
            for s in range(NT):
                acc[s * rows + r] += pp[s, m, r] * res[r]

    def rs_copy(b):
        return remote(accb.at[b], rbuf.at[e], s_rs.at[b], r_rs.at[e], b, t)

    def rs_start():
        for h in range(hi_n):
            value = acc[h] * fin[h % rows]
            for b in range(ens):
                accb[b, h] = tile_of(value, b)
        each_e(lambda b: rs_copy(b).start())

    def rs_wait():
        each_e(
            lambda b: remote(
                accb.at[b], rbuf.at[b], s_rs.at[b], r_rs.at[b], b, t
            ).wait_recv()
        )
        rbuf[e] = accb[e]

    chunks = ny

    def lines_of(g, i, n=1):
        return jnp.concatenate(
            [obs_r[g, j, i : i + n, :] for j in range(group)], axis=1
        )

    lo_iota = lax.broadcasted_iota(jnp.int32, (LANES, group * LANES), 0)

    def hot(g):
        col = lines_of(g, lev).astype(jnp.int32)
        lo = col & (LANES - 1)
        block = (col // LANES) & (ens - 1)
        unit = jnp.where((col >= 0) & (block == e), col // width, -1)
        himask[g] = jnp.broadcast_to(unit, (lev, group * LANES))
        okern[g] = lines_of(g, 0, lev)
        oaux[g, 0:1, :] = lines_of(g, lev + 1)
        oaux[g, 1:2, :] = lines_of(g, lev + 2)
        onehot[g] = jnp.where(
            jnp.broadcast_to(lo, (LANES, group * LANES)) == lo_iota, 1.0, 0.0
        ).astype(BF16)

    def observe():
        points = hi_n * lev
        values = []
        for u in range(hi_n):
            value = stb[e, u]
            for b in range(ens):
                value = value + rbuf[b, u]
            values.append(value)
        table = jnp.concatenate(split2(jnp.concatenate(values, axis=0)), axis=0)
        table = table.astype(BF16)
        total = jnp.zeros((2 * points, LANES), F32)
        for g in range(chunks):
            hi = himask[g]
            kern = okern[g]
            flat = jnp.dot(table, onehot[g], preferred_element_type=F32)
            profile = jnp.zeros(kern.shape, F32)
            for j in range(hi_n):
                value = flat[j * lev : (j + 1) * lev]
                value = value + flat[points + j * lev : points + (j + 1) * lev]
                profile = jnp.where(hi == j, value, profile)
            evolved = jnp.sum(kern * profile, axis=0, keepdims=True)
            dep = oaux[g, 1:2, :] * (evolved - oaux[g, 0:1, :])
            dep = jnp.where(hi[0:1] >= 0, dep, 0.0)
            for j in range(group):
                depp[g, j] = tile_of(dep, j)
            push = kern * dep
            place = jnp.concatenate(
                [jnp.where(hi == j, push, 0.0) for j in range(hi_n)], axis=0
            )
            place = jnp.concatenate(split2(place), axis=0).astype(BF16)
            total = total + lax.dot_general(
                place, onehot[g], (((1,), (1,)), ((), ())), preferred_element_type=F32
            )
        total = total[0:points] + total[points : 2 * points]
        for j in range(hi_n):
            adjb[j] = total[j * lev : (j + 1) * lev]
            abuf[e, j] = total[j * lev : (j + 1) * lev]
        each_e(lambda b: ag_copy(b).start())

    def ag_copy(b):
        return remote(adjb, abuf.at[e], s_ag.at[b], r_ag.at[e], b, t)

    def ag_wait():
        each_e(
            lambda b: remote(
                adjb, abuf.at[b], s_ag.at[b], r_ag.at[b], b, t
            ).wait_recv()
        )
        for h in range(hi_n):
            adjf[h] = jnp.concatenate([abuf[b, h] for b in range(ens)], axis=1)

    dx_copy = remote(depp, dx, s_dx.at[0], r_dx.at[0], partner, t)

    def dg_copy(b):
        return remote(depx, dbuf.at[y], s_dg.at[b], r_dg.at[y], 2 * b + xl, t)

    def dg_mid():
        dx_copy.wait_recv()
        depx[...] = depp[...] + dx[...]
        each_y(lambda b: dg_copy(b).start())

    def force(m):
        for r in range(rows):
            ff[m, r] = pp[0, m, r] * adjf[r] + pp[1, m, r] * adjf[rows + r]
        for copy in halo(m, ff, fu, fd, s_f, r_f):
            copy.start()

    def store_of(m):
        return pltpu.make_async_copy(gens.at[m], gens_hbm.at[m], s_out.at[m])

    def backward(m):
        for copy in halo(m, ff, fu, fd, s_f, r_f):
            copy.wait_recv()
        res = smooth(m, (fu, ff, fd))
        for r in range(rows):
            gens[m, :, r, :] = cc[m, r] + res[r] * fin[r]
        store_of(m).start()

    for h in range(hi_n):
        acc[h] = jnp.zeros((lev, width), F32)
    span(0, members // 2, forward)
    obs_mid()
    span(members // 2, members, forward)
    rs_start()
    obs_wait()
    for g in range(chunks):
        hot(g)
    rs_wait()
    observe()
    dx_copy.start()
    ag_wait()
    wnd_u[...] = winds(0)[2] * adjf[rows]
    wnd_d[...] = winds(rows - 1)[3] * adjf[2 * rows - 1]
    wind = [
        remote(wnd_d, rcv_wu, s_w.at[0], r_w.at[0], e, down),
        remote(wnd_u, rcv_wd, s_w.at[1], r_w.at[1], e, up),
    ]
    q1, q2 = members * 3 // 8, members * 3 // 4
    dg_mid()
    span(0, q1, force)
    for copy in wind:
        copy.start()

    each_y(
        lambda b: remote(
            depx, dbuf.at[b], s_dg.at[b], r_dg.at[b], 2 * b + xl, t
        ).wait_recv()
    )
    dbuf[y] = depx[...]
    value = dbuf[0]
    for b in range(1, ny):
        value = value + dbuf[b]
    deps[...] = value

    def dep_copy(j, s):
        return remote(
            deps.at[y, j], depr.at[y, line_t], s_dep.at[j], r_dep.at[line_t], e, s
        )

    each_kin(lambda j, s: dep_copy(j, s).start())

    @pl.when(alone == 1)
    def _():
        depr[y, line_t] = deps[y, line_t]

    span(q1, q2, force)

    for copy in wind:
        copy.wait_recv()
    for r in range(rows):
        ep, em, np_, nm = winds(r)
        a = adjf[rows + r]
        if r < rows - 1:
            lower = winds(r + 1)[2] * adjf[rows + r + 1]
        else:
            lower = jnp.where(last, 0.0, rcv_wd[...])
        if r:
            upper = winds(r - 1)[3] * adjf[rows + r - 1]
        else:
            upper = jnp.where(first, 0.0, rcv_wu[...])
        moved = a * (1.0 - ep + em - np_ + nm) + right(ep * a) - left(em * a)
        moved = moved + lower - upper
        gsta[:, r, :] = stc[:, r, :] + scale * (adjf[r] + moved)

    span(0, q1, backward)
    each_kin(
        lambda j, s: remote(
            deps.at[y, j], depr.at[y, j], s_dep.at[j], r_dep.at[j], e, s
        ).wait_recv()
    )

    def dep_on(b):
        return remote(depr.at[y], depr.at[y], s_d2.at[b], r_d2.at[y], 2 * b + xl, t)

    each_y(lambda b: dep_on(b).start())
    span(q2, members, force)
    span(q1, members - 1, backward)

    each_y(
        lambda b: remote(
            depr.at[b], depr.at[b], s_d2.at[b], r_d2.at[b], 2 * b + xl, t
        ).wait_recv()
    )
    for d in range(tiles):
        depf[d : d + 1, :] = depr[lax.rem(t + d, ny), d // ny]
    lane, shift, usable = places(start_col, count_col)
    line_row = jnp.broadcast_to(start_row, (tiles, tiles)).astype(jnp.int32) // LANES
    spread0 = jnp.where(d_sub == line_row, 1.0, 0.0).astype(BF16)
    spread1 = jnp.where(d_sub == line_row + 1, 1.0, 0.0).astype(BF16)
    value = turn(jnp.where(usable, depf[...], 0.0), shift, False)
    out = jnp.zeros((tiles, LANES), F32)
    for piece in split3(jnp.where(lane >= shift, value, 0.0)):
        out = out + jnp.dot(spread0, piece, preferred_element_type=F32)
    for piece in split3(jnp.where(lane < shift, value, 0.0)):
        out = out + jnp.dot(spread1, piece, preferred_element_type=F32)
    gdep[...] = out
    span(members - 1, members, backward)

    loop(members, lambda m: store_of(m).wait())
    for copy in pre + wind:
        copy.wait_send()

    def sent(m):
        for copy in halo(m, cc, cu, cd, s_c, r_c) + halo(m, ff, fu, fd, s_f, r_f):
            copy.wait_send()

    loop(members, sent)

    each_kin(lambda j, d: obs_copy(j, d).wait_send())
    each_kin(lambda j, d: dep_copy(j, d).wait_send())
    dx_copy.wait_send()
    def sent_y(b):
        obs_on(b).wait_send()
        dep_on(b).wait_send()
        dg_copy(b).wait_send()

    each_y(sent_y)
    each_e(lambda b: rs_copy(b).wait_send())
    each_e(lambda b: ag_copy(b).wait_send())


def hand_over(x0, x1, x2, y0, y1, y2, b0, b1, b2, s_in, s_out):
    members = x0.shape[0]
    triples = [(x0.at[m], b0.at[m], y0.at[m]) for m in range(members)]
    triples += [(x1, b1, y1), (x2, b2, y2)]
    come = [
        pltpu.make_async_copy(x, b, s_in.at[i]) for i, (x, b, y) in enumerate(triples)
    ]
    go = [
        pltpu.make_async_copy(b, y, s_out.at[i]) for i, (x, b, y) in enumerate(triples)
    ]
    for copy in come:
        copy.start()
    for a, b in zip(come, go):
        a.wait()
        b.start()
    for copy in go:
        copy.wait()


def per_device(
    ens_control,
    static_control,
    perturbations,
    level_sigma,
    length_class,
    courant_east,
    courant_north,
    obs_column,
    obs_count,
    obs_value,
    obs_weight,
    obs_kernel,
):
    members, lev, rows, width = ens_control.shape
    ens = lax.axis_size("ens")
    tiles = lax.axis_size("tile")
    factor = BETA_ENS / math.sqrt(ens * members - 1)
    hi_n = NT * rows
    vmem = lambda *shape, dtype=F32: pltpu.VMEM(shape, dtype)
    dma = lambda *shape: pltpu.SemaphoreType.DMA(shape)
    line = (lev, width)
    ny = ens // 2
    group = tiles // ny
    chunks = ny
    slots = group * LANES
    total_rows = rows + 2 * NDIFF
    fields = (members, rows) + line
    scratch = [
        vmem(*ens_control.shape),
        vmem(*perturbations.shape, dtype=BF16),
        vmem(*ens_control.shape),
        dma(2),
        dma(members),
        vmem(tiles, lev, LANES),
        vmem(rows, width),
        vmem(rows, width),
        vmem(rows, width),
        vmem(total_rows, lev, width),
        vmem(total_rows, lev, width),
        vmem(rows, lev, width),
        vmem(rows, *line),
        vmem(*line),
        vmem(*line),
        vmem(ens, hi_n, lev, LANES),
        vmem(*line),
        vmem(*line),
        vmem(*line),
        vmem(*line),
        vmem(*fields),
        vmem(*fields),
        vmem(*fields),
        vmem(NT, *fields),
        vmem(*fields),
        vmem(*fields),
        vmem(*fields),
        vmem(total_rows, lev, width),
        vmem(total_rows, lev, width),
        vmem(hi_n, lev, width),
        vmem(ens, hi_n, lev, LANES),
        vmem(ens, hi_n, lev, LANES),
        vmem(group, 2 * lev, LANES),
        vmem(ny, group, 2 * lev, LANES),
        vmem(chunks, LANES, slots, dtype=BF16),
        vmem(chunks, lev, slots, dtype=jnp.int32),
        vmem(chunks, lev, slots),
        vmem(chunks, lev, slots),
        vmem(hi_n, lev, LANES),
        vmem(ens, hi_n, lev, LANES),
        vmem(hi_n, *line),
        vmem(ny, group, 1, LANES),
        vmem(ny, group, 1, LANES),
        vmem(ny, group, 1, LANES),
        vmem(ny, ny, group, 1, LANES),
        vmem(ny, group, 1, LANES),
        vmem(ny, group, 1, LANES),
        vmem(tiles, LANES),
        dma(4), dma(4),
        dma(2, members), dma(2, members),
        dma(2, members), dma(2, members),
        dma(group), dma(group),
        dma(ens), dma(ens),
        dma(ens), dma(ens),
        dma(ny), dma(ny),
        dma(2), dma(2),
        dma(group), dma(group),
        dma(ny), dma(ny),
        dma(1), dma(1),
        dma(ny), dma(ny),
    ]
    v = pl.BlockSpec(memory_space=pltpu.VMEM)
    s = pl.BlockSpec(memory_space=pltpu.SMEM)
    a = pl.BlockSpec(memory_space=pl.ANY)
    shape = jax.ShapeDtypeStruct
    grad_ens, grad_static, departures = pl.pallas_call(
        functools.partial(kernel, factor, ens, tiles),
        out_shape=(
            shape(ens_control.shape, F32),
            shape(static_control.shape, F32),
            shape((tiles, LANES), F32),
        ),
        in_specs=[a, v, a, s, v, v, v, v, v, v, v, v],
        out_specs=(a, v, v),
        scratch_shapes=scratch,
        name="gradient",
        compiler_params=pltpu.CompilerParams(
            collective_id=0, has_side_effects=True, vmem_limit_bytes=56 * 2**20
        ),
    )(
        ens_control,
        static_control,
        perturbations,
        level_sigma,
        length_class,
        courant_east,
        courant_north,
        obs_column.reshape(tiles, LANES),
        obs_count.reshape(1, tiles),
        obs_value.reshape(tiles, LANES),
        obs_weight.reshape(tiles, LANES),
        obs_kernel,
    )
    grad_ens, grad_static, departures = pl.pallas_call(
        hand_over,
        out_shape=tuple(shape(x.shape, F32) for x in (grad_ens, grad_static, departures)),
        in_specs=[a, a, a],
        out_specs=(a, a, a),
        scratch_shapes=[
            vmem(*x.shape) for x in (grad_ens, grad_static, departures)
        ]
        + [dma(members + 2), dma(members + 2)],
        name="results",
    )(grad_ens, grad_static, departures)
    return (grad_ens, grad_static, departures.reshape(-1))


def solution(mesh):
    return jax.shard_map(
        per_device,
        mesh=mesh,
        in_specs=(
            P("ens", None, "tile", None),
            P(None, "tile", None),
            P(None, "ens", None, "tile", None),
            P(),
            P("tile", None),
            P("tile", None),
            P("tile", None),
            P("tile"),
            P("tile"),
            P("tile"),
            P("tile"),
            P(None, "tile"),
        ),
        out_specs=(P("ens", None, "tile", None), P(None, "tile", None), P("tile")),
        check_vma=False,
    )
```

```python
import functools
import math

import jax
import jax.numpy as jnp
from jax import lax
from jax.experimental import pallas as pl
from jax.experimental.pallas import tpu as pltpu
from jax.sharding import PartitionSpec as P

NT = 2
NDIFF = 4
BETA_ENS = 0.8
BETA_STATIC = 0.6
DIFF_BASE = 0.06
LANES = 128
MESH = pl.DeviceIdType.MESH
F32 = jnp.float32
BF16 = jnp.bfloat16


def split3(x):
    a = x.astype(BF16)
    rest = x - a.astype(F32)
    b = rest.astype(BF16)
    c = (rest - b.astype(F32)).astype(BF16)
    return a, b, c


def split2(x):
    a = x.astype(BF16).astype(F32)
    return a, x - a


def left(x):
    return pltpu.roll(x, 1, 1)


def right(x):
    return pltpu.roll(x, x.shape[1] - 1, 1)


def kernel(
    factor,
    ens,
    tiles,
    ctl_hbm,
    stc,
    per_hbm,
    sigma,
    cls,
    east,
    north,
    ocol,
    ocnt,
    oval,
    owgt,
    oker,
    gens_hbm,
    gsta,
    gdep,
    ctl,
    per,
    gens,
    s_in,
    s_out,
    okb,
    dif,
    dif_u,
    dif_d,
    dbc,
    dsq,
    fin,
    sta,
    sta_u,
    sta_d,
    stb,
    wnd_u,
    wnd_d,
    rcv_wu,
    rcv_wd,
    cc,
    cu,
    cd,
    pp,
    ff,
    fu,
    fd,
    wa,
    wb,
    acc,
    accb,
    rbuf,
    obs_s,
    obs_r,
    onehot,
    himask,
    okern,
    oaux,
    adjb,
    abuf,
    adjf,
    depp,
    depx,
    dx,
    dbuf,
    deps,
    depr,
    depf,
    s_pre,
    r_pre,
    s_c,
    r_c,
    s_f,
    r_f,
    s_obs,
    r_obs,
    s_rs,
    r_rs,
    s_ag,
    r_ag,
    s_dg,
    r_dg,
    s_w,
    r_w,
    s_dep,
    r_dep,
    s_o2,
    r_o2,
    s_dx,
    r_dx,
    s_d2,
    r_d2,
):
    members, lev, rows, width = ctl.shape
    load_ctl = pltpu.make_async_copy(ctl_hbm, ctl, s_in.at[0])
    load_per = pltpu.make_async_copy(per_hbm, per, s_in.at[1])
    load_ctl.start()
    load_per.start()
    hi_n = NT * rows
    e = lax.axis_index("ens")
    t = lax.axis_index("tile")
    ny = ens // 2
    y = e // 2
    xl = lax.rem(e, 2)
    partner = 2 * y + 1 - xl
    group = tiles // ny
    kin = lax.rem(y - lax.rem(t, ny) + ny, ny)
    line_t = t // ny
    up = lax.rem(t + tiles - 1, tiles)
    down = lax.rem(t + 1, tiles)
    first = t == 0
    last = t == tiles - 1

    def remote(src, dst, ssem, rsem, e_to, t_to):
        return pltpu.make_async_remote_copy(
            src_ref=src,
            dst_ref=dst,
            send_sem=ssem,
            recv_sem=rsem,
            device_id=(e_to, t_to),
            device_id_type=MESH,
        )

    def loop(n, body):
        def step(i, carry):
            body(i)
            return carry

        lax.fori_loop(0, n, step, 0)

    def span(low, high, body):
        def step(i, carry):
            body(i)
            return carry

        lax.fori_loop(low, high, step, 0)

    def each_e(body):
        span(1, ens, lambda k: body(lax.rem(e + k, ens)))

    def peer_y(k):
        return lax.rem(y + k, ny)

    def each_y(body):
        span(1, ny, lambda k: body(peer_y(k)))

    def each_kin(body):
        def one(j):
            pl.when(j * ny + kin != t)(lambda: body(j, j * ny + kin))

        loop(group, one)

    barrier = pltpu.get_barrier_semaphore()

    def greet(e_to, t_to):
        pl.semaphore_signal(barrier, inc=1, device_id=(e_to, t_to), device_id_type=MESH)

    greet(e, up)
    greet(e, down)
    each_kin(lambda j, d: greet(e, d))
    each_e(lambda b: greet(b, t))
    alone = jnp.where(kin == lax.rem(t, ny), 1, 0)
    dif[...] = jnp.sqrt(DIFF_BASE * (cls[...].astype(F32) + 1.0))
    sub = lax.broadcasted_iota(jnp.int32, (lev, width), 0)
    scale = jnp.zeros((lev, width), F32)
    for l in range(lev):
        scale = jnp.where(sub == l, BETA_STATIC * sigma[l], scale)
    for r in range(rows):
        sta[r] = scale * stc[:, r, :]
    load_ctl.wait()
    pl.semaphore_wait(barrier, 2 + group - alone + ens - 1)

    pre = [
        remote(dif, dif_u, s_pre.at[0], r_pre.at[0], e, down),
        remote(dif, dif_d, s_pre.at[1], r_pre.at[1], e, up),
        remote(sta.at[rows - 1], sta_u, s_pre.at[2], r_pre.at[2], e, down),
        remote(sta.at[0], sta_d, s_pre.at[3], r_pre.at[3], e, up),
    ]
    for copy in pre:
        copy.start()

    def halo(m, own, from_up, from_down, ssem, rsem):
        src = own.at[m]
        return (
            remote(src, from_up.at[m], ssem.at[0, m], rsem.at[0, m], e, down),
            remote(src, from_down.at[m], ssem.at[1, m], rsem.at[1, m], e, up),
        )

    def send_control(m):
        for r in range(rows):
            cc[m, r] = ctl[m, :, r, :]
        for copy in halo(m, cc, cu, cd, s_c, r_c):
            copy.start()

    ahead = members // 4
    span(0, ahead, send_control)

    count = jnp.broadcast_to(ocnt[...].astype(F32), (tiles, tiles))
    d_sub = lax.broadcasted_iota(jnp.int32, (tiles, tiles), 0)
    d_lane = lax.broadcasted_iota(jnp.int32, (tiles, tiles), 1)
    count_col = jnp.sum(
        jnp.where(d_lane == d_sub, count, 0.0), axis=1, keepdims=True
    )
    start_col = jnp.sum(jnp.where(d_lane < d_sub, count, 0.0), axis=1, keepdims=True)
    start_row = jnp.sum(
        jnp.where(d_sub < d_lane, jnp.broadcast_to(count_col, (tiles, tiles)), 0.0),
        axis=0,
        keepdims=True,
    )
    def places(start_of, count_of):
        shape = (start_of.shape[0], LANES)
        begin = jnp.broadcast_to(start_of, shape).astype(jnp.int32)
        lane = lax.broadcasted_iota(jnp.int32, shape, 1)
        usable = lane < jnp.broadcast_to(count_of, shape).astype(jnp.int32)
        return lane, begin & (LANES - 1), usable

    def turn(x, shift, back):
        for bit in range(LANES.bit_length() - 1):
            by = LANES - (1 << bit) if back else 1 << bit
            x = jnp.where(shift & (1 << bit) != 0, pltpu.roll(x, by, 1), x)
        return x

    kin_count = jnp.broadcast_to(ocnt[...].astype(F32), (group, tiles))
    kin_sub = lax.broadcasted_iota(jnp.int32, (group, tiles), 0) * ny + kin
    kin_lane = lax.broadcasted_iota(jnp.int32, (group, tiles), 1)
    kin_start = jnp.sum(
        jnp.where(kin_lane < kin_sub, kin_count, 0.0), axis=1, keepdims=True
    )
    kin_own = jnp.sum(
        jnp.where(kin_lane == kin_sub, kin_count, 0.0), axis=1, keepdims=True
    )
    lane, shift, usable = places(kin_start, kin_own)
    line_col = jnp.broadcast_to(kin_start, (group, tiles)).astype(jnp.int32) // LANES
    pick = jnp.concatenate(
        [
            jnp.where(kin_lane == line_col, 1.0, 0.0),
            jnp.where(kin_lane == line_col + 1, 1.0, 0.0),
        ],
        axis=0,
    ).astype(BF16)
    for b in range(tiles):
        okb[b] = oker[:, b * LANES : (b + 1) * LANES]
    for q in range(lev + 3):
        if q < lev:
            part = okb[:, q, :]
        else:
            part = (ocol, oval, owgt)[q - lev][...].astype(F32)
        two = sum(
            jnp.dot(pick, piece, preferred_element_type=F32) for piece in split3(part)
        )
        value = jnp.where(lane >= shift, two[0:group], two[group : 2 * group])
        value = turn(value, shift, True)
        if q == lev:
            value = jnp.where(usable, value, -1.0)
        obs_s[:, q, :] = value
    for q in range(lev + 3, 2 * lev):
        obs_s[:, q, :] = jnp.zeros((group, LANES), F32)

    def obs_copy(j, d):
        return remote(
            obs_s.at[j], obs_r.at[y, line_t], s_obs.at[j], r_obs.at[line_t], e, d
        )

    each_kin(lambda j, d: obs_copy(j, d).start())

    @pl.when(alone == 1)
    def _():
        obs_r[y, line_t] = obs_s[line_t]

    span(ahead, members, send_control)

    def obs_on(b):
        return remote(obs_r.at[y], obs_r.at[y], s_o2.at[b], r_o2.at[y], 2 * b + xl, t)

    def obs_mid():
        each_kin(
            lambda j, d: remote(
                obs_s.at[j], obs_r.at[y, j], s_obs.at[j], r_obs.at[j], e, d
            ).wait_recv()
        )
        each_y(lambda b: obs_on(b).start())

    def obs_wait():
        each_y(
            lambda b: remote(
                obs_r.at[b], obs_r.at[b], s_o2.at[b], r_o2.at[b], 2 * b + xl, t
            ).wait_recv()
        )

    def spread(m):
        for s in range(NT):
            block = per[s, m].astype(F32)
            for r in range(rows):
                pp[s, m, r] = block[:, r, :]

    load_per.wait()
    loop(members, spread)

    pre[0].wait_recv()
    pre[1].wait_recv()
    above = jnp.where(first, 0.0, dif_u[...])
    below = jnp.where(last, 0.0, dif_d[...])
    own = dif[...]
    total_rows = rows + 2 * NDIFF
    for i in range(total_rows):
        src = above if i < NDIFF else (own if i < NDIFF + rows else below)
        j = i if i < NDIFF else (i - NDIFF if i < NDIFF + rows else i - NDIFF - rows)
        line = jnp.broadcast_to(src[j : j + 1, :], (lev, width))
        dbc[i] = line
        dsq[i] = line * line
        if NDIFF <= i < NDIFF + rows:
            fin[i - NDIFF] = factor / line

    def tile_of(x, b):
        return x[:, b * LANES : (b + 1) * LANES]

    pre[2].wait_recv()
    pre[3].wait_recv()

    def winds(r):
        we = jnp.broadcast_to(east[r : r + 1, :], (lev, width))
        wn = jnp.broadcast_to(north[r : r + 1, :], (lev, width))
        return (
            jnp.maximum(we, 0.0),
            jnp.minimum(we, 0.0),
            jnp.maximum(wn, 0.0),
            jnp.minimum(wn, 0.0),
        )

    for r in range(rows):
        ep, em, np_, nm = winds(r)
        q = sta[r]
        above = sta[r - 1] if r else jnp.where(first, 0.0, sta_u[...])
        below = sta[r + 1] if r < rows - 1 else jnp.where(last, 0.0, sta_d[...])
        moved = q - ep * (q - left(q)) - em * (right(q) - q)
        moved = moved - np_ * (q - above) - nm * (below - q)
        for b in range(ens):
            stb[b, r] = tile_of(q, b)
            stb[b, rows + r] = tile_of(moved, b)

    def smooth(m, refs):
        for i in range(total_rows):
            ref, r = source_of(i, refs)
            wa[i] = dbc[i] * ref[m, r]
        src, dst = wa, wb
        for step in range(NDIFF):
            for i in range(step + 1, total_rows - 1 - step):
                w = src[i]
                lap = src[i + 1] + src[i - 1] + left(w) + right(w) - 4.0 * w
                dst[i] = w + dsq[i] * lap
            src, dst = dst, src
        return [src[NDIFF + r] for r in range(rows)]

    def source_of(i, refs):
        if i < NDIFF:
            return refs[0], i
        if i < NDIFF + rows:
            return refs[1], i - NDIFF
        return refs[2], i - NDIFF - rows

    def forward(m):
        for copy in halo(m, cc, cu, cd, s_c, r_c):
            copy.wait_recv()
        res = smooth(m, (cu, cc, cd))
        for r in range(rows):
            for s in range(NT):
                acc[s * rows + r] += pp[s, m, r] * res[r]

    def rs_copy(b):
        return remote(accb.at[b], rbuf.at[e], s_rs.at[b], r_rs.at[e], b, t)

    def rs_start():
        for h in range(hi_n):
            value = acc[h] * fin[h % rows]
            for b in range(ens):
                accb[b, h] = tile_of(value, b)
        each_e(lambda b: rs_copy(b).start())

    def rs_wait():
        each_e(
            lambda b: remote(
                accb.at[b], rbuf.at[b], s_rs.at[b], r_rs.at[b], b, t
            ).wait_recv()
        )
        rbuf[e] = accb[e]

    chunks = ny

    def lines_of(g, i, n=1):
        return jnp.concatenate(
            [obs_r[g, j, i : i + n, :] for j in range(group)], axis=1
        )

    lo_iota = lax.broadcasted_iota(jnp.int32, (LANES, group * LANES), 0)

    def hot(g):
        col = lines_of(g, lev).astype(jnp.int32)
        lo = col & (LANES - 1)
        block = (col // LANES) & (ens - 1)
        unit = jnp.where((col >= 0) & (block == e), col // width, -1)
        himask[g] = jnp.broadcast_to(unit, (lev, group * LANES))
        okern[g] = lines_of(g, 0, lev)
        oaux[g, 0:1, :] = lines_of(g, lev + 1)
        oaux[g, 1:2, :] = lines_of(g, lev + 2)
        onehot[g] = jnp.where(
            jnp.broadcast_to(lo, (LANES, group * LANES)) == lo_iota, 1.0, 0.0
        ).astype(BF16)

    def observe():
        points = hi_n * lev
        values = []
        for u in range(hi_n):
            value = stb[e, u]
            for b in range(ens):
                value = value + rbuf[b, u]
            values.append(value)
        table = jnp.concatenate(split2(jnp.concatenate(values, axis=0)), axis=0)
        table = table.astype(BF16)
        total = jnp.zeros((2 * points, LANES), F32)
        for g in range(chunks):
            hi = himask[g]
            kern = okern[g]
            flat = jnp.dot(table, onehot[g], preferred_element_type=F32)
            profile = jnp.zeros(kern.shape, F32)
            for j in range(hi_n):
                value = flat[j * lev : (j + 1) * lev]
                value = value + flat[points + j * lev : points + (j + 1) * lev]
                profile = jnp.where(hi == j, value, profile)
            evolved = jnp.sum(kern * profile, axis=0, keepdims=True)
            dep = oaux[g, 1:2, :] * (evolved - oaux[g, 0:1, :])
            dep = jnp.where(hi[0:1] >= 0, dep, 0.0)
            for j in range(group):
                depp[g, j] = tile_of(dep, j)
            push = kern * dep
            place = jnp.concatenate(
                [jnp.where(hi == j, push, 0.0) for j in range(hi_n)], axis=0
            )
            place = jnp.concatenate(split2(place), axis=0).astype(BF16)
            total = total + lax.dot_general(
                place, onehot[g], (((1,), (1,)), ((), ())), preferred_element_type=F32
            )
        total = total[0:points] + total[points : 2 * points]
        for j in range(hi_n):
            adjb[j] = total[j * lev : (j + 1) * lev]
            abuf[e, j] = total[j * lev : (j + 1) * lev]
        each_e(lambda b: ag_copy(b).start())

    def ag_copy(b):
        return remote(adjb, abuf.at[e], s_ag.at[b], r_ag.at[e], b, t)

    def ag_wait():
        each_e(
            lambda b: remote(
                adjb, abuf.at[b], s_ag.at[b], r_ag.at[b], b, t
            ).wait_recv()
        )
        for h in range(hi_n):
            adjf[h] = jnp.concatenate([abuf[b, h] for b in range(ens)], axis=1)

    dx_copy = remote(depp, dx, s_dx.at[0], r_dx.at[0], partner, t)

    def dg_copy(b):
        return remote(depx, dbuf.at[y], s_dg.at[b], r_dg.at[y], 2 * b + xl, t)

    def dg_mid():
        dx_copy.wait_recv()
        depx[...] = depp[...] + dx[...]
        each_y(lambda b: dg_copy(b).start())

    def force(m):
        for r in range(rows):
            ff[m, r] = pp[0, m, r] * adjf[r] + pp[1, m, r] * adjf[rows + r]
        for copy in halo(m, ff, fu, fd, s_f, r_f):
            copy.start()

    def store_of(m):
        return pltpu.make_async_copy(gens.at[m], gens_hbm.at[m], s_out.at[m])

    def backward(m):
        for copy in halo(m, ff, fu, fd, s_f, r_f):
            copy.wait_recv()
        res = smooth(m, (fu, ff, fd))
        for r in range(rows):
            gens[m, :, r, :] = cc[m, r] + res[r] * fin[r]
        store_of(m).start()

    for h in range(hi_n):
        acc[h] = jnp.zeros((lev, width), F32)
    span(0, members // 2, forward)
    obs_mid()
    span(members // 2, members, forward)
    rs_start()
    obs_wait()
    for g in range(chunks):
        hot(g)
    rs_wait()
    observe()
    dx_copy.start()
    ag_wait()
    wnd_u[...] = winds(0)[2] * adjf[rows]
    wnd_d[...] = winds(rows - 1)[3] * adjf[2 * rows - 1]
    wind = [
        remote(wnd_d, rcv_wu, s_w.at[0], r_w.at[0], e, down),
        remote(wnd_u, rcv_wd, s_w.at[1], r_w.at[1], e, up),
    ]
    q1 = members * 3 // 8
    dg_mid()
    span(0, q1, force)
    for copy in wind:
        copy.start()

    each_y(
        lambda b: remote(
            depx, dbuf.at[b], s_dg.at[b], r_dg.at[b], 2 * b + xl, t
        ).wait_recv()
    )
    dbuf[y] = depx[...]
    value = dbuf[0]
    for b in range(1, ny):
        value = value + dbuf[b]
    deps[...] = value

    def dep_copy(j, s):
        return remote(
            deps.at[y, j], depr.at[y, line_t], s_dep.at[j], r_dep.at[line_t], e, s
        )

    each_kin(lambda j, s: dep_copy(j, s).start())

    @pl.when(alone == 1)
    def _():
        depr[y, line_t] = deps[y, line_t]

    span(q1, members, force)

    for copy in wind:
        copy.wait_recv()
    for r in range(rows):
        ep, em, np_, nm = winds(r)
        a = adjf[rows + r]
        if r < rows - 1:
            lower = winds(r + 1)[2] * adjf[rows + r + 1]
        else:
            lower = jnp.where(last, 0.0, rcv_wd[...])
        if r:
            upper = winds(r - 1)[3] * adjf[rows + r - 1]
        else:
            upper = jnp.where(first, 0.0, rcv_wu[...])
        moved = a * (1.0 - ep + em - np_ + nm) + right(ep * a) - left(em * a)
        moved = moved + lower - upper
        gsta[:, r, :] = stc[:, r, :] + scale * (adjf[r] + moved)

    span(0, q1, backward)
    each_kin(
        lambda j, s: remote(
            deps.at[y, j], depr.at[y, j], s_dep.at[j], r_dep.at[j], e, s
        ).wait_recv()
    )

    def dep_on(b):
        return remote(depr.at[y], depr.at[y], s_d2.at[b], r_d2.at[y], 2 * b + xl, t)

    each_y(lambda b: dep_on(b).start())
    span(q1, members, backward)

    each_y(
        lambda b: remote(
            depr.at[b], depr.at[b], s_d2.at[b], r_d2.at[b], 2 * b + xl, t
        ).wait_recv()
    )
    for d in range(tiles):
        depf[d : d + 1, :] = depr[lax.rem(t + d, ny), d // ny]
    lane, shift, usable = places(start_col, count_col)
    line_row = jnp.broadcast_to(start_row, (tiles, tiles)).astype(jnp.int32) // LANES
    spread0 = jnp.where(d_sub == line_row, 1.0, 0.0).astype(BF16)
    spread1 = jnp.where(d_sub == line_row + 1, 1.0, 0.0).astype(BF16)
    value = turn(jnp.where(usable, depf[...], 0.0), shift, False)
    out = jnp.zeros((tiles, LANES), F32)
    for piece in split3(jnp.where(lane >= shift, value, 0.0)):
        out = out + jnp.dot(spread0, piece, preferred_element_type=F32)
    for piece in split3(jnp.where(lane < shift, value, 0.0)):
        out = out + jnp.dot(spread1, piece, preferred_element_type=F32)
    gdep[...] = out

    loop(members, lambda m: store_of(m).wait())
    for copy in pre + wind:
        copy.wait_send()

    def sent(m):
        for copy in halo(m, cc, cu, cd, s_c, r_c) + halo(m, ff, fu, fd, s_f, r_f):
            copy.wait_send()

    loop(members, sent)

    each_kin(lambda j, d: obs_copy(j, d).wait_send())
    each_kin(lambda j, d: dep_copy(j, d).wait_send())
    dx_copy.wait_send()
    def sent_y(b):
        obs_on(b).wait_send()
        dep_on(b).wait_send()
        dg_copy(b).wait_send()

    each_y(sent_y)
    each_e(lambda b: rs_copy(b).wait_send())
    each_e(lambda b: ag_copy(b).wait_send())


def hand_over(x0, x1, x2, y0, y1, y2, b0, b1, b2, s_in, s_out):
    members = x0.shape[0]
    triples = [(x0.at[m], b0.at[m], y0.at[m]) for m in range(members)]
    triples += [(x1, b1, y1), (x2, b2, y2)]
    come = [
        pltpu.make_async_copy(x, b, s_in.at[i]) for i, (x, b, y) in enumerate(triples)
    ]
    go = [
        pltpu.make_async_copy(b, y, s_out.at[i]) for i, (x, b, y) in enumerate(triples)
    ]
    for copy in come:
        copy.start()
    for a, b in zip(come, go):
        a.wait()
        b.start()
    for copy in go:
        copy.wait()


def per_device(
    ens_control,
    static_control,
    perturbations,
    level_sigma,
    length_class,
    courant_east,
    courant_north,
    obs_column,
    obs_count,
    obs_value,
    obs_weight,
    obs_kernel,
):
    members, lev, rows, width = ens_control.shape
    ens = lax.axis_size("ens")
    tiles = lax.axis_size("tile")
    factor = BETA_ENS / math.sqrt(ens * members - 1)
    hi_n = NT * rows
    vmem = lambda *shape, dtype=F32: pltpu.VMEM(shape, dtype)
    dma = lambda *shape: pltpu.SemaphoreType.DMA(shape)
    line = (lev, width)
    ny = ens // 2
    group = tiles // ny
    chunks = ny
    slots = group * LANES
    total_rows = rows + 2 * NDIFF
    fields = (members, rows) + line
    scratch = [
        vmem(*ens_control.shape),
        vmem(*perturbations.shape, dtype=BF16),
        vmem(*ens_control.shape),
        dma(2),
        dma(members),
        vmem(tiles, lev, LANES),
        vmem(rows, width),
        vmem(rows, width),
        vmem(rows, width),
        vmem(total_rows, lev, width),
        vmem(total_rows, lev, width),
        vmem(rows, lev, width),
        vmem(rows, *line),
        vmem(*line),
        vmem(*line),
        vmem(ens, hi_n, lev, LANES),
        vmem(*line),
        vmem(*line),
        vmem(*line),
        vmem(*line),
        vmem(*fields),
        vmem(*fields),
        vmem(*fields),
        vmem(NT, *fields),
        vmem(*fields),
        vmem(*fields),
        vmem(*fields),
        vmem(total_rows, lev, width),
        vmem(total_rows, lev, width),
        vmem(hi_n, lev, width),
        vmem(ens, hi_n, lev, LANES),
        vmem(ens, hi_n, lev, LANES),
        vmem(group, 2 * lev, LANES),
        vmem(ny, group, 2 * lev, LANES),
        vmem(chunks, LANES, slots, dtype=BF16),
        vmem(chunks, lev, slots, dtype=jnp.int32),
        vmem(chunks, lev, slots),
        vmem(chunks, lev, slots),
        vmem(hi_n, lev, LANES),
        vmem(ens, hi_n, lev, LANES),
        vmem(hi_n, *line),
        vmem(ny, group, 1, LANES),
        vmem(ny, group, 1, LANES),
        vmem(ny, group, 1, LANES),
        vmem(ny, ny, group, 1, LANES),
        vmem(ny, group, 1, LANES),
        vmem(ny, group, 1, LANES),
        vmem(tiles, LANES),
        dma(4), dma(4),
        dma(2, members), dma(2, members),
        dma(2, members), dma(2, members),
        dma(group), dma(group),
        dma(ens), dma(ens),
        dma(ens), dma(ens),
        dma(ny), dma(ny),
        dma(2), dma(2),
        dma(group), dma(group),
        dma(ny), dma(ny),
        dma(1), dma(1),
        dma(ny), dma(ny),
    ]
    v = pl.BlockSpec(memory_space=pltpu.VMEM)
    s = pl.BlockSpec(memory_space=pltpu.SMEM)
    a = pl.BlockSpec(memory_space=pl.ANY)
    shape = jax.ShapeDtypeStruct
    grad_ens, grad_static, departures = pl.pallas_call(
        functools.partial(kernel, factor, ens, tiles),
        out_shape=(
            shape(ens_control.shape, F32),
            shape(static_control.shape, F32),
            shape((tiles, LANES), F32),
        ),
        in_specs=[a, v, a, s, v, v, v, v, v, v, v, v],
        out_specs=(a, v, v),
        scratch_shapes=scratch,
        name="gradient",
        compiler_params=pltpu.CompilerParams(
            collective_id=0, has_side_effects=True, vmem_limit_bytes=56 * 2**20
        ),
    )(
        ens_control,
        static_control,
        perturbations,
        level_sigma,
        length_class,
        courant_east,
        courant_north,
        obs_column.reshape(tiles, LANES),
        obs_count.reshape(1, tiles),
        obs_value.reshape(tiles, LANES),
        obs_weight.reshape(tiles, LANES),
        obs_kernel,
    )
    grad_ens, grad_static, departures = pl.pallas_call(
        hand_over,
        out_shape=tuple(shape(x.shape, F32) for x in (grad_ens, grad_static, departures)),
        in_specs=[a, a, a],
        out_specs=(a, a, a),
        scratch_shapes=[
            vmem(*x.shape) for x in (grad_ens, grad_static, departures)
        ]
        + [dma(members + 2), dma(members + 2)],
        name="results",
    )(grad_ens, grad_static, departures)
    return (grad_ens, grad_static, departures.reshape(-1))


def solution(mesh):
    return jax.shard_map(
        per_device,
        mesh=mesh,
        in_specs=(
            P("ens", None, "tile", None),
            P(None, "tile", None),
            P(None, "ens", None, "tile", None),
            P(),
            P("tile", None),
            P("tile", None),
            P("tile", None),
            P("tile"),
            P("tile"),
            P("tile"),
            P("tile"),
            P(None, "tile"),
        ),
        out_specs=(P("ens", None, "tile", None), P(None, "tile", None), P("tile")),
        check_vma=False,
    )
```

```python
import functools
import math

import jax
import jax.numpy as jnp
from jax import lax
from jax.experimental import pallas as pl
from jax.experimental.pallas import tpu as pltpu
from jax.sharding import PartitionSpec as P

NT = 2
NDIFF = 4
BETA_ENS = 0.8
BETA_STATIC = 0.6
DIFF_BASE = 0.06
LANES = 128
MESH = pl.DeviceIdType.MESH
F32 = jnp.float32
BF16 = jnp.bfloat16


def split3(x):
    a = x.astype(BF16)
    rest = x - a.astype(F32)
    b = rest.astype(BF16)
    c = (rest - b.astype(F32)).astype(BF16)
    return a, b, c


def split2(x):
    a = x.astype(BF16).astype(F32)
    return a, x - a


def left(x):
    return pltpu.roll(x, 1, 1)


def right(x):
    return pltpu.roll(x, x.shape[1] - 1, 1)


def kernel(
    factor,
    ens,
    tiles,
    ctl_hbm,
    stc_hbm,
    per_hbm,
    sigma_hbm,
    cls_hbm,
    east_hbm,
    north_hbm,
    ocol_hbm,
    ocnt_hbm,
    oval_hbm,
    owgt_hbm,
    oker_hbm,
    gens_hbm,
    gsta_hbm,
    gdep,
    ctl,
    stc,
    per,
    sigma,
    cls,
    east,
    north,
    ocol,
    ocnt,
    oval,
    owgt,
    oker,
    gens,
    gsta,
    s_in,
    s_out,
    okb,
    dif,
    dif_u,
    dif_d,
    dbc,
    dsq,
    fin,
    sta,
    sta_u,
    sta_d,
    stb,
    wnd_u,
    wnd_d,
    rcv_wu,
    rcv_wd,
    cc,
    cu,
    cd,
    pp,
    ff,
    fu,
    fd,
    wa,
    wb,
    acc,
    accb,
    rbuf,
    obs_s,
    obs_r,
    onehot,
    himask,
    okern,
    oaux,
    adjb,
    abuf,
    adjf,
    depp,
    depx,
    dx,
    dbuf,
    deps,
    depr,
    depf,
    s_pre,
    r_pre,
    s_c,
    r_c,
    s_f,
    r_f,
    s_obs,
    r_obs,
    s_rs,
    r_rs,
    s_ag,
    r_ag,
    s_dg,
    r_dg,
    s_w,
    r_w,
    s_dep,
    r_dep,
    s_o2,
    r_o2,
    s_dx,
    r_dx,
    s_d2,
    r_d2,
):
    members, lev, rows, width = ctl.shape
    hi_n = NT * rows
    e = lax.axis_index("ens")
    t = lax.axis_index("tile")
    ny = ens // 2
    y = e // 2
    xl = lax.rem(e, 2)
    partner = 2 * y + 1 - xl
    group = tiles // ny
    kin = lax.rem(y - lax.rem(t, ny) + ny, ny)
    line_t = t // ny
    up = lax.rem(t + tiles - 1, tiles)
    down = lax.rem(t + 1, tiles)
    first = t == 0
    last = t == tiles - 1

    def remote(src, dst, ssem, rsem, e_to, t_to):
        return pltpu.make_async_remote_copy(
            src_ref=src,
            dst_ref=dst,
            send_sem=ssem,
            recv_sem=rsem,
            device_id=(e_to, t_to),
            device_id_type=MESH,
        )

    def loop(n, body):
        def step(i, carry):
            body(i)
            return carry

        lax.fori_loop(0, n, step, 0)

    def span(low, high, body):
        def step(i, carry):
            body(i)
            return carry

        lax.fori_loop(low, high, step, 0)

    def each_e(body):
        span(1, ens, lambda k: body(lax.rem(e + k, ens)))

    def peer_y(k):
        return lax.rem(y + k, ny)

    def each_y(body):
        span(1, ny, lambda k: body(peer_y(k)))

    def each_kin(body):
        def one(j):
            pl.when(j * ny + kin != t)(lambda: body(j, j * ny + kin))

        loop(group, one)

    barrier = pltpu.get_barrier_semaphore()

    def greet(e_to, t_to):
        pl.semaphore_signal(barrier, inc=1, device_id=(e_to, t_to), device_id_type=MESH)

    greet(e, up)
    greet(e, down)
    each_kin(lambda j, d: greet(e, d))
    each_e(lambda b: greet(b, t))
    alone = jnp.where(kin == lax.rem(t, ny), 1, 0)
    inputs = (
        (cls_hbm, cls),
        (stc_hbm, stc),
        (sigma_hbm, sigma),
        (ctl_hbm, ctl),
        (ocnt_hbm, ocnt),
        (oker_hbm, oker),
        (ocol_hbm, ocol),
        (oval_hbm, oval),
        (owgt_hbm, owgt),
        (per_hbm, per),
        (east_hbm, east),
        (north_hbm, north),
    )
    loads = [
        pltpu.make_async_copy(src, dst, s_in.at[i]) for i, (src, dst) in enumerate(inputs)
    ]
    for copy in loads:
        copy.start()
    for copy in loads[0:3]:
        copy.wait()
    dif[...] = jnp.sqrt(DIFF_BASE * (cls[...].astype(F32) + 1.0))
    sub = lax.broadcasted_iota(jnp.int32, (lev, width), 0)
    scale = jnp.zeros((lev, width), F32)
    for l in range(lev):
        scale = jnp.where(sub == l, BETA_STATIC * sigma[l], scale)
    for r in range(rows):
        sta[r] = scale * stc[:, r, :]
    loads[3].wait()
    pl.semaphore_wait(barrier, 2 + group - alone + ens - 1)

    pre = [
        remote(dif, dif_u, s_pre.at[0], r_pre.at[0], e, down),
        remote(dif, dif_d, s_pre.at[1], r_pre.at[1], e, up),
        remote(sta.at[rows - 1], sta_u, s_pre.at[2], r_pre.at[2], e, down),
        remote(sta.at[0], sta_d, s_pre.at[3], r_pre.at[3], e, up),
    ]
    for copy in pre:
        copy.start()

    def halo(m, own, from_up, from_down, ssem, rsem):
        src = own.at[m]
        return (
            remote(src, from_up.at[m], ssem.at[0, m], rsem.at[0, m], e, down),
            remote(src, from_down.at[m], ssem.at[1, m], rsem.at[1, m], e, up),
        )

    def send_control(m):
        for r in range(rows):
            cc[m, r] = ctl[m, :, r, :]
        for copy in halo(m, cc, cu, cd, s_c, r_c):
            copy.start()

    ahead = members // 4
    span(0, ahead, send_control)

    for copy in loads[4:9]:
        copy.wait()

    count = jnp.broadcast_to(ocnt[...].astype(F32), (tiles, tiles))
    d_sub = lax.broadcasted_iota(jnp.int32, (tiles, tiles), 0)
    d_lane = lax.broadcasted_iota(jnp.int32, (tiles, tiles), 1)
    count_col = jnp.sum(
        jnp.where(d_lane == d_sub, count, 0.0), axis=1, keepdims=True
    )
    start_col = jnp.sum(jnp.where(d_lane < d_sub, count, 0.0), axis=1, keepdims=True)
    start_row = jnp.sum(
        jnp.where(d_sub < d_lane, jnp.broadcast_to(count_col, (tiles, tiles)), 0.0),
        axis=0,
        keepdims=True,
    )
    def places(start_of, count_of):
        shape = (start_of.shape[0], LANES)
        begin = jnp.broadcast_to(start_of, shape).astype(jnp.int32)
        lane = lax.broadcasted_iota(jnp.int32, shape, 1)
        usable = lane < jnp.broadcast_to(count_of, shape).astype(jnp.int32)
        return lane, begin & (LANES - 1), usable

    def turn(x, shift, back):
        for bit in range(LANES.bit_length() - 1):
            by = LANES - (1 << bit) if back else 1 << bit
            x = jnp.where(shift & (1 << bit) != 0, pltpu.roll(x, by, 1), x)
        return x

    kin_count = jnp.broadcast_to(ocnt[...].astype(F32), (group, tiles))
    kin_sub = lax.broadcasted_iota(jnp.int32, (group, tiles), 0) * ny + kin
    kin_lane = lax.broadcasted_iota(jnp.int32, (group, tiles), 1)
    kin_start = jnp.sum(
        jnp.where(kin_lane < kin_sub, kin_count, 0.0), axis=1, keepdims=True
    )
    kin_own = jnp.sum(
        jnp.where(kin_lane == kin_sub, kin_count, 0.0), axis=1, keepdims=True
    )
    lane, shift, usable = places(kin_start, kin_own)
    line_col = jnp.broadcast_to(kin_start, (group, tiles)).astype(jnp.int32) // LANES
    pick = jnp.concatenate(
        [
            jnp.where(kin_lane == line_col, 1.0, 0.0),
            jnp.where(kin_lane == line_col + 1, 1.0, 0.0),
        ],
        axis=0,
    ).astype(BF16)
    for b in range(tiles):
        okb[b] = oker[:, b * LANES : (b + 1) * LANES]
    for q in range(lev + 3):
        if q < lev:
            part = okb[:, q, :]
        else:
            part = (ocol, oval, owgt)[q - lev][...].astype(F32)
        two = sum(
            jnp.dot(pick, piece, preferred_element_type=F32) for piece in split3(part)
        )
        value = jnp.where(lane >= shift, two[0:group], two[group : 2 * group])
        value = turn(value, shift, True)
        if q == lev:
            value = jnp.where(usable, value, -1.0)
        obs_s[:, q, :] = value
    for q in range(lev + 3, 2 * lev):
        obs_s[:, q, :] = jnp.zeros((group, LANES), F32)

    def obs_copy(j, d):
        return remote(
            obs_s.at[j], obs_r.at[y, line_t], s_obs.at[j], r_obs.at[line_t], e, d
        )

    each_kin(lambda j, d: obs_copy(j, d).start())

    @pl.when(alone == 1)
    def _():
        obs_r[y, line_t] = obs_s[line_t]

    span(ahead, members, send_control)

    def obs_on(b):
        return remote(obs_r.at[y], obs_r.at[y], s_o2.at[b], r_o2.at[y], 2 * b + xl, t)

    def obs_mid():
        each_kin(
            lambda j, d: remote(
                obs_s.at[j], obs_r.at[y, j], s_obs.at[j], r_obs.at[j], e, d
            ).wait_recv()
        )
        each_y(lambda b: obs_on(b).start())

    def obs_wait():
        each_y(
            lambda b: remote(
                obs_r.at[b], obs_r.at[b], s_o2.at[b], r_o2.at[b], 2 * b + xl, t
            ).wait_recv()
        )

    def spread(m):
        for s in range(NT):
            block = per[s, m].astype(F32)
            for r in range(rows):
                pp[s, m, r] = block[:, r, :]

    for copy in loads[9:12]:
        copy.wait()
    loop(members, spread)

    pre[0].wait_recv()
    pre[1].wait_recv()
    above = jnp.where(first, 0.0, dif_u[...])
    below = jnp.where(last, 0.0, dif_d[...])
    own = dif[...]
    total_rows = rows + 2 * NDIFF
    for i in range(total_rows):
        src = above if i < NDIFF else (own if i < NDIFF + rows else below)
        j = i if i < NDIFF else (i - NDIFF if i < NDIFF + rows else i - NDIFF - rows)
        line = jnp.broadcast_to(src[j : j + 1, :], (lev, width))
        dbc[i] = line
        dsq[i] = line * line
        if NDIFF <= i < NDIFF + rows:
            fin[i - NDIFF] = factor / line

    def tile_of(x, b):
        return x[:, b * LANES : (b + 1) * LANES]

    pre[2].wait_recv()
    pre[3].wait_recv()

    def winds(r):
        we = jnp.broadcast_to(east[r : r + 1, :], (lev, width))
        wn = jnp.broadcast_to(north[r : r + 1, :], (lev, width))
        return (
            jnp.maximum(we, 0.0),
            jnp.minimum(we, 0.0),
            jnp.maximum(wn, 0.0),
            jnp.minimum(wn, 0.0),
        )

    for r in range(rows):
        ep, em, np_, nm = winds(r)
        q = sta[r]
        above = sta[r - 1] if r else jnp.where(first, 0.0, sta_u[...])
        below = sta[r + 1] if r < rows - 1 else jnp.where(last, 0.0, sta_d[...])
        moved = q - ep * (q - left(q)) - em * (right(q) - q)
        moved = moved - np_ * (q - above) - nm * (below - q)
        for b in range(ens):
            stb[b, r] = tile_of(q, b)
            stb[b, rows + r] = tile_of(moved, b)

    def smooth(m, refs):
        for i in range(total_rows):
            ref, r = source_of(i, refs)
            wa[i] = dbc[i] * ref[m, r]
        src, dst = wa, wb
        for step in range(NDIFF):
            for i in range(step + 1, total_rows - 1 - step):
                w = src[i]
                lap = src[i + 1] + src[i - 1] + left(w) + right(w) - 4.0 * w
                dst[i] = w + dsq[i] * lap
            src, dst = dst, src
        return [src[NDIFF + r] for r in range(rows)]

    def source_of(i, refs):
        if i < NDIFF:
            return refs[0], i
        if i < NDIFF + rows:
            return refs[1], i - NDIFF
        return refs[2], i - NDIFF - rows

    def forward(m):
        for copy in halo(m, cc, cu, cd, s_c, r_c):
            copy.wait_recv()
        res = smooth(m, (cu, cc, cd))
        for r in range(rows):
            for s in range(NT):
                acc[s * rows + r] += pp[s, m, r] * res[r]

    def rs_copy(b):
        return remote(accb.at[b], rbuf.at[e], s_rs.at[b], r_rs.at[e], b, t)

    def rs_start():
        for h in range(hi_n):
            value = acc[h] * fin[h % rows]
            for b in range(ens):
                accb[b, h] = tile_of(value, b)
        each_e(lambda b: rs_copy(b).start())

    def rs_wait():
        each_e(
            lambda b: remote(
                accb.at[b], rbuf.at[b], s_rs.at[b], r_rs.at[b], b, t
            ).wait_recv()
        )
        rbuf[e] = accb[e]

    chunks = ny

    def lines_of(g, i, n=1):
        return jnp.concatenate(
            [obs_r[g, j, i : i + n, :] for j in range(group)], axis=1
        )

    lo_iota = lax.broadcasted_iota(jnp.int32, (LANES, group * LANES), 0)

    def hot(g):
        col = lines_of(g, lev).astype(jnp.int32)
        lo = col & (LANES - 1)
        block = (col // LANES) & (ens - 1)
        unit = jnp.where((col >= 0) & (block == e), col // width, -1)
        himask[g] = jnp.broadcast_to(unit, (lev, group * LANES))
        okern[g] = lines_of(g, 0, lev)
        oaux[g, 0:1, :] = lines_of(g, lev + 1)
        oaux[g, 1:2, :] = lines_of(g, lev + 2)
        onehot[g] = jnp.where(
            jnp.broadcast_to(lo, (LANES, group * LANES)) == lo_iota, 1.0, 0.0
        ).astype(BF16)

    def observe():
        points = hi_n * lev
        values = []
        for u in range(hi_n):
            value = stb[e, u]
            for b in range(ens):
                value = value + rbuf[b, u]
            values.append(value)
        table = jnp.concatenate(split2(jnp.concatenate(values, axis=0)), axis=0)
        table = table.astype(BF16)
        total = jnp.zeros((2 * points, LANES), F32)
        for g in range(chunks):
            hi = himask[g]
            kern = okern[g]
            flat = jnp.dot(table, onehot[g], preferred_element_type=F32)
            profile = jnp.zeros(kern.shape, F32)
            for j in range(hi_n):
                value = flat[j * lev : (j + 1) * lev]
                value = value + flat[points + j * lev : points + (j + 1) * lev]
                profile = jnp.where(hi == j, value, profile)
            evolved = jnp.sum(kern * profile, axis=0, keepdims=True)
            dep = oaux[g, 1:2, :] * (evolved - oaux[g, 0:1, :])
            dep = jnp.where(hi[0:1] >= 0, dep, 0.0)
            for j in range(group):
                depp[g, j] = tile_of(dep, j)
            push = kern * dep
            place = jnp.concatenate(
                [jnp.where(hi == j, push, 0.0) for j in range(hi_n)], axis=0
            )
            place = jnp.concatenate(split2(place), axis=0).astype(BF16)
            total = total + lax.dot_general(
                place, onehot[g], (((1,), (1,)), ((), ())), preferred_element_type=F32
            )
        total = total[0:points] + total[points : 2 * points]
        for j in range(hi_n):
            adjb[j] = total[j * lev : (j + 1) * lev]
            abuf[e, j] = total[j * lev : (j + 1) * lev]
        each_e(lambda b: ag_copy(b).start())

    def ag_copy(b):
        return remote(adjb, abuf.at[e], s_ag.at[b], r_ag.at[e], b, t)

    def ag_wait():
        each_e(
            lambda b: remote(
                adjb, abuf.at[b], s_ag.at[b], r_ag.at[b], b, t
            ).wait_recv()
        )
        for h in range(hi_n):
            adjf[h] = jnp.concatenate([abuf[b, h] for b in range(ens)], axis=1)

    dx_copy = remote(depp, dx, s_dx.at[0], r_dx.at[0], partner, t)

    def dg_copy(b):
        return remote(depx, dbuf.at[y], s_dg.at[b], r_dg.at[y], 2 * b + xl, t)

    def dg_mid():
        dx_copy.wait_recv()
        depx[...] = depp[...] + dx[...]
        each_y(lambda b: dg_copy(b).start())

    def force(m):
        for r in range(rows):
            ff[m, r] = pp[0, m, r] * adjf[r] + pp[1, m, r] * adjf[rows + r]
        for copy in halo(m, ff, fu, fd, s_f, r_f):
            copy.start()

    def store_of(m):
        return pltpu.make_async_copy(gens.at[m], gens_hbm.at[m], s_out.at[m])

    def backward(m):
        for copy in halo(m, ff, fu, fd, s_f, r_f):
            copy.wait_recv()
        res = smooth(m, (fu, ff, fd))
        for r in range(rows):
            gens[m, :, r, :] = cc[m, r] + res[r] * fin[r]
        store_of(m).start()

    for h in range(hi_n):
        acc[h] = jnp.zeros((lev, width), F32)
    span(0, members // 2, forward)
    obs_mid()
    span(members // 2, members, forward)
    rs_start()
    obs_wait()
    for g in range(chunks):
        hot(g)
    rs_wait()
    observe()
    dx_copy.start()
    ag_wait()
    wnd_u[...] = winds(0)[2] * adjf[rows]
    wnd_d[...] = winds(rows - 1)[3] * adjf[2 * rows - 1]
    wind = [
        remote(wnd_d, rcv_wu, s_w.at[0], r_w.at[0], e, down),
        remote(wnd_u, rcv_wd, s_w.at[1], r_w.at[1], e, up),
    ]
    q1 = members * 3 // 8
    span(0, 1, force)
    dg_mid()
    span(1, q1, force)
    for copy in wind:
        copy.start()

    each_y(
        lambda b: remote(
            depx, dbuf.at[b], s_dg.at[b], r_dg.at[b], 2 * b + xl, t
        ).wait_recv()
    )
    dbuf[y] = depx[...]
    value = dbuf[0]
    for b in range(1, ny):
        value = value + dbuf[b]
    deps[...] = value

    def dep_copy(j, s):
        return remote(
            deps.at[y, j], depr.at[y, line_t], s_dep.at[j], r_dep.at[line_t], e, s
        )

    each_kin(lambda j, s: dep_copy(j, s).start())

    @pl.when(alone == 1)
    def _():
        depr[y, line_t] = deps[y, line_t]

    span(q1, members, force)

    for copy in wind:
        copy.wait_recv()
    for r in range(rows):
        ep, em, np_, nm = winds(r)
        a = adjf[rows + r]
        if r < rows - 1:
            lower = winds(r + 1)[2] * adjf[rows + r + 1]
        else:
            lower = jnp.where(last, 0.0, rcv_wd[...])
        if r:
            upper = winds(r - 1)[3] * adjf[rows + r - 1]
        else:
            upper = jnp.where(first, 0.0, rcv_wu[...])
        moved = a * (1.0 - ep + em - np_ + nm) + right(ep * a) - left(em * a)
        moved = moved + lower - upper
        gsta[:, r, :] = stc[:, r, :] + scale * (adjf[r] + moved)

    store_static = pltpu.make_async_copy(gsta, gsta_hbm, s_out.at[members])
    store_static.start()

    span(0, q1, backward)
    each_kin(
        lambda j, s: remote(
            deps.at[y, j], depr.at[y, j], s_dep.at[j], r_dep.at[j], e, s
        ).wait_recv()
    )

    def dep_on(b):
        return remote(depr.at[y], depr.at[y], s_d2.at[b], r_d2.at[y], 2 * b + xl, t)

    each_y(lambda b: dep_on(b).start())
    span(q1, members, backward)

    each_y(
        lambda b: remote(
            depr.at[b], depr.at[b], s_d2.at[b], r_d2.at[b], 2 * b + xl, t
        ).wait_recv()
    )
    for d in range(tiles):
        depf[d : d + 1, :] = depr[lax.rem(t + d, ny), d // ny]
    lane, shift, usable = places(start_col, count_col)
    line_row = jnp.broadcast_to(start_row, (tiles, tiles)).astype(jnp.int32) // LANES
    spread0 = jnp.where(d_sub == line_row, 1.0, 0.0).astype(BF16)
    spread1 = jnp.where(d_sub == line_row + 1, 1.0, 0.0).astype(BF16)
    value = turn(jnp.where(usable, depf[...], 0.0), shift, False)
    out = jnp.zeros((tiles, LANES), F32)
    for piece in split3(jnp.where(lane >= shift, value, 0.0)):
        out = out + jnp.dot(spread0, piece, preferred_element_type=F32)
    for piece in split3(jnp.where(lane < shift, value, 0.0)):
        out = out + jnp.dot(spread1, piece, preferred_element_type=F32)
    gdep[...] = out

    loop(members, lambda m: store_of(m).wait())
    store_static.wait()
    for copy in pre + wind:
        copy.wait_send()

    def sent(m):
        for copy in halo(m, cc, cu, cd, s_c, r_c) + halo(m, ff, fu, fd, s_f, r_f):
            copy.wait_send()

    loop(members, sent)

    each_kin(lambda j, d: obs_copy(j, d).wait_send())
    each_kin(lambda j, d: dep_copy(j, d).wait_send())
    dx_copy.wait_send()
    def sent_y(b):
        obs_on(b).wait_send()
        dep_on(b).wait_send()
        dg_copy(b).wait_send()

    each_y(sent_y)
    each_e(lambda b: rs_copy(b).wait_send())
    each_e(lambda b: ag_copy(b).wait_send())


def hand_over(x0, x1, x2, y0, y1, y2, b0, b1, b2, s_in, s_out):
    members = x0.shape[0]
    triples = [(x0.at[m], b0.at[m], y0.at[m]) for m in range(members)]
    triples += [(x1, b1, y1), (x2, b2, y2)]
    come = [
        pltpu.make_async_copy(x, b, s_in.at[i]) for i, (x, b, y) in enumerate(triples)
    ]
    go = [
        pltpu.make_async_copy(b, y, s_out.at[i]) for i, (x, b, y) in enumerate(triples)
    ]
    for copy in come:
        copy.start()
    for a, b in zip(come, go):
        a.wait()
        b.start()
    for copy in go:
        copy.wait()


def per_device(
    ens_control,
    static_control,
    perturbations,
    level_sigma,
    length_class,
    courant_east,
    courant_north,
    obs_column,
    obs_count,
    obs_value,
    obs_weight,
    obs_kernel,
):
    members, lev, rows, width = ens_control.shape
    ens = lax.axis_size("ens")
    tiles = lax.axis_size("tile")
    factor = BETA_ENS / math.sqrt(ens * members - 1)
    hi_n = NT * rows
    vmem = lambda *shape, dtype=F32: pltpu.VMEM(shape, dtype)
    dma = lambda *shape: pltpu.SemaphoreType.DMA(shape)
    line = (lev, width)
    ny = ens // 2
    group = tiles // ny
    chunks = ny
    slots = group * LANES
    total_rows = rows + 2 * NDIFF
    fields = (members, rows) + line
    scratch = [
        vmem(*ens_control.shape),
        vmem(*static_control.shape),
        vmem(*perturbations.shape, dtype=BF16),
        pltpu.SMEM(level_sigma.shape, F32),
        vmem(*length_class.shape, dtype=jnp.int32),
        vmem(*courant_east.shape),
        vmem(*courant_north.shape),
        vmem(tiles, LANES, dtype=jnp.int32),
        vmem(1, tiles, dtype=jnp.int32),
        vmem(tiles, LANES),
        vmem(tiles, LANES),
        vmem(*obs_kernel.shape),
        vmem(*ens_control.shape),
        vmem(*static_control.shape),
        dma(12),
        dma(members + 1),
        vmem(tiles, lev, LANES),
        vmem(rows, width),
        vmem(rows, width),
        vmem(rows, width),
        vmem(total_rows, lev, width),
        vmem(total_rows, lev, width),
        vmem(rows, lev, width),
        vmem(rows, *line),
        vmem(*line),
        vmem(*line),
        vmem(ens, hi_n, lev, LANES),
        vmem(*line),
        vmem(*line),
        vmem(*line),
        vmem(*line),
        vmem(*fields),
        vmem(*fields),
        vmem(*fields),
        vmem(NT, *fields),
        vmem(*fields),
        vmem(*fields),
        vmem(*fields),
        vmem(total_rows, lev, width),
        vmem(total_rows, lev, width),
        vmem(hi_n, lev, width),
        vmem(ens, hi_n, lev, LANES),
        vmem(ens, hi_n, lev, LANES),
        vmem(group, 2 * lev, LANES),
        vmem(ny, group, 2 * lev, LANES),
        vmem(chunks, LANES, slots, dtype=BF16),
        vmem(chunks, lev, slots, dtype=jnp.int32),
        vmem(chunks, lev, slots),
        vmem(chunks, lev, slots),
        vmem(hi_n, lev, LANES),
        vmem(ens, hi_n, lev, LANES),
        vmem(hi_n, *line),
        vmem(ny, group, 1, LANES),
        vmem(ny, group, 1, LANES),
        vmem(ny, group, 1, LANES),
        vmem(ny, ny, group, 1, LANES),
        vmem(ny, group, 1, LANES),
        vmem(ny, group, 1, LANES),
        vmem(tiles, LANES),
        dma(4), dma(4),
        dma(2, members), dma(2, members),
        dma(2, members), dma(2, members),
        dma(group), dma(group),
        dma(ens), dma(ens),
        dma(ens), dma(ens),
        dma(ny), dma(ny),
        dma(2), dma(2),
        dma(group), dma(group),
        dma(ny), dma(ny),
        dma(1), dma(1),
        dma(ny), dma(ny),
    ]
    v = pl.BlockSpec(memory_space=pltpu.VMEM)
    a = pl.BlockSpec(memory_space=pl.ANY)
    shape = jax.ShapeDtypeStruct
    grad_ens, grad_static, departures = pl.pallas_call(
        functools.partial(kernel, factor, ens, tiles),
        out_shape=(
            shape(ens_control.shape, F32),
            shape(static_control.shape, F32),
            shape((tiles, LANES), F32),
        ),
        in_specs=[a] * 12,
        out_specs=(a, a, v),
        scratch_shapes=scratch,
        name="gradient",
        compiler_params=pltpu.CompilerParams(
            collective_id=0, has_side_effects=True, vmem_limit_bytes=56 * 2**20
        ),
    )(
        ens_control,
        static_control,
        perturbations,
        level_sigma,
        length_class,
        courant_east,
        courant_north,
        obs_column.reshape(tiles, LANES),
        obs_count.reshape(1, tiles),
        obs_value.reshape(tiles, LANES),
        obs_weight.reshape(tiles, LANES),
        obs_kernel,
    )
    grad_ens, grad_static, departures = pl.pallas_call(
        hand_over,
        out_shape=tuple(shape(x.shape, F32) for x in (grad_ens, grad_static, departures)),
        in_specs=[a, a, a],
        out_specs=(a, a, a),
        scratch_shapes=[
            vmem(*x.shape) for x in (grad_ens, grad_static, departures)
        ]
        + [dma(members + 2), dma(members + 2)],
        name="results",
    )(grad_ens, grad_static, departures)
    return (grad_ens, grad_static, departures.reshape(-1))


def solution(mesh):
    return jax.shard_map(
        per_device,
        mesh=mesh,
        in_specs=(
            P("ens", None, "tile", None),
            P(None, "tile", None),
            P(None, "ens", None, "tile", None),
            P(),
            P("tile", None),
            P("tile", None),
            P("tile", None),
            P("tile"),
            P("tile"),
            P("tile"),
            P("tile"),
            P(None, "tile"),
        ),
        out_specs=(P("ens", None, "tile", None), P(None, "tile", None), P("tile")),
        check_vma=False,
    )
```

```python
import functools
import math

import jax
import jax.numpy as jnp
from jax import lax
from jax.experimental import pallas as pl
from jax.experimental.pallas import tpu as pltpu
from jax.sharding import PartitionSpec as P

NT = 2
NDIFF = 4
BETA_ENS = 0.8
BETA_STATIC = 0.6
DIFF_BASE = 0.06
LANES = 128
MESH = pl.DeviceIdType.MESH
F32 = jnp.float32
BF16 = jnp.bfloat16


def split3(x):
    a = x.astype(BF16)
    rest = x - a.astype(F32)
    b = rest.astype(BF16)
    c = (rest - b.astype(F32)).astype(BF16)
    return a, b, c


def split2(x):
    a = x.astype(BF16).astype(F32)
    return a, x - a


def left(x):
    return pltpu.roll(x, 1, 1)


def right(x):
    return pltpu.roll(x, x.shape[1] - 1, 1)


def kernel(
    factor,
    ens,
    tiles,
    ctl_hbm,
    stc_hbm,
    per_hbm,
    sigma_hbm,
    cls_hbm,
    east_hbm,
    north_hbm,
    ocol_hbm,
    ocnt_hbm,
    oval_hbm,
    owgt_hbm,
    oker_hbm,
    gens_hbm,
    gsta_hbm,
    gdep,
    ctl,
    stc,
    per,
    sigma,
    cls,
    east,
    north,
    ocol,
    ocnt,
    oval,
    owgt,
    oker,
    gens,
    gsta,
    s_in,
    s_out,
    okb,
    dif,
    dif_u,
    dif_d,
    dbc,
    dsq,
    fin,
    sta,
    sta_u,
    sta_d,
    stb,
    wnd_u,
    wnd_d,
    rcv_wu,
    rcv_wd,
    cc,
    cu,
    cd,
    pp,
    ff,
    fu,
    fd,
    wa,
    wb,
    acc,
    accb,
    rbuf,
    obs_s,
    obs_r,
    onehot,
    himask,
    okern,
    oaux,
    adjb,
    abuf,
    adjf,
    depp,
    depx,
    dx,
    dbuf,
    deps,
    depr,
    depf,
    s_pre,
    r_pre,
    s_c,
    r_c,
    s_f,
    r_f,
    s_obs,
    r_obs,
    s_rs,
    r_rs,
    s_ag,
    r_ag,
    s_dg,
    r_dg,
    s_w,
    r_w,
    s_dep,
    r_dep,
    s_o2,
    r_o2,
    s_dx,
    r_dx,
    s_d2,
    r_d2,
):
    members, lev, rows, width = ctl.shape
    hi_n = NT * rows
    e = lax.axis_index("ens")
    t = lax.axis_index("tile")
    ny = ens // 2
    y = e // 2
    xl = lax.rem(e, 2)
    partner = 2 * y + 1 - xl
    group = tiles // ny
    kin = lax.rem(y - lax.rem(t, ny) + ny, ny)
    line_t = t // ny
    up = lax.rem(t + tiles - 1, tiles)
    down = lax.rem(t + 1, tiles)
    first = t == 0
    last = t == tiles - 1

    def remote(src, dst, ssem, rsem, e_to, t_to):
        return pltpu.make_async_remote_copy(
            src_ref=src,
            dst_ref=dst,
            send_sem=ssem,
            recv_sem=rsem,
            device_id=(e_to, t_to),
            device_id_type=MESH,
        )

    def loop(n, body):
        def step(i, carry):
            body(i)
            return carry

        lax.fori_loop(0, n, step, 0)

    def span(low, high, body):
        def step(i, carry):
            body(i)
            return carry

        lax.fori_loop(low, high, step, 0)

    def each_e(body):
        span(1, ens, lambda k: body(lax.rem(e + k, ens)))

    def peer_y(k):
        return lax.rem(y + k, ny)

    def each_y(body):
        span(1, ny, lambda k: body(peer_y(k)))

    def each_kin(body):
        def one(j):
            pl.when(j * ny + kin != t)(lambda: body(j, j * ny + kin))

        loop(group, one)

    barrier = pltpu.get_barrier_semaphore()

    def greet(e_to, t_to):
        pl.semaphore_signal(barrier, inc=1, device_id=(e_to, t_to), device_id_type=MESH)

    greet(e, up)
    greet(e, down)
    each_kin(lambda j, d: greet(e, d))
    each_e(lambda b: greet(b, t))
    alone = jnp.where(kin == lax.rem(t, ny), 1, 0)
    inputs = (
        (cls_hbm, cls),
        (stc_hbm, stc),
        (sigma_hbm, sigma),
        (ctl_hbm, ctl),
        (ocnt_hbm, ocnt),
        (oker_hbm, oker),
        (ocol_hbm, ocol),
        (oval_hbm, oval),
        (owgt_hbm, owgt),
        (per_hbm, per),
        (east_hbm, east),
        (north_hbm, north),
    )
    loads = [
        pltpu.make_async_copy(src, dst, s_in.at[i]) for i, (src, dst) in enumerate(inputs)
    ]
    for copy in loads:
        copy.start()
    for copy in loads[0:3]:
        copy.wait()
    dif[...] = jnp.sqrt(DIFF_BASE * (cls[...].astype(F32) + 1.0))
    sub = lax.broadcasted_iota(jnp.int32, (lev, width), 0)
    scale = jnp.zeros((lev, width), F32)
    for l in range(lev):
        scale = jnp.where(sub == l, BETA_STATIC * sigma[l], scale)
    for r in range(rows):
        sta[r] = scale * stc[:, r, :]
    loads[3].wait()
    pl.semaphore_wait(barrier, 2 + group - alone + ens - 1)

    pre = [
        remote(dif, dif_u, s_pre.at[0], r_pre.at[0], e, down),
        remote(dif, dif_d, s_pre.at[1], r_pre.at[1], e, up),
        remote(sta.at[rows - 1], sta_u, s_pre.at[2], r_pre.at[2], e, down),
        remote(sta.at[0], sta_d, s_pre.at[3], r_pre.at[3], e, up),
    ]
    for copy in pre:
        copy.start()

    def halo(m, own, from_up, from_down, ssem, rsem):
        src = own.at[m]
        return (
            remote(src, from_up.at[m], ssem.at[0, m], rsem.at[0, m], e, down),
            remote(src, from_down.at[m], ssem.at[1, m], rsem.at[1, m], e, up),
        )

    def send_control(m):
        for r in range(rows):
            cc[m, r] = ctl[m, :, r, :]
        for copy in halo(m, cc, cu, cd, s_c, r_c):
            copy.start()

    ahead = members // 4
    span(0, ahead, send_control)

    for copy in loads[4:9]:
        copy.wait()

    count = jnp.broadcast_to(ocnt[...].astype(F32), (tiles, tiles))
    d_sub = lax.broadcasted_iota(jnp.int32, (tiles, tiles), 0)
    d_lane = lax.broadcasted_iota(jnp.int32, (tiles, tiles), 1)
    count_col = jnp.sum(
        jnp.where(d_lane == d_sub, count, 0.0), axis=1, keepdims=True
    )
    start_col = jnp.sum(jnp.where(d_lane < d_sub, count, 0.0), axis=1, keepdims=True)
    start_row = jnp.sum(
        jnp.where(d_sub < d_lane, jnp.broadcast_to(count_col, (tiles, tiles)), 0.0),
        axis=0,
        keepdims=True,
    )
    def places(start_of, count_of):
        shape = (start_of.shape[0], LANES)
        begin = jnp.broadcast_to(start_of, shape).astype(jnp.int32)
        lane = lax.broadcasted_iota(jnp.int32, shape, 1)
        usable = lane < jnp.broadcast_to(count_of, shape).astype(jnp.int32)
        return lane, begin & (LANES - 1), usable

    def turn(x, shift, back):
        for bit in range(LANES.bit_length() - 1):
            by = LANES - (1 << bit) if back else 1 << bit
            x = jnp.where(shift & (1 << bit) != 0, pltpu.roll(x, by, 1), x)
        return x

    kin_count = jnp.broadcast_to(ocnt[...].astype(F32), (group, tiles))
    kin_sub = lax.broadcasted_iota(jnp.int32, (group, tiles), 0) * ny + kin
    kin_lane = lax.broadcasted_iota(jnp.int32, (group, tiles), 1)
    kin_start = jnp.sum(
        jnp.where(kin_lane < kin_sub, kin_count, 0.0), axis=1, keepdims=True
    )
    kin_own = jnp.sum(
        jnp.where(kin_lane == kin_sub, kin_count, 0.0), axis=1, keepdims=True
    )
    lane, shift, usable = places(kin_start, kin_own)
    line_col = jnp.broadcast_to(kin_start, (group, tiles)).astype(jnp.int32) // LANES
    pick = jnp.concatenate(
        [
            jnp.where(kin_lane == line_col, 1.0, 0.0),
            jnp.where(kin_lane == line_col + 1, 1.0, 0.0),
        ],
        axis=0,
    ).astype(BF16)
    for b in range(tiles):
        okb[b] = oker[:, b * LANES : (b + 1) * LANES]
    for q in range(lev + 3):
        if q < lev:
            part = okb[:, q, :]
        else:
            part = (ocol, oval, owgt)[q - lev][...].astype(F32)
        two = sum(
            jnp.dot(pick, piece, preferred_element_type=F32) for piece in split3(part)
        )
        value = jnp.where(lane >= shift, two[0:group], two[group : 2 * group])
        value = turn(value, shift, True)
        if q == lev:
            value = jnp.where(usable, value, -1.0)
        obs_s[:, q // rows, q % rows, :] = value
    for q in range(lev + 3, lev + rows):
        obs_s[:, q // rows, q % rows, :] = jnp.zeros((group, LANES), F32)

    def obs_copy(j, d):
        return remote(
            obs_s.at[j], obs_r.at[y, line_t], s_obs.at[j], r_obs.at[line_t], e, d
        )

    each_kin(lambda j, d: obs_copy(j, d).start())

    @pl.when(alone == 1)
    def _():
        obs_r[y, line_t] = obs_s[line_t]

    span(ahead, members, send_control)

    def obs_on(b):
        return remote(obs_r.at[y], obs_r.at[y], s_o2.at[b], r_o2.at[y], 2 * b + xl, t)

    def obs_mid():
        each_kin(
            lambda j, d: remote(
                obs_s.at[j], obs_r.at[y, j], s_obs.at[j], r_obs.at[j], e, d
            ).wait_recv()
        )
        each_y(lambda b: obs_on(b).start())

    def obs_wait():
        each_y(
            lambda b: remote(
                obs_r.at[b], obs_r.at[b], s_o2.at[b], r_o2.at[b], 2 * b + xl, t
            ).wait_recv()
        )

    def spread(m):
        for s in range(NT):
            block = per[s, m].astype(F32)
            for r in range(rows):
                pp[s, m, r] = block[:, r, :]

    for copy in loads[9:12]:
        copy.wait()
    loop(members, spread)

    pre[0].wait_recv()
    pre[1].wait_recv()
    above = jnp.where(first, 0.0, dif_u[...])
    below = jnp.where(last, 0.0, dif_d[...])
    own = dif[...]
    total_rows = rows + 2 * NDIFF
    for i in range(total_rows):
        src = above if i < NDIFF else (own if i < NDIFF + rows else below)
        j = i if i < NDIFF else (i - NDIFF if i < NDIFF + rows else i - NDIFF - rows)
        line = jnp.broadcast_to(src[j : j + 1, :], (lev, width))
        dbc[i] = line
        dsq[i] = line * line
        if NDIFF <= i < NDIFF + rows:
            fin[i - NDIFF] = factor / line

    def tile_of(x, b):
        return x[:, b * LANES : (b + 1) * LANES]

    pre[2].wait_recv()
    pre[3].wait_recv()

    def winds(r):
        we = jnp.broadcast_to(east[r : r + 1, :], (lev, width))
        wn = jnp.broadcast_to(north[r : r + 1, :], (lev, width))
        return (
            jnp.maximum(we, 0.0),
            jnp.minimum(we, 0.0),
            jnp.maximum(wn, 0.0),
            jnp.minimum(wn, 0.0),
        )

    for r in range(rows):
        ep, em, np_, nm = winds(r)
        q = sta[r]
        above = sta[r - 1] if r else jnp.where(first, 0.0, sta_u[...])
        below = sta[r + 1] if r < rows - 1 else jnp.where(last, 0.0, sta_d[...])
        moved = q - ep * (q - left(q)) - em * (right(q) - q)
        moved = moved - np_ * (q - above) - nm * (below - q)
        for b in range(ens):
            stb[b, r] = tile_of(q, b)
            stb[b, rows + r] = tile_of(moved, b)

    def smooth(m, refs):
        for i in range(total_rows):
            ref, r = source_of(i, refs)
            wa[i] = dbc[i] * ref[m, r]
        src, dst = wa, wb
        for step in range(NDIFF):
            for i in range(step + 1, total_rows - 1 - step):
                w = src[i]
                lap = src[i + 1] + src[i - 1] + left(w) + right(w) - 4.0 * w
                dst[i] = w + dsq[i] * lap
            src, dst = dst, src
        return [src[NDIFF + r] for r in range(rows)]

    def source_of(i, refs):
        if i < NDIFF:
            return refs[0], i
        if i < NDIFF + rows:
            return refs[1], i - NDIFF
        return refs[2], i - NDIFF - rows

    def forward(m):
        for copy in halo(m, cc, cu, cd, s_c, r_c):
            copy.wait_recv()
        res = smooth(m, (cu, cc, cd))
        for r in range(rows):
            for s in range(NT):
                acc[s * rows + r] += pp[s, m, r] * res[r]

    def rs_copy(b):
        return remote(accb.at[b], rbuf.at[e], s_rs.at[b], r_rs.at[e], b, t)

    def rs_start():
        for h in range(hi_n):
            value = acc[h] * fin[h % rows]
            for b in range(ens):
                accb[b, h] = tile_of(value, b)
        each_e(lambda b: rs_copy(b).start())

    def rs_wait():
        each_e(
            lambda b: remote(
                accb.at[b], rbuf.at[b], s_rs.at[b], r_rs.at[b], b, t
            ).wait_recv()
        )
        rbuf[e] = accb[e]

    chunks = ny

    def lines_of(g, i):
        at = i % rows
        return jnp.concatenate(
            [obs_r[g, j, i // rows, at : at + 1, :] for j in range(group)], axis=1
        )

    def kernel_of(g):
        return jnp.concatenate(
            [
                jnp.concatenate([obs_r[g, j, k] for k in range(lev // rows)], axis=0)
                for j in range(group)
            ],
            axis=1,
        )

    lo_iota = lax.broadcasted_iota(jnp.int32, (LANES, group * LANES), 0)

    def hot(g):
        col = lines_of(g, lev).astype(jnp.int32)
        lo = col & (LANES - 1)
        block = (col // LANES) & (ens - 1)
        unit = jnp.where((col >= 0) & (block == e), col // width, -1)
        himask[g] = jnp.broadcast_to(unit, (lev, group * LANES))
        okern[g] = kernel_of(g)
        oaux[g, 0:1, :] = lines_of(g, lev + 1)
        oaux[g, 1:2, :] = lines_of(g, lev + 2)
        onehot[g] = jnp.where(
            jnp.broadcast_to(lo, (LANES, group * LANES)) == lo_iota, 1.0, 0.0
        ).astype(BF16)

    def observe():
        points = hi_n * lev
        values = []
        for u in range(hi_n):
            value = stb[e, u]
            for b in range(ens):
                value = value + rbuf[b, u]
            values.append(value)
        table = jnp.concatenate(split2(jnp.concatenate(values, axis=0)), axis=0)
        table = table.astype(BF16)
        total = jnp.zeros((2 * points, LANES), F32)
        for g in range(chunks):
            hi = himask[g]
            kern = okern[g]
            flat = jnp.dot(table, onehot[g], preferred_element_type=F32)
            profile = jnp.zeros(kern.shape, F32)
            for j in range(hi_n):
                value = flat[j * lev : (j + 1) * lev]
                value = value + flat[points + j * lev : points + (j + 1) * lev]
                profile = jnp.where(hi == j, value, profile)
            evolved = jnp.sum(kern * profile, axis=0, keepdims=True)
            dep = oaux[g, 1:2, :] * (evolved - oaux[g, 0:1, :])
            dep = jnp.where(hi[0:1] >= 0, dep, 0.0)
            for j in range(group):
                depp[g, j] = tile_of(dep, j)
            push = kern * dep
            place = jnp.concatenate(
                [jnp.where(hi == j, push, 0.0) for j in range(hi_n)], axis=0
            )
            place = jnp.concatenate(split2(place), axis=0).astype(BF16)
            total = total + lax.dot_general(
                place, onehot[g], (((1,), (1,)), ((), ())), preferred_element_type=F32
            )
        total = total[0:points] + total[points : 2 * points]
        for j in range(hi_n):
            adjb[j] = total[j * lev : (j + 1) * lev]
            abuf[e, j] = total[j * lev : (j + 1) * lev]
        each_e(lambda b: ag_copy(b).start())

    def ag_copy(b):
        return remote(adjb, abuf.at[e], s_ag.at[b], r_ag.at[e], b, t)

    def ag_wait():
        each_e(
            lambda b: remote(
                adjb, abuf.at[b], s_ag.at[b], r_ag.at[b], b, t
            ).wait_recv()
        )
        for h in range(hi_n):
            adjf[h] = jnp.concatenate([abuf[b, h] for b in range(ens)], axis=1)

    dx_copy = remote(depp, dx, s_dx.at[0], r_dx.at[0], partner, t)

    def dg_copy(b):
        return remote(depx, dbuf.at[y], s_dg.at[b], r_dg.at[y], 2 * b + xl, t)

    def dg_mid():
        dx_copy.wait_recv()
        depx[...] = depp[...] + dx[...]
        each_y(lambda b: dg_copy(b).start())

    def force(m):
        for r in range(rows):
            ff[m, r] = pp[0, m, r] * adjf[r] + pp[1, m, r] * adjf[rows + r]
        for copy in halo(m, ff, fu, fd, s_f, r_f):
            copy.start()

    def store_of(m):
        return pltpu.make_async_copy(gens.at[m], gens_hbm.at[m], s_out.at[m])

    def backward(m):
        for copy in halo(m, ff, fu, fd, s_f, r_f):
            copy.wait_recv()
        res = smooth(m, (fu, ff, fd))
        for r in range(rows):
            gens[m, :, r, :] = cc[m, r] + res[r] * fin[r]
        store_of(m).start()

    for h in range(hi_n):
        acc[h] = jnp.zeros((lev, width), F32)
    span(0, members // 2, forward)
    obs_mid()
    span(members // 2, members, forward)
    rs_start()
    obs_wait()
    for g in range(chunks):
        hot(g)
    rs_wait()
    observe()
    dx_copy.start()
    ag_wait()
    wnd_u[...] = winds(0)[2] * adjf[rows]
    wnd_d[...] = winds(rows - 1)[3] * adjf[2 * rows - 1]
    wind = [
        remote(wnd_d, rcv_wu, s_w.at[0], r_w.at[0], e, down),
        remote(wnd_u, rcv_wd, s_w.at[1], r_w.at[1], e, up),
    ]
    q1 = members * 3 // 8
    span(0, 1, force)
    dg_mid()
    span(1, q1, force)
    for copy in wind:
        copy.start()

    each_y(
        lambda b: remote(
            depx, dbuf.at[b], s_dg.at[b], r_dg.at[b], 2 * b + xl, t
        ).wait_recv()
    )
    dbuf[y] = depx[...]
    value = dbuf[0]
    for b in range(1, ny):
        value = value + dbuf[b]
    deps[...] = value

    def dep_copy(j, s):
        return remote(
            deps.at[y, j], depr.at[y, line_t], s_dep.at[j], r_dep.at[line_t], e, s
        )

    each_kin(lambda j, s: dep_copy(j, s).start())

    @pl.when(alone == 1)
    def _():
        depr[y, line_t] = deps[y, line_t]

    span(q1, members, force)

    for copy in wind:
        copy.wait_recv()
    for r in range(rows):
        ep, em, np_, nm = winds(r)
        a = adjf[rows + r]
        if r < rows - 1:
            lower = winds(r + 1)[2] * adjf[rows + r + 1]
        else:
            lower = jnp.where(last, 0.0, rcv_wd[...])
        if r:
            upper = winds(r - 1)[3] * adjf[rows + r - 1]
        else:
            upper = jnp.where(first, 0.0, rcv_wu[...])
        moved = a * (1.0 - ep + em - np_ + nm) + right(ep * a) - left(em * a)
        moved = moved + lower - upper
        gsta[:, r, :] = stc[:, r, :] + scale * (adjf[r] + moved)

    store_static = pltpu.make_async_copy(gsta, gsta_hbm, s_out.at[members])
    store_static.start()

    span(0, q1, backward)
    each_kin(
        lambda j, s: remote(
            deps.at[y, j], depr.at[y, j], s_dep.at[j], r_dep.at[j], e, s
        ).wait_recv()
    )

    def dep_on(b):
        return remote(depr.at[y], depr.at[y], s_d2.at[b], r_d2.at[y], 2 * b + xl, t)

    each_y(lambda b: dep_on(b).start())
    span(q1, members, backward)

    each_y(
        lambda b: remote(
            depr.at[b], depr.at[b], s_d2.at[b], r_d2.at[b], 2 * b + xl, t
        ).wait_recv()
    )
    for d in range(tiles):
        depf[d : d + 1, :] = depr[lax.rem(t + d, ny), d // ny]
    lane, shift, usable = places(start_col, count_col)
    line_row = jnp.broadcast_to(start_row, (tiles, tiles)).astype(jnp.int32) // LANES
    spread0 = jnp.where(d_sub == line_row, 1.0, 0.0).astype(BF16)
    spread1 = jnp.where(d_sub == line_row + 1, 1.0, 0.0).astype(BF16)
    value = turn(jnp.where(usable, depf[...], 0.0), shift, False)
    out = jnp.zeros((tiles, LANES), F32)
    for piece in split3(jnp.where(lane >= shift, value, 0.0)):
        out = out + jnp.dot(spread0, piece, preferred_element_type=F32)
    for piece in split3(jnp.where(lane < shift, value, 0.0)):
        out = out + jnp.dot(spread1, piece, preferred_element_type=F32)
    gdep[...] = out

    loop(members, lambda m: store_of(m).wait())
    store_static.wait()
    for copy in pre + wind:
        copy.wait_send()

    def sent(m):
        for copy in halo(m, cc, cu, cd, s_c, r_c) + halo(m, ff, fu, fd, s_f, r_f):
            copy.wait_send()

    loop(members, sent)

    each_kin(lambda j, d: obs_copy(j, d).wait_send())
    each_kin(lambda j, d: dep_copy(j, d).wait_send())
    dx_copy.wait_send()
    def sent_y(b):
        obs_on(b).wait_send()
        dep_on(b).wait_send()
        dg_copy(b).wait_send()

    each_y(sent_y)
    each_e(lambda b: rs_copy(b).wait_send())
    each_e(lambda b: ag_copy(b).wait_send())


def hand_over(x0, x1, x2, y0, y1, y2, b0, b1, b2, s_in, s_out):
    members = x0.shape[0]
    triples = [(x0.at[m], b0.at[m], y0.at[m]) for m in range(members)]
    triples += [(x1, b1, y1), (x2, b2, y2)]
    come = [
        pltpu.make_async_copy(x, b, s_in.at[i]) for i, (x, b, y) in enumerate(triples)
    ]
    go = [
        pltpu.make_async_copy(b, y, s_out.at[i]) for i, (x, b, y) in enumerate(triples)
    ]
    for copy in come:
        copy.start()
    for a, b in zip(come, go):
        a.wait()
        b.start()
    for copy in go:
        copy.wait()


def per_device(
    ens_control,
    static_control,
    perturbations,
    level_sigma,
    length_class,
    courant_east,
    courant_north,
    obs_column,
    obs_count,
    obs_value,
    obs_weight,
    obs_kernel,
):
    members, lev, rows, width = ens_control.shape
    ens = lax.axis_size("ens")
    tiles = lax.axis_size("tile")
    factor = BETA_ENS / math.sqrt(ens * members - 1)
    hi_n = NT * rows
    vmem = lambda *shape, dtype=F32: pltpu.VMEM(shape, dtype)
    dma = lambda *shape: pltpu.SemaphoreType.DMA(shape)
    line = (lev, width)
    ny = ens // 2
    group = tiles // ny
    chunks = ny
    slots = group * LANES
    total_rows = rows + 2 * NDIFF
    fields = (members, rows) + line
    scratch = [
        vmem(*ens_control.shape),
        vmem(*static_control.shape),
        vmem(*perturbations.shape, dtype=BF16),
        pltpu.SMEM(level_sigma.shape, F32),
        vmem(*length_class.shape, dtype=jnp.int32),
        vmem(*courant_east.shape),
        vmem(*courant_north.shape),
        vmem(tiles, LANES, dtype=jnp.int32),
        vmem(1, tiles, dtype=jnp.int32),
        vmem(tiles, LANES),
        vmem(tiles, LANES),
        vmem(*obs_kernel.shape),
        vmem(*ens_control.shape),
        vmem(*static_control.shape),
        dma(12),
        dma(members + 1),
        vmem(tiles, lev, LANES),
        vmem(rows, width),
        vmem(rows, width),
        vmem(rows, width),
        vmem(total_rows, lev, width),
        vmem(total_rows, lev, width),
        vmem(rows, lev, width),
        vmem(rows, *line),
        vmem(*line),
        vmem(*line),
        vmem(ens, hi_n, lev, LANES),
        vmem(*line),
        vmem(*line),
        vmem(*line),
        vmem(*line),
        vmem(*fields),
        vmem(*fields),
        vmem(*fields),
        vmem(NT, *fields),
        vmem(*fields),
        vmem(*fields),
        vmem(*fields),
        vmem(total_rows, lev, width),
        vmem(total_rows, lev, width),
        vmem(hi_n, lev, width),
        vmem(ens, hi_n, lev, LANES),
        vmem(ens, hi_n, lev, LANES),
        vmem(group, lev // rows + 1, rows, LANES),
        vmem(ny, group, lev // rows + 1, rows, LANES),
        vmem(chunks, LANES, slots, dtype=BF16),
        vmem(chunks, lev, slots, dtype=jnp.int32),
        vmem(chunks, lev, slots),
        vmem(chunks, lev, slots),
        vmem(hi_n, lev, LANES),
        vmem(ens, hi_n, lev, LANES),
        vmem(hi_n, *line),
        vmem(ny, group, 1, LANES),
        vmem(ny, group, 1, LANES),
        vmem(ny, group, 1, LANES),
        vmem(ny, ny, group, 1, LANES),
        vmem(ny, group, 1, LANES),
        vmem(ny, group, 1, LANES),
        vmem(tiles, LANES),
        dma(4), dma(4),
        dma(2, members), dma(2, members),
        dma(2, members), dma(2, members),
        dma(group), dma(group),
        dma(ens), dma(ens),
        dma(ens), dma(ens),
        dma(ny), dma(ny),
        dma(2), dma(2),
        dma(group), dma(group),
        dma(ny), dma(ny),
        dma(1), dma(1),
        dma(ny), dma(ny),
    ]
    v = pl.BlockSpec(memory_space=pltpu.VMEM)
    a = pl.BlockSpec(memory_space=pl.ANY)
    shape = jax.ShapeDtypeStruct
    grad_ens, grad_static, departures = pl.pallas_call(
        functools.partial(kernel, factor, ens, tiles),
        out_shape=(
            shape(ens_control.shape, F32),
            shape(static_control.shape, F32),
            shape((tiles, LANES), F32),
        ),
        in_specs=[a] * 12,
        out_specs=(a, a, v),
        scratch_shapes=scratch,
        name="gradient",
        compiler_params=pltpu.CompilerParams(
            collective_id=0, has_side_effects=True, vmem_limit_bytes=56 * 2**20
        ),
    )(
        ens_control,
        static_control,
        perturbations,
        level_sigma,
        length_class,
        courant_east,
        courant_north,
        obs_column.reshape(tiles, LANES),
        obs_count.reshape(1, tiles),
        obs_value.reshape(tiles, LANES),
        obs_weight.reshape(tiles, LANES),
        obs_kernel,
    )
    grad_ens, grad_static, departures = pl.pallas_call(
        hand_over,
        out_shape=tuple(shape(x.shape, F32) for x in (grad_ens, grad_static, departures)),
        in_specs=[a, a, a],
        out_specs=(a, a, a),
        scratch_shapes=[
            vmem(*x.shape) for x in (grad_ens, grad_static, departures)
        ]
        + [dma(members + 2), dma(members + 2)],
        name="results",
    )(grad_ens, grad_static, departures)
    return (grad_ens, grad_static, departures.reshape(-1))


def solution(mesh):
    return jax.shard_map(
        per_device,
        mesh=mesh,
        in_specs=(
            P("ens", None, "tile", None),
            P(None, "tile", None),
            P(None, "ens", None, "tile", None),
            P(),
            P("tile", None),
            P("tile", None),
            P("tile", None),
            P("tile"),
            P("tile"),
            P("tile"),
            P("tile"),
            P(None, "tile"),
        ),
        out_specs=(P("ens", None, "tile", None), P(None, "tile", None), P("tile")),
        check_vma=False,
    )
```
